256 devices in a mesh: slot: 8 (over x, core), seq: 32 (over z, y).
Axes of the slice: x: 4, y: 4, z: 8, core: 2. Of those that a mesh axis runs over, the one named last changes fastest.
Arguments:
- latent: bfloat16 [8, 1024, 3072], P('slot', 'seq'), may hold values from -6 to 6
- noise_frame: bfloat16 [512, 3072], replicated, may hold values from -6 to 6
- frame_pos: int32 [8, 2], P('slot'), may hold values from 0 to 15
- t_index: int32 [8], P('slot'), may hold values from 0 to 49
- pos_table: bfloat16 [16, 3072], replicated, may hold values from -6 to 6
- mod_table: bfloat16 [50, 2, 3, 3072], replicated, may hold values from -5 to 5
- w_qkv: bfloat16 [2, 3072, 32, 192], P(None, None, 'seq'), may hold values from -0.109375 to 0.109375
- qk_gain: bfloat16 [2, 32, 128], P(None, 'seq'), may hold values from 0.5 to 3
- w_out: bfloat16 [2, 2048, 3072], P(None, 'seq'), may hold values from -0.25 to 0.25
Outputs:
- denoised: bfloat16 [8, 1024, 3072], P('slot', 'seq')
- queue_next: bfloat16 [8, 1024, 3072], P('slot', 'seq')
The draws below stay inside these ranges and needn't reach their ends.
All inputs are finite; a program needn't handle non-finite values.
Results may differ from the reference program's by a relative error of at most 0.039.
Values may be sent and summed in bfloat16 or wider, within the bound.
No kernel may reach another device: no remote copies, remote signals or barrier semaphores. Data moves between devices by JAX's collectives and lax.ppermute only.
A program may use at most 128 MiB of HBM per device.

```python
import math
import jax
import jax.numpy as jnp
from jax import lax

D = 3072
HD = 64
HEAD_DEV = 1
LAYERS = 2
NT = 50
NF = 16
HEADS = 32
SLOTS = 8
SLOT_TOK = 1024
FRAME_TOK = 512
N_SEQ = 32


def place_ends(result, rng, low, largest):
    dims = result.shape
    spot = [jax.random.randint(jax.random.fold_in(rng, axis), (), 0, dims[axis]) for axis in range(len(dims))]
    result = result.at[tuple(spot)].set(low)
    longest = dims.index(max(dims))
    spot[longest] = (spot[longest] + 1) % dims[longest]
    return result.at[tuple(spot)].set(largest)


def block_scale(rng, extent, pieces, smallest, largest):
    loudness, own = 1.0, jax.random.fold_in(rng, 6)
    for dim, shards_of in pieces:
        steps = jnp.exp(jax.random.uniform(jax.random.fold_in(own, dim), (shards_of,), jnp.float32, smallest / len(pieces), largest / len(pieces)))
        loudness = loudness * jnp.repeat(steps, extent[dim] // shards_of).reshape([-1 if axis == dim else 1 for axis in range(len(extent))])
    return loudness


def normal_values(stream_key, dims, scale, bound, split=(), dtype=jnp.bfloat16):
    gain = block_scale(stream_key, dims, split, -0.22, 0.18) if split else 1.0
    entries = jax.random.normal(stream_key, dims, jnp.float32) * scale * gain
    return jnp.minimum(jnp.maximum(entries, -bound), bound).astype(dtype)


def setup_inputs(seed: int = 0) -> dict:
    streams_of = jax.random.split(jax.random.key(seed), 10)
    latent = normal_values(streams_of[0], (SLOTS, SLOT_TOK, D), 1.0, 6.0, ((0, 8), (1, 32)))
    noise_frame = normal_values(streams_of[1], (FRAME_TOK, D), 1.0, 6.0)
    frame_pos = place_ends(jax.random.randint(streams_of[2], (SLOTS, 2), 0, NF), jax.random.fold_in(streams_of[2], 1), 0, NF - 1).astype(jnp.int32)
    t_index = place_ends(jax.random.randint(streams_of[3], (SLOTS,), 0, NT), jax.random.fold_in(streams_of[3], 1), 0, NT - 1).astype(jnp.int32)
    pos_table = normal_values(streams_of[4], (NF, D), 1.0, 6.0)
    mod_table = normal_values(streams_of[5], (NT, LAYERS, 3, D), 1.0, 5.0)
    w_qkv = normal_values(streams_of[6], (LAYERS, D, HEADS, 3 * HD), D ** -0.5, 0.109375, ((2, 32),))
    qk_gain = jnp.clip(jnp.exp(math.log(3.0) - 1.7917595 * jax.random.uniform(streams_of[7], (LAYERS, HEADS, 2 * HD), jnp.float32) ** block_scale(streams_of[7], (LAYERS, HEADS, 2 * HD), ((1, 32),), -0.2, 0.2)), 0.5, 3.0).astype(jnp.bfloat16)
    w_out = normal_values(streams_of[8], (LAYERS, HEADS * HD, D), (HD * 8) ** -0.5, 0.25, ((1, 32),))
    return {"latent": latent, "noise_frame": noise_frame, "frame_pos": frame_pos, "t_index": t_index, "pos_table": pos_table, "mod_table": mod_table, "w_qkv": w_qkv, "qk_gain": qk_gain, "w_out": w_out}


def layer_norm(value):
    center = value - lax.optimization_barrier(jnp.mean(value, axis=-1, keepdims=True))
    spread = lax.optimization_barrier(jnp.mean(center * center, axis=-1, keepdims=True))
    return center * lax.rsqrt(spread + 1e-06)

def window(array):
    padded = jnp.pad(array, ((1, 1), (0, 0), (0, 0)))
    return jnp.concatenate([padded[:-2], padded[1:-1], padded[2:]], axis=1)

def reference(latent, noise_frame, frame_pos, t_index, pos_table, mod_table, w_qkv, qk_gain, w_out):
    slots = latent.shape[0]
    length = latent.shape[1]
    width = latent.shape[2]
    half_len = length // 2
    head_dim = qk_gain.shape[2] // 2
    inv = 1.0 / jnp.sqrt(jnp.float32(head_dim))
    position = pos_table[frame_pos].astype(jnp.float32)
    stream = latent.reshape(slots, 2, half_len, width).astype(jnp.float32) + position[:, :, None, :]
    stream = stream.reshape(slots, length, width).astype(jnp.bfloat16)
    mods = mod_table[t_index].astype(jnp.float32)
    slot_ids = jnp.arange(slots)
    valid = jnp.stack([slot_ids > 0, slot_ids >= 0, slot_ids < slots - 1], axis=1).astype(jnp.float32)
    key_mask = jnp.repeat(valid, length, axis=1)
    for layer in range(LAYERS):
        shift = mods[:, layer, 0][:, None, :]
        scale = mods[:, layer, 1][:, None, :]
        gate = mods[:, layer, 2][:, None, :]
        normed = (layer_norm(stream.astype(jnp.float32)) * (1.0 + scale) + shift).astype(jnp.bfloat16)
        normed = normed.reshape(slots * length, width)
        w_group = jnp.moveaxis(w_qkv[layer].reshape(width, N_SEQ, HEAD_DEV * 3 * head_dim), 1, 0)
        g_group = qk_gain[layer].astype(jnp.float32).reshape(N_SEQ, HEAD_DEV, 2 * head_dim)
        out_group = w_out[layer].reshape(N_SEQ, HEAD_DEV * head_dim, width)

        def group_step(total, items):
            w_one, g_one, out_one = items
            qkv = jnp.dot(normed, w_one, preferred_element_type=jnp.float32)
            qkv = qkv.reshape(slots, length, HEAD_DEV, 3, head_dim)
            outputs = []
            for head in range(HEAD_DEV):
                query = (layer_norm(qkv[:, :, head, 0]) * g_one[head, :head_dim]).astype(jnp.bfloat16)
                keyed = (layer_norm(qkv[:, :, head, 1]) * g_one[head, head_dim:]).astype(jnp.bfloat16)
                valued = qkv[:, :, head, 2].astype(jnp.bfloat16)
                keys = window(keyed)
                values = window(valued)
                scores = jnp.einsum('sqd,skd->sqk', query.astype(jnp.float32), keys.astype(jnp.float32)) * inv
                weights = jnp.exp(scores) * key_mask[:, None, :]
                denom = lax.optimization_barrier(jnp.sum(weights, axis=-1))
                probs = weights.astype(jnp.bfloat16)
                attended = jnp.einsum('sqk,skd->sqd', probs.astype(jnp.float32), values.astype(jnp.float32))
                outputs.append((attended / denom[..., None]).astype(jnp.bfloat16))
            joined = jnp.concatenate(outputs, axis=-1).reshape(slots * length, HEAD_DEV * head_dim)
            term = jnp.dot(joined, out_one, preferred_element_type=jnp.float32).astype(jnp.bfloat16)
            return (total + term.astype(jnp.float32), None)
        attn, _ = lax.scan(group_step, jnp.zeros((slots * length, width), jnp.float32), (w_group, g_group, out_group))
        stream = (stream.astype(jnp.float32) + gate * attn.reshape(slots, length, width)).astype(jnp.bfloat16)
    denoised = stream
    frames = denoised.reshape(slots * 2, half_len, width)
    queue_next = jnp.concatenate([frames[1:], noise_frame[None]], axis=0).reshape(slots, length, width)
    return (denoised, queue_next)
```

```python
import functools

import jax
import jax.numpy as jnp
from jax import lax
from jax.experimental import pallas as pl
from jax.experimental.pallas import tpu as pltpu
from jax.sharding import Mesh, PartitionSpec as P

BF = jnp.bfloat16
F32 = jnp.float32
EPS = 1e-6
NX, NC, NZ, NY = 4, 2, 8, 4
D = 3072
HD = 64
ROWS = 32
QUARTER = D // NY
EIGHTH = QUARTER // 2
VMEM_LIMIT = 48 * 1024 * 1024

VM = pl.BlockSpec(memory_space=pltpu.VMEM)
SM = pl.BlockSpec(memory_space=pltpu.SMEM)


def params():
    return pltpu.CompilerParams(vmem_limit_bytes=VMEM_LIMIT)


def normalized(blocks):
    mean = sum(jnp.sum(b, axis=-1, keepdims=True) for b in blocks) / D
    centers = [b - mean for b in blocks]
    spread = sum(jnp.sum(c * c, axis=-1, keepdims=True) for c in centers) / D
    inv = lax.rsqrt(spread + EPS)
    return [c * inv for c in centers]


def head_rows(value):
    center = value - jnp.mean(value, axis=0, keepdims=True)
    spread = jnp.mean(center * center, axis=0, keepdims=True)
    return center * lax.rsqrt(spread + EPS)


def store_head(out, result):
    out[0:HD, :] = head_rows(result[0:HD]).astype(BF)
    out[HD : 2 * HD, :] = head_rows(result[HD : 2 * HD]).astype(BF)
    out[2 * HD :, :] = result[2 * HD :].astype(BF)


def times(weight, h):
    return lax.dot_general(weight, h, (((1,), (1,)), ((), ())), preferred_element_type=F32)


def qkv_first_kernel(idx, *refs):
    shards = refs[0:8]
    shift, scale, own = refs[8:11]
    mine, other = refs[11:14], refs[14:17]
    out, h = refs[17:19]
    z, y, core = idx[0], idx[1], idx[2]
    for k in range(NZ):
        value = shards[k][...].astype(F32)
        at = lax.rem(z + k, NZ)
        (norm,) = normalized([value])
        for b in range(NY):
            cols = slice(b * QUARTER, (b + 1) * QUARTER)
            part = norm[:, cols] * (1.0 + scale[b : b + 1, :]) + shift[b : b + 1, :]
            h[b, at] = part.astype(BF)

    def tokens(b):
        return h[b].reshape(NZ * ROWS, QUARTER)

    for j in range(NY):
        if j == 0:
            total = sum(times(own[:, b * QUARTER : (b + 1) * QUARTER], tokens(b)) for b in range(NY))
        else:
            total = None
            for weight, side in ((mine[j - 1], core), (other[j - 1], 1 - core)):
                for t in range(2):
                    term = times(weight[:, t * QUARTER : (t + 1) * QUARTER], tokens(2 * side + t))
                    total = term if total is None else total + term
        store_head(out.at[lax.rem(y + j, NY)], total)


def qkv_first(idx, shards, shift, scale, own, mine, other):
    return pl.pallas_call(
        qkv_first_kernel,
        out_shape=jax.ShapeDtypeStruct((NY, 3 * HD, NZ * ROWS), BF),
        in_specs=[SM] + [VM] * 17,
        out_specs=VM,
        scratch_shapes=[pltpu.VMEM((NY, NZ, ROWS, QUARTER), BF)],
        compiler_params=params(),
        cost_estimate=pl.CostEstimate(flops=1_200_000_000, bytes_accessed=7_000_000, transcendentals=0),
        name="qkv_first",
    )(idx, *shards, shift, scale, own, *mine, *other)


def qkv_second_kernel(idx, x0, x1, x2, x3, shift, scale, mine, other, out, h):
    y, core = idx[1], idx[2]

    @pl.when(pl.program_id(0) == 0)
    def _():
        for r in range(NY):
            rows = slice(r * ROWS, (r + 1) * ROWS)
            blocks = [x[s, rows, :].astype(F32) for x in (x0, x1, x2, x3) for s in range(2)]
            norms = normalized(blocks)
            for j in range(NY):
                b = lax.rem(y + j, NY)
                for s in range(2):
                    cols = slice(s * EIGHTH, (s + 1) * EIGHTH)
                    part = norms[2 * j + s] * (1.0 + scale[b, :, cols]) + shift[b, :, cols]
                    h[b, rows, cols] = part.astype(BF)

    total = None
    for weight, side in ((mine, core), (other, 1 - core)):
        for t in range(2):
            term = times(weight[0, :, t * QUARTER : (t + 1) * QUARTER], h[2 * side + t])
            total = term if total is None else total + term
    store_head(out.at[0], total)


def qkv_second(idx, tiles, shift, scale, mine, other):
    tile = pl.BlockSpec((2, NY * ROWS, EIGHTH), lambda i: (0, 0, 0))
    mods = pl.BlockSpec((NY, 1, QUARTER), lambda i: (0, 0, 0))
    weight = pl.BlockSpec((1, 3 * HD, D // 2), lambda i: (i, 0, 0))
    return pl.pallas_call(
        qkv_second_kernel,
        grid=(NZ,),
        out_shape=jax.ShapeDtypeStruct((NZ, 3 * HD, NY * ROWS), BF),
        in_specs=[SM] + [tile] * 4 + [mods] * 2 + [weight] * 2,
        out_specs=pl.BlockSpec((1, 3 * HD, NY * ROWS), lambda i: (i, 0, 0)),
        scratch_shapes=[pltpu.VMEM((NY, NY * ROWS, QUARTER), BF)],
        compiler_params=params(),
        cost_estimate=pl.CostEstimate(flops=1_200_000_000, bytes_accessed=10_500_000, transcendentals=0),
        name="qkv_second",
    )(idx, *tiles, shift, scale, mine, other)


def attention_kernel(groups, idx, own, lower, upper, gain, out, acc, den, queries):
    length = 1024 // groups
    per = 256 // length
    g = gain[0:HD, :] * gain[HD:, :] * 0.125

    def wide(ref, n, lo, hi):
        if per == 1:
            return ref[n, lo:hi, :]
        return jnp.concatenate([ref[n * per + i, lo:hi, :] for i in range(per)], axis=1)

    for n in range(4):
        queries[n] = (wide(own, n, 0, HD).astype(F32) * g).astype(BF)
    acc[...] = jnp.zeros_like(acc)
    den[...] = jnp.zeros_like(den)

    def source(ref, first):
        def body(m, carry):
            q = queries[m]
            total = acc[m]
            norm = den[m]
            for n in range(4):
                keys = wide(ref, n, first, first + HD)
                values = wide(ref, n, first + HD, first + 2 * HD)
                score = lax.dot_general(keys, q, (((0,), (0,)), ((), ())), preferred_element_type=F32)
                e = jnp.exp(score)
                norm = norm + jnp.sum(e, axis=0, keepdims=True)
                total = total + jnp.dot(values, e.astype(BF), preferred_element_type=F32)
            acc[m] = total
            den[m] = norm
            return carry

        lax.fori_loop(0, 4, body, 0)

    source(own, HD)

    @pl.when(idx[3] == 1)
    def _():
        source(lower, 0)

    @pl.when(idx[4] == 1)
    def _():
        source(upper, 0)

    if per == 1:
        done = [acc[n] / den[n] for n in range(4)]
        for z in range(NZ):
            cols = slice(z * ROWS, (z + 1) * ROWS)
            out[z] = jnp.concatenate([d[:, cols] for d in done], axis=1).astype(BF)
    else:
        for n in range(4):
            done = (acc[n] / den[n]).astype(BF)
            for i in range(per):
                out[n * per + i] = done[:, i * length : (i + 1) * length]


def attention(idx, own, lower, upper, gain):
    groups = own.shape[0]
    return pl.pallas_call(
        functools.partial(attention_kernel, groups),
        out_shape=jax.ShapeDtypeStruct((NZ, HD, NY * ROWS), BF),
        in_specs=[SM] + [VM] * 4,
        out_specs=VM,
        scratch_shapes=[
            pltpu.VMEM((4, HD, 256), F32),
            pltpu.VMEM((4, 1, 256), F32),
            pltpu.VMEM((4, HD, 256), BF),
        ],
        compiler_params=params(),
        cost_estimate=pl.CostEstimate(flops=3_000_000_000, bytes_accessed=1_200_000, transcendentals=3_000_000),
        name="attention_%d" % groups,
    )(idx, own, lower, upper, gain)


def project_kernel(idx, o0, o1, o2, o3, mine, other, gate, x, out, joined):
    core = idx[2]
    for j, o in enumerate((o0, o1, o2, o3)):
        for z in range(NZ):
            joined[z, j] = o[z]
    rows = joined[...].reshape(NZ * NY * HD, NY * ROWS)
    for weight, side in ((mine, core), (other, 1 - core)):
        w = weight[...].reshape(NZ * NY * HD, EIGHTH)
        attn = lax.dot_general(rows, w, (((0,), (0,)), ((), ())), preferred_element_type=F32)
        out[side] = (x[side].astype(F32) + gate[side] * attn).astype(BF)


def project(idx, parts, mine, other, gate, x):
    return pl.pallas_call(
        project_kernel,
        out_shape=jax.ShapeDtypeStruct((2, NY * ROWS, EIGHTH), BF),
        in_specs=[SM] + [VM] * 8,
        out_specs=VM,
        scratch_shapes=[pltpu.VMEM((NZ, NY, HD, NY * ROWS), BF)],
        compiler_params=params(),
        cost_estimate=pl.CostEstimate(flops=420_000_000, bytes_accessed=4_000_000, transcendentals=0),
        name="project",
    )(idx, *parts, mine, other, gate, x)


def from_ahead(block, axis, size, distance):
    return lax.ppermute(block, axis, [(i, (i - distance) % size) for i in range(size)])


def swap(block):
    return lax.ppermute(block, "core", [(0, 1), (1, 0)])


def shifted(block, axis, distance):
    devices = range(lax.axis_size(axis))
    route = [(i - distance, i) for i in devices if i - distance in devices]
    return lax.ppermute(block, axis, route)


def per_device(
    latent, noise_frame, frame_pos, t_index, pos_table, mod_table, w_qkv, qk_gain, w_out
):
    core, z, y = lax.axis_index("core"), lax.axis_index("z"), lax.axis_index("y")
    slot = lax.axis_index(("x", "core"))
    slots = NX * NC
    has_prev = (slot > 0).astype(jnp.int32)
    has_next = (slot < slots - 1).astype(jnp.int32)
    idx = jnp.stack([z, y, core, has_prev, has_next]).astype(jnp.int32)
    second = z >= NZ // 2

    frame_id = jnp.where(second, frame_pos[0, 1], frame_pos[0, 0])
    pos_row = lax.dynamic_slice_in_dim(pos_table, frame_id, 1, 0)
    x0 = (latent[0].astype(F32) + pos_row.astype(F32)).astype(BF)
    mods = lax.dynamic_slice_in_dim(mod_table, t_index[0], 1, 0)[0].astype(F32)
    gates = lax.dynamic_slice_in_dim(mods[:, 2].reshape(2, NY, 2, 1, EIGHTH), y, 1, 1)[:, 0]
    gains = qk_gain[:, 0].astype(F32)[:, :, None]

    w_t = jnp.transpose(w_qkv[:, :, 0, :], (0, 2, 1))
    half = lax.dynamic_slice_in_dim(w_t, core * (D // 2), D // 2, 2)

    shards = [x0] + [from_ahead(x0, "z", NZ, k) for k in range(1, NZ)]
    mine = [from_ahead(half[0], "y", NY, j) for j in range(1, NY)]
    other = [swap(m) for m in mine]

    def out_columns(layer):
        parts = []
        for j in range(NY):
            start = lax.rem(y - j + NY, NY) * QUARTER + core * EIGHTH
            part = lax.dynamic_slice_in_dim(w_out[layer], start, EIGHTH, 1)
            parts.append(part if j == 0 else from_ahead(part, "y", NY, j))
        return lax.all_gather(jnp.stack(parts), "z", axis=0, tiled=False)

    x_split = jnp.transpose(x0.reshape(ROWS, NY, 2, EIGHTH), (1, 2, 0, 3))
    x_tile = lax.all_to_all(x_split, "y", 0, 0, tiled=True)
    x_tile = jnp.transpose(x_tile, (1, 0, 2, 3)).reshape(2, NY * ROWS, EIGHTH)

    wo_mine = out_columns(0)
    wo_other = swap(wo_mine)
    wq_mine = lax.all_gather(half[1], "z", axis=0, tiled=False)
    wq_other = swap(wq_mine)
    wo1_mine = out_columns(1)
    wo1_other = swap(wo1_mine)

    def attend(heads, axis, layer):
        own = lax.all_to_all(heads, axis, 0, 0, tiled=True)
        kv = own[:, HD:]
        lower = shifted(kv, ("x", "core"), 1)
        upper = shifted(kv, ("x", "core"), -1)
        done = attention(idx, own, lower, upper, gains[layer])
        done = lax.all_to_all(done, "z", 0, 0, tiled=True)
        return [done] + [from_ahead(done, "y", NY, j) for j in range(1, NY)]

    shift, scale = mods[0, 0].reshape(NY, QUARTER), mods[0, 1].reshape(NY, QUARTER)
    heads = qkv_first(idx, shards, shift, scale, w_t[0], mine, other)
    x_tile = project(idx, attend(heads, "y", 0), wo_mine, wo_other, gates[0], x_tile)

    tiles = [x_tile] + [from_ahead(x_tile, "y", NY, j) for j in range(1, NY)]
    shift, scale = mods[1, 0].reshape(NY, 1, QUARTER), mods[1, 1].reshape(NY, 1, QUARTER)
    heads = qkv_second(idx, tiles, shift, scale, wq_mine, wq_other)
    x_tile = project(idx, attend(heads, "z", 1), wo1_mine, wo1_other, gates[1], x_tile)

    split = jnp.transpose(x_tile.reshape(2, NY, ROWS, EIGHTH), (1, 0, 2, 3))
    rows = lax.all_to_all(split, "y", 0, 0, tiled=True)
    stream = jnp.transpose(rows, (2, 0, 1, 3)).reshape(ROWS, D)

    seq_half = NZ * NY // 2
    rank = z * NY + y
    moved = shifted(stream, ("x", "core", "z", "y"), -seq_half)
    start_row = jnp.maximum(rank - seq_half, 0) * ROWS
    fresh = lax.dynamic_slice_in_dim(noise_frame, start_row, ROWS, 0)
    at_tail = jnp.logical_and(slot == slots - 1, second)
    queue_rows = jnp.where(at_tail, fresh, moved)
    return (stream[None], queue_rows[None])


def solution(mesh):
    grid = Mesh(mesh.devices.reshape(NX, NC, NZ, NY), ("x", "core", "z", "y"))
    slot, seq = ("x", "core"), ("z", "y")
    placed = (
        P(slot, seq, None),
        P(),
        P(slot, None),
        P(slot),
        P(),
        P(),
        P(None, None, seq, None),
        P(None, seq, None),
        P(None, seq, None),
    )
    return jax.shard_map(
        per_device,
        mesh=grid,
        in_specs=placed,
        out_specs=(P(slot, seq, None), P(slot, seq, None)),
        check_vma=False,
    )
```

```python
import functools

import jax
import jax.numpy as jnp
from jax import lax
from jax.experimental import pallas as pl
from jax.experimental.pallas import tpu as pltpu
from jax.sharding import Mesh, PartitionSpec as P

BF = jnp.bfloat16
F32 = jnp.float32
EPS = 1e-6
NX, NC, NZ, NY = 4, 2, 8, 4
D = 3072
HD = 64
ROWS = 32
QUARTER = D // NY
EIGHTH = QUARTER // 2
VMEM_LIMIT = 48 * 1024 * 1024

VM = pl.BlockSpec(memory_space=pltpu.VMEM)
SM = pl.BlockSpec(memory_space=pltpu.SMEM)


def params():
    return pltpu.CompilerParams(vmem_limit_bytes=VMEM_LIMIT)


def normalized(blocks):
    mean = sum(jnp.sum(b, axis=-1, keepdims=True) for b in blocks) / D
    centers = [b - mean for b in blocks]
    spread = sum(jnp.sum(c * c, axis=-1, keepdims=True) for c in centers) / D
    inv = lax.rsqrt(spread + EPS)
    return [c * inv for c in centers]


def head_rows(value):
    center = value - jnp.mean(value, axis=0, keepdims=True)
    spread = jnp.mean(center * center, axis=0, keepdims=True)
    return center * lax.rsqrt(spread + EPS)


def store_head(out, result):
    out[0:HD, :] = head_rows(result[0:HD]).astype(BF)
    out[HD : 2 * HD, :] = head_rows(result[HD : 2 * HD]).astype(BF)
    out[2 * HD :, :] = result[2 * HD :].astype(BF)


def times(weight, h):
    return lax.dot_general(weight, h, (((1,), (1,)), ((), ())), preferred_element_type=F32)


def qkv_first_kernel(idx, *refs):
    shards = refs[0:8]
    mods, own = refs[8:10]
    mine, other = refs[10:13], refs[13:16]
    out, h = refs[16:18]
    core, z, y = idx[1], idx[2], idx[3]
    for k in range(NZ):
        value = shards[k][...].astype(F32)
        at = lax.rem(z + k, NZ)
        (norm,) = normalized([value])
        for b in range(NY):
            cols = slice(b * QUARTER, (b + 1) * QUARTER)
            part = norm[:, cols] * (1.0 + mods[1:2, cols]) + mods[0:1, cols]
            h[b, at] = part.astype(BF)

    def tokens(b):
        return h[b].reshape(NZ * ROWS, QUARTER)

    for j in range(NY):
        if j == 0:
            total = sum(times(own[0, :, b * QUARTER : (b + 1) * QUARTER], tokens(b)) for b in range(NY))
        else:
            total = None
            for weight, side in ((mine[j - 1], core), (other[j - 1], 1 - core)):
                for t in range(2):
                    term = times(weight[:, t * QUARTER : (t + 1) * QUARTER], tokens(2 * side + t))
                    total = term if total is None else total + term
        store_head(out.at[lax.rem(y + j, NY)], total)


def qkv_first(idx, shards, mods, w_t, mine, other):
    return pl.pallas_call(
        qkv_first_kernel,
        out_shape=jax.ShapeDtypeStruct((NY, 3 * HD, NZ * ROWS), BF),
        in_specs=[SM] + [VM] * 16,
        out_specs=VM,
        scratch_shapes=[pltpu.VMEM((NY, NZ, ROWS, QUARTER), BF)],
        compiler_params=params(),
        cost_estimate=pl.CostEstimate(flops=1_200_000_000, bytes_accessed=7_000_000, transcendentals=0),
        name="qkv_first",
    )(idx, *shards, mods, w_t, *mine, *other)


def qkv_second_kernel(idx, x0, x1, x2, x3, mods, weight, out, h):
    y = idx[3]

    @pl.when(pl.program_id(0) == 0)
    def _():
        for r in range(NY):
            rows = slice(r * ROWS, (r + 1) * ROWS)
            blocks = [x[s, rows, :].astype(F32) for x in (x0, x1, x2, x3) for s in range(2)]
            norms = normalized(blocks)
            for j in range(NY):
                b = lax.rem(y + j, NY)
                for s in range(2):
                    cols = pl.ds(pl.multiple_of(b * QUARTER + s * EIGHTH, 128), EIGHTH)
                    part = norms[2 * j + s] * (1.0 + mods[4:5, cols]) + mods[3:4, cols]
                    h[b, rows, s * EIGHTH : (s + 1) * EIGHTH] = part.astype(BF)

    total = None
    for b in range(NY):
        w = jnp.concatenate([weight[2 * b, 0], weight[2 * b + 1, 0]], axis=1)
        term = times(w, h[b])
        total = term if total is None else total + term
    store_head(out.at[0], total)


def qkv_second(idx, tiles, mods, weight):
    tile = pl.BlockSpec((2, NY * ROWS, EIGHTH), lambda i: (0, 0, 0))
    return pl.pallas_call(
        qkv_second_kernel,
        grid=(NZ,),
        out_shape=jax.ShapeDtypeStruct((NZ, 3 * HD, NY * ROWS), BF),
        in_specs=[SM]
        + [tile] * 4
        + [pl.BlockSpec((6, D), lambda i: (0, 0))]
        + [pl.BlockSpec((8, 1, 3 * HD, EIGHTH), lambda i: (0, i, 0, 0))],
        out_specs=pl.BlockSpec((1, 3 * HD, NY * ROWS), lambda i: (i, 0, 0)),
        scratch_shapes=[pltpu.VMEM((NY, NY * ROWS, QUARTER), BF)],
        compiler_params=params(),
        cost_estimate=pl.CostEstimate(flops=1_200_000_000, bytes_accessed=10_500_000, transcendentals=0),
        name="qkv_second",
    )(idx, *tiles, mods, weight)


def attention_kernel(groups, idx, own, lower, upper, gain, out, acc, den, queries):
    length = 1024 // groups
    per = 256 // length
    slot = idx[0] * NC + idx[1]
    column = jnp.transpose(jnp.broadcast_to(gain[...], (8, 2 * HD)))[:, 0:1]
    g = column[0:HD] * column[HD:] * 0.125

    def wide(ref, n, lo, hi):
        if per == 1:
            return ref[n, lo:hi, :]
        return jnp.concatenate([ref[n * per + i, lo:hi, :] for i in range(per)], axis=1)

    for n in range(4):
        queries[n] = (wide(own, n, 0, HD).astype(F32) * g).astype(BF)
    acc[...] = jnp.zeros_like(acc)
    den[...] = jnp.zeros_like(den)

    def source(ref, first):
        def body(m, carry):
            q = queries[m]
            total = acc[m]
            norm = den[m]
            for n in range(4):
                keys = wide(ref, n, first, first + HD)
                values = wide(ref, n, first + HD, first + 2 * HD)
                score = lax.dot_general(keys, q, (((0,), (0,)), ((), ())), preferred_element_type=F32)
                e = jnp.exp(score)
                norm = norm + jnp.sum(e, axis=0, keepdims=True)
                total = total + jnp.dot(values, e.astype(BF), preferred_element_type=F32)
            acc[m] = total
            den[m] = norm
            return carry

        lax.fori_loop(0, 4, body, 0)

    source(own, HD)

    @pl.when(slot > 0)
    def _():
        source(lower, 0)

    @pl.when(slot < NX * NC - 1)
    def _():
        source(upper, 0)

    if per == 1:
        done = [acc[n] / den[n] for n in range(4)]
        for z in range(NZ):
            cols = slice(z * ROWS, (z + 1) * ROWS)
            out[z] = jnp.concatenate([d[:, cols] for d in done], axis=1).astype(BF)
    else:
        for n in range(4):
            done = (acc[n] / den[n]).astype(BF)
            for i in range(per):
                out[n * per + i] = done[:, i * length : (i + 1) * length]


def attention(idx, own, lower, upper, gain):
    groups = own.shape[0]
    return pl.pallas_call(
        functools.partial(attention_kernel, groups),
        out_shape=jax.ShapeDtypeStruct((NZ, HD, NY * ROWS), BF),
        in_specs=[SM] + [VM] * 4,
        out_specs=VM,
        scratch_shapes=[
            pltpu.VMEM((4, HD, 256), F32),
            pltpu.VMEM((4, 1, 256), F32),
            pltpu.VMEM((4, HD, 256), BF),
        ],
        compiler_params=params(),
        cost_estimate=pl.CostEstimate(flops=3_000_000_000, bytes_accessed=1_200_000, transcendentals=3_000_000),
        name="attention_%d" % groups,
    )(idx, own, lower, upper, gain)


def project_kernel(layer, relative, idx, o0, o1, o2, o3, *refs):
    weights = refs[: 2 if relative else 1]
    mods, x, out, absolute = refs[len(weights) :]
    x_pos, core, y = idx[0], idx[1], idx[3]
    for j, o in enumerate((o0, o1, o2, o3)):
        b = lax.rem(y + j, NY)
        for z in range(NZ):
            for half in range(2):
                absolute[b, half, z] = o[z, half * ROWS : (half + 1) * ROWS, :]
    for h in range(2):
        attn = None
        for n, weight in enumerate(weights):
            if relative:
                side = core if n == 0 else 1 - core
                rows = [absolute[lax.rem(x_pos + k, NX), side] for k in range(NX)]
            else:
                rows = [absolute[s // 2, s % 2] for s in range(8)]
            rows = jnp.concatenate([r.reshape(NZ * ROWS, NY * ROWS) for r in rows], axis=0)
            w = weight[:, :, h * ROWS : (h + 1) * ROWS, :].reshape(-1, EIGHTH)
            term = lax.dot_general(rows, w, (((0,), (0,)), ((), ())), preferred_element_type=F32)
            attn = term if attn is None else attn + term
        cols = pl.ds(pl.multiple_of(y * QUARTER + h * EIGHTH, 128), EIGHTH)
        gate = mods[3 * layer + 2 : 3 * layer + 3, cols]
        out[h] = (x[h].astype(F32) + gate * attn).astype(BF)


def project(layer, idx, parts, weights, mods, x):
    relative = len(weights) == 2
    return pl.pallas_call(
        functools.partial(project_kernel, layer, relative),
        out_shape=jax.ShapeDtypeStruct((2, NY * ROWS, EIGHTH), BF),
        in_specs=[SM] + [VM] * (6 + len(weights)),
        out_specs=VM,
        scratch_shapes=[pltpu.VMEM((NY, 2, NZ, ROWS, NY * ROWS), BF)],
        compiler_params=params(),
        cost_estimate=pl.CostEstimate(flops=420_000_000, bytes_accessed=4_000_000, transcendentals=0),
        name="project_%d" % layer,
    )(idx, *parts, *weights, mods, x)


def finish_kernel(idx, rows, q0, q1, q2, q3, fresh, out, queue):
    slot = idx[0] * NC + idx[1]
    z, y = idx[2], idx[3]
    for b in range(NY):
        for h in range(2):
            out[:, b * QUARTER + h * EIGHTH : b * QUARTER + (h + 1) * EIGHTH] = rows[b, h]
    tail = jnp.logical_and(slot == NX * NC - 1, z >= NZ // 2)

    @pl.when(tail)
    def _():
        queue[...] = fresh[...]

    @pl.when(jnp.logical_not(tail))
    def _():
        for j, q in enumerate((q0, q1, q2, q3)):
            b = lax.rem(y - j + NY, NY)
            for h in range(2):
                cols = pl.ds(pl.multiple_of(b * QUARTER + h * EIGHTH, 128), EIGHTH)
                queue[:, cols] = q[h]


def finish(idx, rows, pieces, fresh):
    shape = jax.ShapeDtypeStruct((ROWS, D), BF)
    return pl.pallas_call(
        finish_kernel,
        out_shape=(shape, shape),
        in_specs=[SM] + [VM] * 6,
        out_specs=(VM, VM),
        compiler_params=params(),
        cost_estimate=pl.CostEstimate(flops=0, bytes_accessed=800_000, transcendentals=0),
        name="finish",
    )(idx, rows, *pieces, fresh)


def from_ahead(block, axis, size, distance):
    return lax.ppermute(block, axis, [(i, (i - distance) % size) for i in range(size)])


def swap(block):
    return lax.ppermute(block, "core", [(0, 1), (1, 0)])


def shifted(block, axis, distance):
    devices = range(lax.axis_size(axis))
    route = [(i - distance, i) for i in devices if i - distance in devices]
    return lax.ppermute(block, axis, route)


def after(value, *others):
    return lax.optimization_barrier((value, *others))[0]


ALL = ("x", "core", "z", "y")
SEQ = NZ * NY


def per_device(
    latent, noise_frame, frame_pos, t_index, pos_table, mod_table, w_qkv, qk_gain, w_out
):
    x_pos, core = lax.axis_index("x"), lax.axis_index("core")
    z, y = lax.axis_index("z"), lax.axis_index("y")
    slot = x_pos * NC + core
    idx = jnp.stack([x_pos, core, z, y]).astype(jnp.int32)

    frame_id = jnp.where(z >= NZ // 2, frame_pos[0, 1], frame_pos[0, 0])
    pos_row = lax.dynamic_slice_in_dim(pos_table, frame_id, 1, 0)
    x0 = (latent[0].astype(F32) + pos_row.astype(F32)).astype(BF)
    mods = lax.dynamic_slice_in_dim(mod_table, t_index[0], 1, 0)[0].astype(F32).reshape(6, D)
    gains = qk_gain[:, 0].astype(F32)
    w_t = jnp.transpose(w_qkv[:, :, 0, :], (0, 2, 1))

    half = lax.dynamic_slice_in_dim(w_t[0], core * (D // 2), D // 2, 1)
    mine = [from_ahead(half, "y", NY, j) for j in range(1, NY)]
    ahead, behind = [x0], [x0]
    for _ in range(NZ // 2):
        ahead.append(from_ahead(ahead[-1], "z", NZ, 1))
    for _ in range(NZ // 2 - 1):
        behind.append(from_ahead(behind[-1], "z", NZ, -1))
    shards = ahead + behind[:0:-1]
    other = [swap(m) for m in mine]

    rows_half = lax.dynamic_slice_in_dim(w_out, core * ROWS, ROWS, 1)
    wo = None
    for j in range(NY):
        columns = lax.dynamic_slice_in_dim(rows_half, lax.rem(y + j, NY) * QUARTER, QUARTER, 2)
        if j:
            route = [
                ((s * NZ + c) * NY + s // NC, (s * NZ + c) * NY + (s // NC + j) % NY)
                for s in range(NX * NC)
                for c in range(NZ)
            ]
            columns = lax.ppermute(columns, ALL, route)
        else:
            columns = jnp.where(y == x_pos, columns, jnp.zeros_like(columns))
        wo = columns if wo is None else wo + columns
    wo = jnp.transpose(wo.reshape(2, ROWS, 2, EIGHTH), (0, 2, 1, 3)).reshape(4 * ROWS, EIGHTH)
    wq = lax.dynamic_slice_in_dim(w_t[1], slot * EIGHTH, EIGHTH, 1)
    later = lax.all_gather(jnp.concatenate([wq, wo], axis=0), "z", axis=0, tiled=False)

    x_split = jnp.transpose(x0.reshape(ROWS, NY, 2, EIGHTH), (1, 2, 0, 3))
    x_tile = lax.all_to_all(x_split, "y", 0, 0, tiled=True)
    x_tile = jnp.transpose(x_tile, (1, 0, 2, 3)).reshape(2, NY * ROWS, EIGHTH)

    def attend(own, layer):
        kv = own[:, HD:]
        lower = shifted(kv, ("x", "core"), 1)
        upper = shifted(kv, ("x", "core"), -1)
        done = attention(idx, own, lower, upper, gains[layer : layer + 1])
        done = lax.all_to_all(done, "z", 0, 0, tiled=True)
        return [done] + [from_ahead(done, "y", NY, j) for j in range(1, NY)]

    heads = qkv_first(idx, shards, mods, w_t, mine, other)
    heads, later, x_tile = lax.optimization_barrier((heads, later, x_tile))
    wq1 = lax.all_gather(later[:, : 3 * HD], ("x", "core"), axis=0, tiled=False)
    wo0 = later[:, 3 * HD : 3 * HD + 2 * ROWS]
    wo0 = jnp.stack([wo0] + [from_ahead(wo0, "x", NX, k) for k in range(1, NX)])
    wo0 = [wo0, swap(wo0)]
    wo1 = lax.all_gather(later[:, 3 * HD + 2 * ROWS :], ("x", "core"), axis=0, tiled=False)

    own = lax.all_to_all(heads, "y", 0, 0, tiled=True)
    x_tile = project(0, idx, attend(own, 0), wo0, mods, x_tile)

    tiles = [x_tile] + [from_ahead(x_tile, "y", NY, j) for j in range(1, NY)]
    heads = qkv_second(idx, tiles, mods, wq1)
    own = lax.all_to_all(heads, "z", 0, 0, tiled=True)
    x_tile = project(1, idx, attend(own, 1), [wo1], mods, x_tile)

    split = x_tile.reshape(2, NY, ROWS, EIGHTH)
    rows = lax.all_to_all(jnp.transpose(split, (1, 0, 2, 3)), "y", 0, 0, tiled=True)
    pieces = []
    for j in range(NY):
        piece = lax.dynamic_index_in_dim(split, lax.rem(y + j, NY), 1, keepdims=False)
        route = []
        for source in range(NX * NC * SEQ):
            target = source - source % NY + (source + j) % NY - SEQ // 2
            if target >= 0:
                route.append((source, target))
        pieces.append(lax.ppermute(piece, ALL, route))
    start_row = jnp.maximum(z * NY + y - SEQ // 2, 0) * ROWS
    fresh = lax.dynamic_slice_in_dim(noise_frame, start_row, ROWS, 0)
    stream, queue = finish(idx, rows, pieces, fresh)
    return (stream[None], queue[None])


def solution(mesh):
    grid = Mesh(mesh.devices.reshape(NX, NC, NZ, NY), ("x", "core", "z", "y"))
    slot, seq = ("x", "core"), ("z", "y")
    placed = (
        P(slot, seq, None),
        P(),
        P(slot, None),
        P(slot),
        P(),
        P(),
        P(None, None, seq, None),
        P(None, seq, None),
        P(None, seq, None),
    )
    return jax.shard_map(
        per_device,
        mesh=grid,
        in_specs=placed,
        out_specs=(P(slot, seq, None), P(slot, seq, None)),
        check_vma=False,
    )
```

```python
import functools

import jax
import jax.numpy as jnp
from jax import lax
from jax.experimental import pallas as pl
from jax.experimental.pallas import tpu as pltpu
from jax.sharding import Mesh, PartitionSpec as P

BF = jnp.bfloat16
F32 = jnp.float32
EPS = 1e-6
NX, NC, NZ, NY = 4, 2, 8, 4
D = 3072
HD = 64
ROWS = 32
QUARTER = D // NY
EIGHTH = QUARTER // 2
VMEM_LIMIT = 48 * 1024 * 1024

VM = pl.BlockSpec(memory_space=pltpu.VMEM)
SM = pl.BlockSpec(memory_space=pltpu.SMEM)


def params():
    return pltpu.CompilerParams(vmem_limit_bytes=VMEM_LIMIT)


def normalized(blocks):
    mean = sum(jnp.sum(b, axis=-1, keepdims=True) for b in blocks) / D
    centers = [b - mean for b in blocks]
    spread = sum(jnp.sum(c * c, axis=-1, keepdims=True) for c in centers) / D
    inv = lax.rsqrt(spread + EPS)
    return [c * inv for c in centers]


def head_rows(value):
    center = value - jnp.mean(value, axis=0, keepdims=True)
    spread = jnp.mean(center * center, axis=0, keepdims=True)
    return center * lax.rsqrt(spread + EPS)


def store_head(out, result):
    out[0:HD, :] = head_rows(result[0:HD]).astype(BF)
    out[HD : 2 * HD, :] = head_rows(result[HD : 2 * HD]).astype(BF)
    out[2 * HD :, :] = result[2 * HD :].astype(BF)


def times(weight, h):
    return lax.dot_general(weight, h, (((1,), (1,)), ((), ())), preferred_element_type=F32)


def qkv_first_kernel(idx, *refs):
    shards = refs[0:8]
    mods, own = refs[8:10]
    mine, other = refs[10:13], refs[13:16]
    out, h = refs[16:18]
    core, z, y = idx[1], idx[2], idx[3]
    for k in range(NZ):
        value = shards[k][...].astype(F32)
        at = lax.rem(z + k, NZ)
        (norm,) = normalized([value])
        for b in range(NY):
            cols = slice(b * QUARTER, (b + 1) * QUARTER)
            part = norm[:, cols] * (1.0 + mods[1:2, cols]) + mods[0:1, cols]
            h[b, at] = part.astype(BF)

    def tokens(b):
        return h[b].reshape(NZ * ROWS, QUARTER)

    for j in range(NY):
        if j == 0:
            total = sum(times(own[0, :, b * QUARTER : (b + 1) * QUARTER], tokens(b)) for b in range(NY))
        else:
            total = None
            for weight, side in ((mine[j - 1], core), (other[j - 1], 1 - core)):
                for t in range(2):
                    term = times(weight[:, t * QUARTER : (t + 1) * QUARTER], tokens(2 * side + t))
                    total = term if total is None else total + term
        store_head(out.at[lax.rem(y + j, NY)], total)


def qkv_first(idx, shards, mods, w_t, mine, other):
    return pl.pallas_call(
        qkv_first_kernel,
        out_shape=jax.ShapeDtypeStruct((NY, 3 * HD, NZ * ROWS), BF),
        in_specs=[SM] + [VM] * 16,
        out_specs=VM,
        scratch_shapes=[pltpu.VMEM((NY, NZ, ROWS, QUARTER), BF)],
        compiler_params=params(),
        cost_estimate=pl.CostEstimate(flops=1_200_000_000, bytes_accessed=7_000_000, transcendentals=0),
        name="qkv_first",
    )(idx, *shards, mods, w_t, *mine, *other)


def qkv_second_kernel(idx, x0, x1, x2, x3, mods, weight, out, h):
    y = idx[3]

    @pl.when(pl.program_id(0) == 0)
    def _():
        for j, x in enumerate((x0, x1, x2, x3)):
            (norm,) = normalized([x[...].astype(F32)])
            at = lax.rem(y + j, NY)
            for b in range(NY):
                cols = slice(b * QUARTER, (b + 1) * QUARTER)
                part = norm[:, cols] * (1.0 + mods[4:5, cols]) + mods[3:4, cols]
                h[b, at] = part.astype(BF)

    total = None
    for b in range(NY):
        w = jnp.concatenate([weight[2 * b, 0], weight[2 * b + 1, 0]], axis=1)
        term = times(w, h[b].reshape(NY * ROWS, QUARTER))
        total = term if total is None else total + term
    store_head(out.at[0], total)


def qkv_second(idx, shards, mods, weight):
    shard = pl.BlockSpec((ROWS, D), lambda i: (0, 0))
    return pl.pallas_call(
        qkv_second_kernel,
        grid=(NZ,),
        out_shape=jax.ShapeDtypeStruct((NZ, 3 * HD, NY * ROWS), BF),
        in_specs=[SM]
        + [shard] * 4
        + [pl.BlockSpec((6, D), lambda i: (0, 0))]
        + [pl.BlockSpec((8, 1, 3 * HD, EIGHTH), lambda i: (0, i, 0, 0))],
        out_specs=pl.BlockSpec((1, 3 * HD, NY * ROWS), lambda i: (i, 0, 0)),
        scratch_shapes=[pltpu.VMEM((NY, NY, ROWS, QUARTER), BF)],
        compiler_params=params(),
        cost_estimate=pl.CostEstimate(flops=1_200_000_000, bytes_accessed=10_500_000, transcendentals=0),
        name="qkv_second",
    )(idx, *shards, mods, weight)


def attention_kernel(groups, idx, own, lower, upper, gain, out, acc, den, queries):
    length = 1024 // groups
    per = 256 // length
    slot = idx[0] * NC + idx[1]
    column = jnp.transpose(jnp.broadcast_to(gain[...], (8, 2 * HD)))[:, 0:1]
    g = column[0:HD] * column[HD:] * 0.125

    def wide(ref, n, lo, hi):
        if per == 1:
            return ref[n, lo:hi, :]
        return jnp.concatenate([ref[n * per + i, lo:hi, :] for i in range(per)], axis=1)

    for n in range(4):
        queries[n] = (wide(own, n, 0, HD).astype(F32) * g).astype(BF)
    acc[...] = jnp.zeros_like(acc)
    den[...] = jnp.zeros_like(den)

    def source(ref, first):
        def body(m, carry):
            q = queries[m]
            total = acc[m]
            norm = den[m]
            for n in range(4):
                keys = wide(ref, n, first, first + HD)
                values = wide(ref, n, first + HD, first + 2 * HD)
                score = lax.dot_general(keys, q, (((0,), (0,)), ((), ())), preferred_element_type=F32)
                e = jnp.exp(score)
                norm = norm + jnp.sum(e, axis=0, keepdims=True)
                total = total + jnp.dot(values, e.astype(BF), preferred_element_type=F32)
            acc[m] = total
            den[m] = norm
            return carry

        lax.fori_loop(0, 4, body, 0)

    source(own, HD)

    @pl.when(slot > 0)
    def _():
        source(lower, 0)

    @pl.when(slot < NX * NC - 1)
    def _():
        source(upper, 0)

    if per == 1:
        done = [acc[n] / den[n] for n in range(4)]
        for z in range(NZ):
            cols = slice(z * ROWS, (z + 1) * ROWS)
            out[z] = jnp.concatenate([d[:, cols] for d in done], axis=1).astype(BF)
    else:
        for n in range(4):
            done = (acc[n] / den[n]).astype(BF)
            for i in range(per):
                out[n * per + i] = done[:, i * length : (i + 1) * length]


def attention(idx, own, lower, upper, gain):
    groups = own.shape[0]
    return pl.pallas_call(
        functools.partial(attention_kernel, groups),
        out_shape=jax.ShapeDtypeStruct((NZ, HD, NY * ROWS), BF),
        in_specs=[SM] + [VM] * 4,
        out_specs=VM,
        scratch_shapes=[
            pltpu.VMEM((4, HD, 256), F32),
            pltpu.VMEM((4, 1, 256), F32),
            pltpu.VMEM((4, HD, 256), BF),
        ],
        compiler_params=params(),
        cost_estimate=pl.CostEstimate(flops=3_000_000_000, bytes_accessed=1_200_000, transcendentals=3_000_000),
        name="attention_%d" % groups,
    )(idx, own, lower, upper, gain)


def project_kernel(relative, idx, o, *refs):
    weights, out = refs[:-1], refs[-1]
    rows = o[...].reshape(NZ * HD, NY * ROWS)

    def put(weight, eighth):
        w = weight.reshape(NZ * HD, EIGHTH)
        term = lax.dot_general(rows, w, (((0,), (0,)), ((), ())), preferred_element_type=F32)
        if isinstance(eighth, int):
            cols = slice(eighth * EIGHTH, (eighth + 1) * EIGHTH)
        else:
            cols = pl.ds(pl.multiple_of(eighth * EIGHTH, 128), EIGHTH)
        out[:, cols] = term.astype(BF)

    if relative:
        x_pos, core = idx[0], idx[1]
        for k in range(NX):
            at = lax.rem(x_pos + k, NX) * NC
            put(weights[k][...], at + core)
            put(weights[NX][k], at + 1 - core)
    else:
        for s in range(NX * NC):
            put(weights[0][s], s)


def project(layer, idx, o, weights):
    relative = len(weights) > 1
    out = pl.pallas_call(
        functools.partial(project_kernel, relative),
        out_shape=jax.ShapeDtypeStruct((NY * ROWS, D), BF),
        in_specs=[SM] + [VM] * (1 + len(weights)),
        out_specs=VM,
        compiler_params=params(),
        cost_estimate=pl.CostEstimate(flops=420_000_000, bytes_accessed=4_000_000, transcendentals=0),
        name="project_%d" % layer,
    )(idx, o, *weights)
    return out.reshape(NY, ROWS, D)


def residual_kernel(layer, terms, mods, x, out):
    attn = sum(terms[j].astype(F32) for j in range(NY))
    gate = mods[3 * layer + 2 : 3 * layer + 3, :]
    out[...] = (x[...].astype(F32) + gate * attn).astype(BF)


def residual(layer, terms, mods, x):
    return pl.pallas_call(
        functools.partial(residual_kernel, layer),
        out_shape=jax.ShapeDtypeStruct((ROWS, D), BF),
        in_specs=[VM] * 3,
        out_specs=VM,
        compiler_params=params(),
        cost_estimate=pl.CostEstimate(flops=600_000, bytes_accessed=1_400_000, transcendentals=0),
        name="residual_%d" % layer,
    )(terms, mods, x)


def from_ahead(block, axis, size, distance):
    return lax.ppermute(block, axis, [(i, (i - distance) % size) for i in range(size)])


def swap(block):
    return lax.ppermute(block, "core", [(0, 1), (1, 0)])


def shifted(block, axis, distance):
    devices = range(lax.axis_size(axis))
    route = [(i - distance, i) for i in devices if i - distance in devices]
    return lax.ppermute(block, axis, route)


def after(value, *others):
    return lax.optimization_barrier((value, *others))[0]


SEQ = NZ * NY


def per_device(
    latent, noise_frame, frame_pos, t_index, pos_table, mod_table, w_qkv, qk_gain, w_out
):
    x_pos, core = lax.axis_index("x"), lax.axis_index("core")
    z, y = lax.axis_index("z"), lax.axis_index("y")
    slot = x_pos * NC + core
    idx = jnp.stack([x_pos, core, z, y]).astype(jnp.int32)

    frame_id = jnp.where(z >= NZ // 2, frame_pos[0, 1], frame_pos[0, 0])
    pos_row = lax.dynamic_slice_in_dim(pos_table, frame_id, 1, 0)
    x0 = (latent[0].astype(F32) + pos_row.astype(F32)).astype(BF)
    mods = lax.dynamic_slice_in_dim(mod_table, t_index[0], 1, 0)[0].astype(F32).reshape(6, D)
    gains = qk_gain[:, 0].astype(F32)
    w_t = jnp.transpose(w_qkv[:, :, 0, :], (0, 2, 1))

    half = lax.dynamic_slice_in_dim(w_t[0], core * (D // 2), D // 2, 1)
    mine = [from_ahead(half, "y", NY, j) for j in range(1, NY)]
    ahead, behind = [x0], [x0]
    for _ in range(NZ // 2):
        ahead.append(from_ahead(ahead[-1], "z", NZ, 1))
    for _ in range(NZ // 2 - 1):
        behind.append(from_ahead(behind[-1], "z", NZ, -1))
    shards = ahead + behind[:0:-1]
    other = [swap(m) for m in mine]

    eighth = lambda w: lax.dynamic_slice_in_dim(w, slot * EIGHTH, EIGHTH, 1)
    pack = jnp.concatenate([eighth(w_t[1]), eighth(w_out[0]), eighth(w_out[1])], axis=0)
    later = lax.all_gather(after(pack, x0), "z", axis=0, tiled=False)

    def attend(own, layer):
        kv = own[:, HD:]
        lower = shifted(kv, ("x", "core"), 1)
        upper = shifted(kv, ("x", "core"), -1)
        return attention(idx, own, lower, upper, gains[layer : layer + 1])

    heads = qkv_first(idx, shards, mods, w_t, mine, other)
    heads, later = lax.optimization_barrier((heads, later))
    wq1 = lax.all_gather(later[:, : 3 * HD], ("x", "core"), axis=0, tiled=False)

    own = lax.all_to_all(heads, "y", 0, 0, tiled=True)
    own, later = lax.optimization_barrier((own, later))
    wo0 = later[:, 3 * HD : 4 * HD]
    wo0 = [wo0] + [from_ahead(wo0, "x", NX, k) for k in range(1, NX)]
    wo1 = lax.all_gather(later[:, 4 * HD :], ("x", "core"), axis=0, tiled=False)
    done, *wo0 = lax.optimization_barrier((attend(own, 0), *wo0))
    wo0 = [*wo0, swap(jnp.stack(wo0))]
    done = lax.all_to_all(done, "z", 0, 0, tiled=True)
    terms = lax.all_to_all(project(0, idx, done, wo0), "y", 0, 0, tiled=True)
    x1 = residual(0, terms, mods, x0)

    shards = [x1] + [from_ahead(x1, "y", NY, j) for j in range(1, NY)]
    heads = qkv_second(idx, shards, mods, wq1)
    own = lax.all_to_all(heads, "z", 0, 0, tiled=True)
    done = lax.all_to_all(attend(own, 1), "z", 0, 0, tiled=True)
    terms = lax.all_to_all(project(1, idx, done, [wo1]), "y", 0, 0, tiled=True)
    stream = residual(1, terms, mods, x1)

    moved = shifted(stream, ("x", "core", "z", "y"), -(SEQ // 2))
    start_row = jnp.maximum(z * NY + y - SEQ // 2, 0) * ROWS
    fresh = lax.dynamic_slice_in_dim(noise_frame, start_row, ROWS, 0)
    tail = jnp.logical_and(slot == NX * NC - 1, z >= NZ // 2)
    queue = jnp.where(tail, fresh, moved)
    return (stream[None], queue[None])


def solution(mesh):
    grid = Mesh(mesh.devices.reshape(NX, NC, NZ, NY), ("x", "core", "z", "y"))
    slot, seq = ("x", "core"), ("z", "y")
    placed = (
        P(slot, seq, None),
        P(),
        P(slot, None),
        P(slot),
        P(),
        P(),
        P(None, None, seq, None),
        P(None, seq, None),
        P(None, seq, None),
    )
    return jax.shard_map(
        per_device,
        mesh=grid,
        in_specs=placed,
        out_specs=(P(slot, seq, None), P(slot, seq, None)),
        check_vma=False,
    )
```

```python
import functools

import jax
import jax.numpy as jnp
from jax import lax
from jax.experimental import pallas as pl
from jax.experimental.pallas import tpu as pltpu
from jax.sharding import Mesh, PartitionSpec as P

BF = jnp.bfloat16
F32 = jnp.float32
EPS = 1e-6
NX, NC, NZ, NY = 4, 2, 8, 4
D = 3072
HD = 64
ROWS = 32
QUARTER = D // NY
EIGHTH = QUARTER // 2
PACK = (8 * ROWS, 3 * HD, 4 * HD, HD)
VMEM_LIMIT = 48 * 1024 * 1024

VM = pl.BlockSpec(memory_space=pltpu.VMEM)
SM = pl.BlockSpec(memory_space=pltpu.SMEM)


def params():
    return pltpu.CompilerParams(vmem_limit_bytes=VMEM_LIMIT)


def normalized(blocks):
    mean = sum(jnp.sum(b, axis=-1, keepdims=True) for b in blocks) / D
    centers = [b - mean for b in blocks]
    spread = sum(jnp.sum(c * c, axis=-1, keepdims=True) for c in centers) / D
    inv = lax.rsqrt(spread + EPS)
    return [c * inv for c in centers]


def head_rows(value):
    center = value - jnp.mean(value, axis=0, keepdims=True)
    spread = jnp.mean(center * center, axis=0, keepdims=True)
    return center * lax.rsqrt(spread + EPS)


def store_head(out, result):
    out[0:HD, :] = head_rows(result[0:HD]).astype(BF)
    out[HD : 2 * HD, :] = head_rows(result[HD : 2 * HD]).astype(BF)
    out[2 * HD :, :] = result[2 * HD :].astype(BF)


def times(weight, h):
    return lax.dot_general(weight, h, (((1,), (1,)), ((), ())), preferred_element_type=F32)


def qkv_first_kernel(idx, later, mods, w_t, *refs):
    mine, other = refs[0:3], refs[3:6]
    out, wq, wo0, wo1, h, x, own, sems = refs[6:]
    core, y = idx[1], idx[3]
    copies = []
    row = 0
    for n, (rows, target) in enumerate(zip(PACK, (x, wq, wo0, wo1))):
        copies.append(pltpu.make_async_copy(later.at[:, row : row + rows, :], target, sems.at[n]))
        row += rows
    copies.insert(1, pltpu.make_async_copy(w_t.at[0], own, sems.at[4]))
    for copy in copies:
        copy.start()
    copies[0].wait()
    for z in range(NZ):
        blocks = [x[z, e * ROWS : (e + 1) * ROWS, :].astype(F32) for e in range(8)]
        for e, norm in enumerate(normalized(blocks)):
            cols = slice(e * EIGHTH, (e + 1) * EIGHTH)
            part = norm * (1.0 + mods[1:2, cols]) + mods[0:1, cols]
            h[e // 2, z, :, (e % 2) * EIGHTH : (e % 2 + 1) * EIGHTH] = part.astype(BF)

    def tokens(b):
        return h[b].reshape(NZ * ROWS, QUARTER)

    copies[1].wait()
    for j in range(NY):
        if j == 0:
            total = sum(times(own[:, b * QUARTER : (b + 1) * QUARTER], tokens(b)) for b in range(NY))
        else:
            total = None
            for weight, side in ((mine[j - 1], core), (other[j - 1], 1 - core)):
                for t in range(2):
                    term = times(weight[:, t * QUARTER : (t + 1) * QUARTER], tokens(2 * side + t))
                    total = term if total is None else total + term
        store_head(out.at[lax.rem(y + j, NY)], total)
    for copy in copies[2:]:
        copy.wait()


def qkv_first(idx, later, mods, w_t, mine, other):
    anywhere = pl.BlockSpec(memory_space=pl.ANY)
    return pl.pallas_call(
        qkv_first_kernel,
        out_shape=[jax.ShapeDtypeStruct((NY, 3 * HD, NZ * ROWS), BF)]
        + [jax.ShapeDtypeStruct((NZ, rows, EIGHTH), BF) for rows in PACK[1:]],
        in_specs=[SM, anywhere, VM, anywhere] + [VM] * 6,
        out_specs=[VM] + [anywhere] * 3,
        scratch_shapes=[
            pltpu.VMEM((NY, NZ, ROWS, QUARTER), BF),
            pltpu.VMEM((NZ, PACK[0], EIGHTH), BF),
            pltpu.VMEM((3 * HD, D), BF),
            pltpu.SemaphoreType.DMA((5,)),
        ],
        compiler_params=params(),
        cost_estimate=pl.CostEstimate(flops=1_200_000_000, bytes_accessed=14_000_000, transcendentals=0),
        name="qkv_first",
    )(idx, later, mods, w_t, *mine, *other)


def qkv_second_kernel(idx, x0, x1, x2, x3, mods, weight, out, h):
    y = idx[3]

    @pl.when(pl.program_id(0) == 0)
    def _():
        for j, x in enumerate((x0, x1, x2, x3)):
            (norm,) = normalized([x[...].astype(F32)])
            at = lax.rem(y + j, NY)
            for b in range(NY):
                cols = slice(b * QUARTER, (b + 1) * QUARTER)
                part = norm[:, cols] * (1.0 + mods[4:5, cols]) + mods[3:4, cols]
                h[b, at] = part.astype(BF)

    total = None
    for b in range(NY):
        w = jnp.concatenate([weight[2 * b, 0], weight[2 * b + 1, 0]], axis=1)
        term = times(w, h[b].reshape(NY * ROWS, QUARTER))
        total = term if total is None else total + term
    store_head(out.at[0], total)


def qkv_second(idx, shards, mods, weight):
    shard = pl.BlockSpec((ROWS, D), lambda i: (0, 0))
    return pl.pallas_call(
        qkv_second_kernel,
        grid=(NZ,),
        out_shape=jax.ShapeDtypeStruct((NZ, 3 * HD, NY * ROWS), BF),
        in_specs=[SM]
        + [shard] * 4
        + [pl.BlockSpec((6, D), lambda i: (0, 0))]
        + [pl.BlockSpec((8, 1, 3 * HD, EIGHTH), lambda i: (0, i, 0, 0))],
        out_specs=pl.BlockSpec((1, 3 * HD, NY * ROWS), lambda i: (i, 0, 0)),
        scratch_shapes=[pltpu.VMEM((NY, NY, ROWS, QUARTER), BF)],
        compiler_params=params(),
        cost_estimate=pl.CostEstimate(flops=1_200_000_000, bytes_accessed=10_500_000, transcendentals=0),
        name="qkv_second",
    )(idx, *shards, mods, weight)


def attention_kernel(groups, idx, own, lower, upper, gain, out, acc, den, queries):
    length = 1024 // groups
    per = 256 // length
    slot = idx[0] * NC + idx[1]
    column = jnp.transpose(jnp.broadcast_to(gain[...], (8, 2 * HD)))[:, 0:1]
    g = column[0:HD] * column[HD:] * 0.125

    def wide(ref, n, lo, hi):
        if per == 1:
            return ref[n, lo:hi, :]
        return jnp.concatenate([ref[n * per + i, lo:hi, :] for i in range(per)], axis=1)

    for n in range(4):
        queries[n] = (wide(own, n, 0, HD).astype(F32) * g).astype(BF)
    acc[...] = jnp.zeros_like(acc)
    den[...] = jnp.zeros_like(den)

    def source(ref):
        def body(m, carry):
            q = queries[m]
            total = acc[m]
            norm = den[m]
            for n in range(4):
                keys = wide(ref, n, HD, 2 * HD)
                values = wide(ref, n, 2 * HD, 3 * HD)
                score = lax.dot_general(keys, q, (((0,), (0,)), ((), ())), preferred_element_type=F32)
                e = jnp.exp(score)
                norm = norm + jnp.sum(e, axis=0, keepdims=True)
                total = total + jnp.dot(values, e.astype(BF), preferred_element_type=F32)
            acc[m] = total
            den[m] = norm
            return carry

        lax.fori_loop(0, 4, body, 0)

    source(own)

    @pl.when(slot > 0)
    def _():
        source(lower)

    @pl.when(slot < NX * NC - 1)
    def _():
        source(upper)

    if per == 1:
        done = [acc[n] / den[n] for n in range(4)]
        for z in range(NZ):
            cols = slice(z * ROWS, (z + 1) * ROWS)
            out[z] = jnp.concatenate([d[:, cols] for d in done], axis=1).astype(BF)
    else:
        for n in range(4):
            done = (acc[n] / den[n]).astype(BF)
            for i in range(per):
                out[n * per + i] = done[:, i * length : (i + 1) * length]


def attention(idx, own, lower, upper, gain):
    groups = own.shape[0]
    return pl.pallas_call(
        functools.partial(attention_kernel, groups),
        out_shape=jax.ShapeDtypeStruct((NZ, HD, NY * ROWS), BF),
        in_specs=[SM] + [VM] * 4,
        out_specs=VM,
        scratch_shapes=[
            pltpu.VMEM((4, HD, 256), F32),
            pltpu.VMEM((4, 1, 256), F32),
            pltpu.VMEM((4, HD, 256), BF),
        ],
        compiler_params=params(),
        cost_estimate=pl.CostEstimate(flops=3_000_000_000, bytes_accessed=1_200_000, transcendentals=3_000_000),
        name="attention_%d" % groups,
    )(idx, own, lower, upper, gain)


def project_kernel(halves, idx, o, *refs):
    weights, out = refs[:-1], refs[-1]
    rows = o[...].reshape(NZ * HD, NY * ROWS)

    def put(w, eighth):
        term = lax.dot_general(rows, w, (((0,), (0,)), ((), ())), preferred_element_type=F32)
        if isinstance(eighth, int):
            cols = slice(eighth * EIGHTH, (eighth + 1) * EIGHTH)
        else:
            cols = pl.ds(pl.multiple_of(eighth * EIGHTH, 128), EIGHTH)
        out[:, cols] = term.astype(BF)

    if halves:
        for weight, side in zip(weights, (idx[1], 1 - idx[1])):
            for e in range(4):
                w = weight[:, e * HD : (e + 1) * HD, :].reshape(NZ * HD, EIGHTH)
                put(w, 4 * side + e)
    else:
        for s in range(NX * NC):
            put(weights[0][s].reshape(NZ * HD, EIGHTH), s)


def project(layer, idx, o, weights):
    out = pl.pallas_call(
        functools.partial(project_kernel, len(weights) == 2),
        out_shape=jax.ShapeDtypeStruct((NY * ROWS, D), BF),
        in_specs=[SM] + [VM] * (1 + len(weights)),
        out_specs=VM,
        compiler_params=params(),
        cost_estimate=pl.CostEstimate(flops=420_000_000, bytes_accessed=4_000_000, transcendentals=0),
        name="project_%d" % layer,
    )(idx, o, *weights)
    return out.reshape(NY, ROWS, D)


def residual_kernel(layer, terms, mods, x, out):
    attn = sum(terms[j].astype(F32) for j in range(NY))
    gate = mods[3 * layer + 2 : 3 * layer + 3, :]
    out[...] = (x[...].astype(F32) + gate * attn).astype(BF)


def residual(layer, terms, mods, x):
    return pl.pallas_call(
        functools.partial(residual_kernel, layer),
        out_shape=jax.ShapeDtypeStruct((ROWS, D), BF),
        in_specs=[VM] * 3,
        out_specs=VM,
        compiler_params=params(),
        cost_estimate=pl.CostEstimate(flops=600_000, bytes_accessed=1_400_000, transcendentals=0),
        name="residual_%d" % layer,
    )(terms, mods, x)


def from_ahead(block, axis, size, distance):
    return lax.ppermute(block, axis, [(i, (i - distance) % size) for i in range(size)])


def swap(block):
    return lax.ppermute(block, "core", [(0, 1), (1, 0)])


def shifted(block, axis, distance):
    devices = range(lax.axis_size(axis))
    route = [(i - distance, i) for i in devices if i - distance in devices]
    return lax.ppermute(block, axis, route)


SEQ = NZ * NY


def per_device(
    latent, noise_frame, frame_pos, t_index, pos_table, mod_table, w_qkv, qk_gain, w_out
):
    x_pos, core = lax.axis_index("x"), lax.axis_index("core")
    z, y = lax.axis_index("z"), lax.axis_index("y")
    slot = x_pos * NC + core
    idx = jnp.stack([x_pos, core, z, y]).astype(jnp.int32)

    frame_id = jnp.where(z >= NZ // 2, frame_pos[0, 1], frame_pos[0, 0])
    pos_row = lax.dynamic_slice_in_dim(pos_table, frame_id, 1, 0)
    x0 = (latent[0].astype(F32) + pos_row.astype(F32)).astype(BF)
    mods = lax.dynamic_slice_in_dim(mod_table, t_index[0], 1, 0)[0].astype(F32).reshape(6, D)
    gains = qk_gain[:, 0].astype(F32)
    w_t = jnp.transpose(w_qkv[:, :, 0, :], (0, 2, 1))

    half = lax.dynamic_slice_in_dim(w_t[0], core * (D // 2), D // 2, 1)
    mine = [from_ahead(half, "y", NY, j) for j in range(1, NY)]
    other = [swap(m) for m in mine]

    def split(w, parts):
        return jnp.transpose(w.reshape(-1, parts, EIGHTH), (1, 0, 2)).reshape(-1, EIGHTH)

    def eighth(w):
        return lax.dynamic_slice_in_dim(w, slot * EIGHTH, EIGHTH, 1)

    wo_half = lax.dynamic_slice_in_dim(w_out[0], core * (D // 2), D // 2, 1)
    pack = jnp.concatenate([split(x0, 8), eighth(w_t[1]), split(wo_half, 4), eighth(w_out[1])], axis=0)
    later = lax.all_gather(pack, "z", axis=0, tiled=False)

    def attend(own, layer):
        lower = shifted(own, ("x", "core"), 1)
        upper = shifted(own, ("x", "core"), -1)
        return attention(idx, own, lower, upper, gains[layer : layer + 1])

    heads, wq1, wo0, wo1 = qkv_first(idx, later, mods, w_t, mine, other)
    wq1 = lax.all_gather(wq1, ("x", "core"), axis=0, tiled=False)
    own = lax.all_to_all(heads, "y", 0, 0, tiled=True)
    own, wo0, wo1 = lax.optimization_barrier((own, wo0, wo1))
    wo1 = lax.all_gather(wo1, ("x", "core"), axis=0, tiled=False)
    done = lax.all_to_all(attend(own, 0), "z", 0, 0, tiled=True)
    terms = lax.all_to_all(project(0, idx, done, [wo0, swap(wo0)]), "y", 0, 0, tiled=True)
    x1 = residual(0, terms, mods, x0)

    shards = [x1] + [from_ahead(x1, "y", NY, j) for j in range(1, NY)]
    heads = qkv_second(idx, shards, mods, wq1)
    own = lax.all_to_all(heads, "z", 0, 0, tiled=True)
    done = lax.all_to_all(attend(own, 1), "z", 0, 0, tiled=True)
    terms = lax.all_to_all(project(1, idx, done, [wo1]), "y", 0, 0, tiled=True)
    stream = residual(1, terms, mods, x1)

    moved = shifted(stream, ("x", "core", "z", "y"), -(SEQ // 2))
    start_row = jnp.maximum(z * NY + y - SEQ // 2, 0) * ROWS
    fresh = lax.dynamic_slice_in_dim(noise_frame, start_row, ROWS, 0)
    tail = jnp.logical_and(slot == NX * NC - 1, z >= NZ // 2)
    queue = jnp.where(tail, fresh, moved)
    return (stream[None], queue[None])


def solution(mesh):
    grid = Mesh(mesh.devices.reshape(NX, NC, NZ, NY), ("x", "core", "z", "y"))
    slot, seq = ("x", "core"), ("z", "y")
    placed = (
        P(slot, seq, None),
        P(),
        P(slot, None),
        P(slot),
        P(),
        P(),
        P(None, None, seq, None),
        P(None, seq, None),
        P(None, seq, None),
    )
    return jax.shard_map(
        per_device,
        mesh=grid,
        in_specs=placed,
        out_specs=(P(slot, seq, None), P(slot, seq, None)),
        check_vma=False,
    )
```

```python
import functools

import jax
import jax.numpy as jnp
from jax import lax
from jax.experimental import pallas as pl
from jax.experimental.pallas import tpu as pltpu
from jax.sharding import Mesh, PartitionSpec as P

BF = jnp.bfloat16
F32 = jnp.float32
EPS = 1e-6
NX, NC, NZ, NY = 4, 2, 8, 4
D = 3072
HD = 64
ROWS = 32
QUARTER = D // NY
EIGHTH = QUARTER // 2
PACK = (8 * ROWS, 3 * HD, HD)
VMEM_LIMIT = 48 * 1024 * 1024

VM = pl.BlockSpec(memory_space=pltpu.VMEM)
SM = pl.BlockSpec(memory_space=pltpu.SMEM)


def params():
    return pltpu.CompilerParams(vmem_limit_bytes=VMEM_LIMIT)


def normalized(blocks):
    mean = sum(jnp.sum(b, axis=-1, keepdims=True) for b in blocks) / D
    centers = [b - mean for b in blocks]
    spread = sum(jnp.sum(c * c, axis=-1, keepdims=True) for c in centers) / D
    inv = lax.rsqrt(spread + EPS)
    return [c * inv for c in centers]


def head_rows(value):
    center = value - jnp.mean(value, axis=0, keepdims=True)
    spread = jnp.mean(center * center, axis=0, keepdims=True)
    return center * lax.rsqrt(spread + EPS)


def store_head(out, result):
    out[0:HD, :] = head_rows(result[0:HD]).astype(BF)
    out[HD : 2 * HD, :] = head_rows(result[HD : 2 * HD]).astype(BF)
    out[2 * HD :, :] = result[2 * HD :].astype(BF)


def times(weight, h):
    return lax.dot_general(weight, h, (((1,), (1,)), ((), ())), preferred_element_type=F32)


def qkv_first_kernel(idx, later, mods, w_t, *refs):
    mine, other = refs[0:3], refs[3:6]
    out, wq, wo1, h, x, own, sems = refs[6:]
    core, y = idx[1], idx[3]
    copies = []
    row = 0
    for n, (rows, target) in enumerate(zip(PACK, (x, wq, wo1))):
        copies.append(pltpu.make_async_copy(later.at[:, row : row + rows, :], target, sems.at[n]))
        row += rows
    copies.insert(1, pltpu.make_async_copy(w_t.at[0], own, sems.at[3]))
    for copy in copies:
        copy.start()
    copies[0].wait()
    for z in range(NZ):
        blocks = [x[z, e * ROWS : (e + 1) * ROWS, :].astype(F32) for e in range(8)]
        for e, norm in enumerate(normalized(blocks)):
            cols = slice(e * EIGHTH, (e + 1) * EIGHTH)
            part = norm * (1.0 + mods[1:2, cols]) + mods[0:1, cols]
            h[e // 2, z, :, (e % 2) * EIGHTH : (e % 2 + 1) * EIGHTH] = part.astype(BF)

    def tokens(b):
        return h[b].reshape(NZ * ROWS, QUARTER)

    copies[1].wait()
    for j in range(NY):
        if j == 0:
            total = sum(times(own[:, b * QUARTER : (b + 1) * QUARTER], tokens(b)) for b in range(NY))
        else:
            total = None
            for weight, side in ((mine[j - 1], core), (other[j - 1], 1 - core)):
                for t in range(2):
                    term = times(weight[:, t * QUARTER : (t + 1) * QUARTER], tokens(2 * side + t))
                    total = term if total is None else total + term
        store_head(out.at[lax.rem(y + j, NY)], total)
    for copy in copies[2:]:
        copy.wait()


def qkv_first(idx, later, mods, w_t, mine, other):
    anywhere = pl.BlockSpec(memory_space=pl.ANY)
    return pl.pallas_call(
        qkv_first_kernel,
        out_shape=[jax.ShapeDtypeStruct((NY, 3 * HD, NZ * ROWS), BF)]
        + [jax.ShapeDtypeStruct((NZ, rows, EIGHTH), BF) for rows in PACK[1:]],
        in_specs=[SM, anywhere, VM, anywhere] + [VM] * 6,
        out_specs=[VM] * 3,
        scratch_shapes=[
            pltpu.VMEM((NY, NZ, ROWS, QUARTER), BF),
            pltpu.VMEM((NZ, PACK[0], EIGHTH), BF),
            pltpu.VMEM((3 * HD, D), BF),
            pltpu.SemaphoreType.DMA((4,)),
        ],
        compiler_params=params(),
        cost_estimate=pl.CostEstimate(flops=1_200_000_000, bytes_accessed=14_000_000, transcendentals=0),
        name="qkv_first",
    )(idx, later, mods, w_t, *mine, *other)


def qkv_second_kernel(idx, x0, x1, x2, x3, mods, *refs):
    weights, (out, h) = refs[:10], refs[10:]
    x_pos, core, y = idx[0], idx[1], idx[3]
    step = pl.program_id(0)

    @pl.when(step == 0)
    def _():
        for j, x in enumerate((x0, x1, x2, x3)):
            (norm,) = normalized([x[...].astype(F32)])
            at = lax.rem(y + j, NY)
            for e in range(8):
                cols = slice(e * EIGHTH, (e + 1) * EIGHTH)
                part = norm[:, cols] * (1.0 + mods[4:5, cols]) + mods[3:4, cols]
                h[e, at] = part.astype(BF)

    total = None
    for n in range(2):
        side = core if n == 0 else 1 - core
        group = [w[0] for w in weights[5 * n : 5 * n + 5]]
        group[3:] = [jnp.where(step < NZ // 2, group[3], group[4])]
        for k, weight in zip((0, 1, 3, 2), group):
            tokens = h[lax.rem(x_pos + k, NX) * NC + side].reshape(NY * ROWS, EIGHTH)
            term = times(weight, tokens)
            total = term if total is None else total + term
    store_head(out.at[0], total)


def qkv_second(idx, shards, mods, weights):
    half = NZ // 2
    shard = pl.BlockSpec((ROWS, D), lambda i: (0, 0))
    head = lambda at: pl.BlockSpec((1, 3 * HD, EIGHTH), lambda i: (at(i), 0, 0))
    heads = [head(lambda i: i)] * 3 + [head(lambda i: jnp.minimum(i, half - 1)), head(lambda i: jnp.maximum(i - half, 0))]
    return pl.pallas_call(
        qkv_second_kernel,
        grid=(NZ,),
        out_shape=jax.ShapeDtypeStruct((NZ, 3 * HD, NY * ROWS), BF),
        in_specs=[SM] + [shard] * 4 + [pl.BlockSpec((6, D), lambda i: (0, 0))] + heads * 2,
        out_specs=pl.BlockSpec((1, 3 * HD, NY * ROWS), lambda i: (i, 0, 0)),
        scratch_shapes=[pltpu.VMEM((8, NY, ROWS, EIGHTH), BF)],
        compiler_params=params(),
        cost_estimate=pl.CostEstimate(flops=1_200_000_000, bytes_accessed=10_500_000, transcendentals=0),
        name="qkv_second",
    )(idx, *shards, mods, *weights)


def attention_kernel(groups, idx, own, lower, upper, gain, out, acc, den, queries):
    length = 1024 // groups
    per = 256 // length
    slot = idx[0] * NC + idx[1]
    column = jnp.transpose(jnp.broadcast_to(gain[...], (8, 2 * HD)))[:, 0:1]
    g = column[0:HD] * column[HD:] * 0.125

    def wide(ref, n, lo, hi):
        if per == 1:
            return ref[n, lo:hi, :]
        return jnp.concatenate([ref[n * per + i, lo:hi, :] for i in range(per)], axis=1)

    for n in range(4):
        queries[n] = (wide(own, n, 0, HD).astype(F32) * g).astype(BF)
    acc[...] = jnp.zeros_like(acc)
    den[...] = jnp.zeros_like(den)

    def source(ref):
        def body(m, carry):
            q = queries[m]
            total = acc[m]
            norm = den[m]
            for n in range(4):
                keys = wide(ref, n, HD, 2 * HD)
                values = wide(ref, n, 2 * HD, 3 * HD)
                score = lax.dot_general(keys, q, (((0,), (0,)), ((), ())), preferred_element_type=F32)
                e = jnp.exp(score)
                norm = norm + jnp.sum(e, axis=0, keepdims=True)
                total = total + jnp.dot(values, e.astype(BF), preferred_element_type=F32)
            acc[m] = total
            den[m] = norm
            return carry

        lax.fori_loop(0, 4, body, 0)

    source(own)

    @pl.when(slot > 0)
    def _():
        source(lower)

    @pl.when(slot < NX * NC - 1)
    def _():
        source(upper)

    if per == 1:
        done = [acc[n] / den[n] for n in range(4)]
        for z in range(NZ):
            cols = slice(z * ROWS, (z + 1) * ROWS)
            out[z] = jnp.concatenate([d[:, cols] for d in done], axis=1).astype(BF)
    else:
        for n in range(4):
            done = (acc[n] / den[n]).astype(BF)
            for i in range(per):
                out[n * per + i] = done[:, i * length : (i + 1) * length]


def attention(idx, own, lower, upper, gain):
    groups = own.shape[0]
    return pl.pallas_call(
        functools.partial(attention_kernel, groups),
        out_shape=jax.ShapeDtypeStruct((NZ, HD, NY * ROWS), BF),
        in_specs=[SM] + [VM] * 4,
        out_specs=VM,
        scratch_shapes=[
            pltpu.VMEM((4, HD, 256), F32),
            pltpu.VMEM((4, 1, 256), F32),
            pltpu.VMEM((4, HD, 256), BF),
        ],
        compiler_params=params(),
        cost_estimate=pl.CostEstimate(flops=0, bytes_accessed=1_200_000, transcendentals=0),
        name="attention_%d" % groups,
    )(idx, own, lower, upper, gain)


def project_kernel(halves, idx, o, *refs):
    weights, out = refs[:-1], refs[-1]
    rows = o[...].reshape(NZ * HD, NY * ROWS)

    def put(w, eighth):
        term = lax.dot_general(rows, w, (((0,), (0,)), ((), ())), preferred_element_type=F32)
        if isinstance(eighth, int):
            cols = slice(eighth * EIGHTH, (eighth + 1) * EIGHTH)
        else:
            cols = pl.ds(pl.multiple_of(eighth * EIGHTH, 128), EIGHTH)
        out[:, cols] = term.astype(BF)

    if halves:
        for weight, side in zip(weights, (idx[1], 1 - idx[1])):
            for e in range(4):
                w = weight[:, :, e * EIGHTH : (e + 1) * EIGHTH].reshape(NZ * HD, EIGHTH)
                put(w, 4 * side + e)
    else:
        for s in range(NX * NC):
            put(weights[0][s].reshape(NZ * HD, EIGHTH), s)


def project(layer, idx, o, weights):
    out = pl.pallas_call(
        functools.partial(project_kernel, len(weights) == 2),
        out_shape=jax.ShapeDtypeStruct((NY * ROWS, D), BF),
        in_specs=[SM] + [VM] * (1 + len(weights)),
        out_specs=VM,
        compiler_params=params(),
        cost_estimate=pl.CostEstimate(flops=420_000_000, bytes_accessed=4_000_000, transcendentals=0),
        name="project_%d" % layer,
    )(idx, o, *weights)
    return out.reshape(NY, ROWS, D)


def residual_kernel(layer, terms, mods, x, out):
    attn = sum(terms[j].astype(F32) for j in range(NY))
    gate = mods[3 * layer + 2 : 3 * layer + 3, :]
    out[...] = (x[...].astype(F32) + gate * attn).astype(BF)


def residual(layer, terms, mods, x):
    return pl.pallas_call(
        functools.partial(residual_kernel, layer),
        out_shape=jax.ShapeDtypeStruct((ROWS, D), BF),
        in_specs=[VM] * 3,
        out_specs=VM,
        compiler_params=params(),
        cost_estimate=pl.CostEstimate(flops=600_000, bytes_accessed=1_400_000, transcendentals=0),
        name="residual_%d" % layer,
    )(terms, mods, x)


def from_ahead(block, axis, size, distance):
    return lax.ppermute(block, axis, [(i, (i - distance) % size) for i in range(size)])


def swap(block):
    return lax.ppermute(block, "core", [(0, 1), (1, 0)])


def shifted(block, axis, distance):
    devices = range(lax.axis_size(axis))
    route = [(i - distance, i) for i in devices if i - distance in devices]
    return lax.ppermute(block, axis, route)


SEQ = NZ * NY


def per_device(
    latent, noise_frame, frame_pos, t_index, pos_table, mod_table, w_qkv, qk_gain, w_out
):
    x_pos, core = lax.axis_index("x"), lax.axis_index("core")
    z, y = lax.axis_index("z"), lax.axis_index("y")
    slot = x_pos * NC + core
    idx = jnp.stack([x_pos, core, z, y]).astype(jnp.int32)

    frame_id = jnp.where(z >= NZ // 2, frame_pos[0, 1], frame_pos[0, 0])
    pos_row = lax.dynamic_slice_in_dim(pos_table, frame_id, 1, 0)
    x0 = (latent[0].astype(F32) + pos_row.astype(F32)).astype(BF)
    mods = lax.dynamic_slice_in_dim(mod_table, t_index[0], 1, 0)[0].astype(F32).reshape(6, D)
    gains = qk_gain[:, 0].astype(F32)
    w_t = jnp.transpose(w_qkv[:, :, 0, :], (0, 2, 1))

    half = lax.dynamic_slice_in_dim(w_t[0], core * (D // 2), D // 2, 1)
    mine = [from_ahead(half, "y", NY, j) for j in range(1, NY)]
    other = [swap(m) for m in mine]

    def eighth(w):
        return lax.dynamic_slice_in_dim(w, slot * EIGHTH, EIGHTH, 1)

    tokens = jnp.transpose(x0.reshape(ROWS, 8, EIGHTH), (1, 0, 2)).reshape(8 * ROWS, EIGHTH)
    pack = jnp.concatenate([tokens, eighth(w_t[1]), eighth(w_out[1])], axis=0)
    later = lax.all_gather(pack, "z", axis=0, tiled=False)
    wo_half = lax.dynamic_slice_in_dim(w_out[0], core * (D // 2), D // 2, 1)
    wo0 = lax.all_gather(wo_half, "z", axis=0, tiled=False)

    def attend(own, layer):
        lower = shifted(own, ("x", "core"), 1)
        upper = shifted(own, ("x", "core"), -1)
        return attention(idx, own, lower, upper, gains[layer : layer + 1])

    heads, wq1, wo1 = qkv_first(idx, later, mods, w_t, mine, other)
    ahead, behind = from_ahead(wq1, "x", NX, 1), from_ahead(wq1, "x", NX, 3)
    own = lax.all_to_all(heads, "y", 0, 0, tiled=True)
    own, wo1 = lax.optimization_barrier((own, wo1))
    wo1 = lax.all_gather(wo1, ("x", "core"), axis=0, tiled=False)
    done, wo0, ahead, behind = lax.optimization_barrier((attend(own, 0), wo0, ahead, behind))
    far = [from_ahead(ahead[: NZ // 2], "x", NX, 1), from_ahead(behind[NZ // 2 :], "x", NX, 3)]
    done = lax.all_to_all(done, "z", 0, 0, tiled=True)
    done, *wq1 = lax.optimization_barrier((done, wq1, ahead, behind, *far))
    wq1 = wq1 + [swap(w) for w in wq1]
    terms = lax.all_to_all(project(0, idx, done, [wo0, swap(wo0)]), "y", 0, 0, tiled=True)
    x1 = residual(0, terms, mods, x0)

    shards = [x1] + [from_ahead(x1, "y", NY, j) for j in range(1, NY)]
    heads = qkv_second(idx, shards, mods, wq1)
    own = lax.all_to_all(heads, "z", 0, 0, tiled=True)
    done = lax.all_to_all(attend(own, 1), "z", 0, 0, tiled=True)
    terms = lax.all_to_all(project(1, idx, done, [wo1]), "y", 0, 0, tiled=True)
    stream = residual(1, terms, mods, x1)

    moved = shifted(stream, ("x", "core", "z", "y"), -(SEQ // 2))
    start_row = jnp.maximum(z * NY + y - SEQ // 2, 0) * ROWS
    fresh = lax.dynamic_slice_in_dim(noise_frame, start_row, ROWS, 0)
    tail = jnp.logical_and(slot == NX * NC - 1, z >= NZ // 2)
    queue = jnp.where(tail, fresh, moved)
    return (stream[None], queue[None])


def solution(mesh):
    grid = Mesh(mesh.devices.reshape(NX, NC, NZ, NY), ("x", "core", "z", "y"))
    slot, seq = ("x", "core"), ("z", "y")
    placed = (
        P(slot, seq, None),
        P(),
        P(slot, None),
        P(slot),
        P(),
        P(),
        P(None, None, seq, None),
        P(None, seq, None),
        P(None, seq, None),
    )
    return jax.shard_map(
        per_device,
        mesh=grid,
        in_specs=placed,
        out_specs=(P(slot, seq, None), P(slot, seq, None)),
        check_vma=False,
    )
```

```python
import functools

import jax
import jax.numpy as jnp
from jax import lax
from jax.experimental import pallas as pl
from jax.experimental.pallas import tpu as pltpu
from jax.sharding import Mesh, PartitionSpec as P

BF = jnp.bfloat16
F32 = jnp.float32
EPS = 1e-6
NX, NC, NZ, NY = 4, 2, 8, 4
D = 3072
NF = 16
HD = 64
ROWS = 32
SEQ = NZ * NY
QUARTER = D // NY
EIGHTH = QUARTER // 2
PACK = (8 * ROWS, 3 * HD)

VM = pl.BlockSpec(memory_space=pltpu.VMEM)
SM = pl.BlockSpec(memory_space=pltpu.SMEM)
HB = pl.BlockSpec(memory_space=pltpu.HBM)
ANY = pl.BlockSpec(memory_space=pl.ANY)


def params(mebibytes):
    return pltpu.CompilerParams(vmem_limit_bytes=mebibytes * 1024 * 1024)


def position():
    return [lax.axis_index(name) for name in ("x", "core", "z", "y")]


def in_hbm(array):
    return pltpu.with_memory_space_constraint(array, pltpu.HBM)


def normalized(blocks):
    mean = sum(jnp.sum(b, axis=-1, keepdims=True) for b in blocks) / D
    centers = [b - mean for b in blocks]
    spread = sum(jnp.sum(c * c, axis=-1, keepdims=True) for c in centers) / D
    inv = lax.rsqrt(spread + EPS)
    return [c * inv for c in centers]


def head_rows(value):
    center = value - jnp.mean(value, axis=0, keepdims=True)
    spread = jnp.mean(center * center, axis=0, keepdims=True)
    return center * lax.rsqrt(spread + EPS)


def store_head(out, result):
    out[0:HD, :] = head_rows(result[0:HD]).astype(BF)
    out[HD : 2 * HD, :] = head_rows(result[HD : 2 * HD]).astype(BF)
    out[2 * HD :, :] = result[2 * HD :].astype(BF)


def times(weight, h):
    return lax.dot_general(weight, h, (((1,), (1,)), ((), ())), preferred_element_type=F32)


def prepare_kernel(frame_pos, latent, pos, w_t, w_out, x0, pack, half, wo, x, table, sems):
    x_pos, core, z, _ = position()

    def columns(start, width):
        return pl.ds(pl.multiple_of(start, 128), width)

    eighth = columns((x_pos * NC + core) * EIGHTH, EIGHTH)
    copies = [
        (latent.at[0], x),
        (pos, table),
        (w_t.at[1, :, eighth], pack.at[PACK[0] :, :]),
        (w_t.at[0, :, columns(core * (D // 2), D // 2)], half),
    ]
    for e in range(4):
        part = columns((4 * core + e) * EIGHTH, EIGHTH)
        copies.append((w_out.at[0, :, part], wo.at[e * HD : (e + 1) * HD, :]))
    copies.append((w_out.at[1, :, eighth], wo.at[4 * HD :, :]))
    copies = [pltpu.make_async_copy(*pair, sems.at[n]) for n, pair in enumerate(copies)]
    for copy in copies:
        copy.start()
    frame = jnp.where(z >= NZ // 2, frame_pos[0, 1], frame_pos[0, 0])
    for copy in copies[:2]:
        copy.wait()
    chosen = lax.broadcasted_iota(jnp.int32, table.shape, 0) == frame
    row = jnp.sum(jnp.where(chosen, table[...].astype(F32), 0.0), axis=0, keepdims=True)
    value = (x[...].astype(F32) + row).astype(BF)
    x0[...] = value
    for e in range(8):
        pack[e * ROWS : (e + 1) * ROWS, :] = value[:, e * EIGHTH : (e + 1) * EIGHTH]
    for copy in copies[2:]:
        copy.wait()


def prepare(frame_pos, latent, pos, w_t, w_out):
    shapes = ((ROWS, D), (sum(PACK), EIGHTH), (3 * HD, D // 2), (5 * HD, EIGHTH))
    return pl.pallas_call(
        prepare_kernel,
        out_shape=[jax.ShapeDtypeStruct(shape, BF) for shape in shapes],
        in_specs=[SM] + [HB] * 4,
        out_specs=[VM] * 4,
        scratch_shapes=[
            pltpu.VMEM((ROWS, D), BF),
            pltpu.VMEM((NF, D), BF),
            pltpu.SemaphoreType.DMA((9,)),
        ],
        compiler_params=params(8),
        cost_estimate=pl.CostEstimate(flops=300_000, bytes_accessed=2_500_000, transcendentals=0),
        name="prepare",
    )(frame_pos, *map(in_hbm, (latent, pos, w_t, w_out)))


def qkv_first_kernel(later, mods, w_t, *refs):
    mine, other = refs[0:3], refs[3:6]
    out, wq_low, wq_high, h, x, own, held, sems = refs[6:]
    _, core, _, y = position()
    first = pl.ds(PACK[0], PACK[1])
    copies = [
        pltpu.make_async_copy(later.at[:, : PACK[0], :], x, sems.at[0]),
        pltpu.make_async_copy(w_t.at[0], own, sems.at[1]),
        pltpu.make_async_copy(later.at[:, first, :], held, sems.at[2]),
        pltpu.make_async_copy(held.at[: NZ // 2], wq_low, sems.at[3]),
        pltpu.make_async_copy(held.at[NZ // 2 :], wq_high, sems.at[4]),
    ]
    for copy in copies[:3]:
        copy.start()
    copies[0].wait()
    for z in range(NZ):
        blocks = [x[z, e * ROWS : (e + 1) * ROWS, :].astype(F32) for e in range(8)]
        for e, norm in enumerate(normalized(blocks)):
            cols = slice(e * EIGHTH, (e + 1) * EIGHTH)
            part = norm * (1.0 + mods[1:2, cols]) + mods[0:1, cols]
            h[e // 2, z, :, (e % 2) * EIGHTH : (e % 2 + 1) * EIGHTH] = part.astype(BF)

    def tokens(b):
        return h[b].reshape(NZ * ROWS, QUARTER)

    copies[2].wait()
    for copy in copies[3:]:
        copy.start()
    copies[1].wait()
    for j in range(NY):
        if j == 0:
            total = sum(times(own[:, b * QUARTER : (b + 1) * QUARTER], tokens(b)) for b in range(NY))
        else:
            total = None
            for weight, side in ((mine[j - 1], core), (other[j - 1], 1 - core)):
                for t in range(2):
                    term = times(weight[:, t * QUARTER : (t + 1) * QUARTER], tokens(2 * side + t))
                    total = term if total is None else total + term
        store_head(out.at[lax.rem(y + j, NY)], total)
    for copy in copies[3:]:
        copy.wait()


def qkv_first(later, mods, w_t, mine, other):
    return pl.pallas_call(
        qkv_first_kernel,
        out_shape=[jax.ShapeDtypeStruct((NY, 3 * HD, NZ * ROWS), BF)]
        + [jax.ShapeDtypeStruct((NZ // 2, 3 * HD, EIGHTH), BF)] * 2,
        in_specs=[HB, VM, HB] + [VM] * 6,
        out_specs=[VM, HB, HB],
        scratch_shapes=[
            pltpu.VMEM((NY, NZ, ROWS, QUARTER), BF),
            pltpu.VMEM((NZ, PACK[0], EIGHTH), BF),
            pltpu.VMEM((3 * HD, D), BF),
            pltpu.VMEM((NZ, PACK[1], EIGHTH), BF),
            pltpu.SemaphoreType.DMA((5,)),
        ],
        compiler_params=params(24),
        cost_estimate=pl.CostEstimate(flops=1_200_000_000, bytes_accessed=14_000_000, transcendentals=0),
        name="qkv_first",
    )(in_hbm(later), mods, in_hbm(w_t), *mine, *other)


def qkv_second_kernel(x0, x1, x2, x3, mods, gathered, *refs):
    weights, (out, h) = refs[:8], refs[8:]
    x_pos, core, _, y = position()

    @pl.when(pl.program_id(0) == 0)
    def _():
        for j, x in enumerate((x0, x1, x2, x3)):
            (norm,) = normalized([x[...].astype(F32)])
            at = lax.rem(y + j, NY)
            for e in range(8):
                cols = slice(e * EIGHTH, (e + 1) * EIGHTH)
                part = norm[:, cols] * (1.0 + mods[4:5, cols]) + mods[3:4, cols]
                h[e, at] = part.astype(BF)

    def tokens(e):
        return h[e].reshape(NY * ROWS, EIGHTH)

    @pl.when(pl.program_id(0) < NZ // 2)
    def _():
        store_head(out.at[0], sum(times(gathered[e, 0], tokens(e)) for e in range(8)))

    @pl.when(pl.program_id(0) >= NZ // 2)
    def _():
        total = None
        for n, weight in enumerate(weights):
            side = core if n < NX else 1 - core
            term = times(weight[0], tokens(lax.rem(x_pos + n % NX, NX) * NC + side))
            total = term if total is None else total + term
        store_head(out.at[0], total)


def qkv_second(shards, mods, gathered, weights):
    half = NZ // 2
    shard = pl.BlockSpec((ROWS, D), lambda i: (0, 0))
    low = pl.BlockSpec((8, 1, 3 * HD, EIGHTH), lambda i: (0, jnp.minimum(i, half - 1), 0, 0))
    high = pl.BlockSpec((1, 3 * HD, EIGHTH), lambda i: (jnp.maximum(i - half, 0), 0, 0))
    return pl.pallas_call(
        qkv_second_kernel,
        grid=(NZ,),
        out_shape=jax.ShapeDtypeStruct((NZ, 3 * HD, NY * ROWS), BF),
        in_specs=[shard] * 4 + [pl.BlockSpec((6, D), lambda i: (0, 0)), low] + [high] * 8,
        out_specs=pl.BlockSpec((1, 3 * HD, NY * ROWS), lambda i: (i, 0, 0)),
        scratch_shapes=[pltpu.VMEM((8, NY, ROWS, EIGHTH), BF)],
        compiler_params=params(24),
        cost_estimate=pl.CostEstimate(flops=1_200_000_000, bytes_accessed=10_500_000, transcendentals=0),
        name="qkv_second",
    )(*shards, mods, in_hbm(gathered), *weights)


def over_keys(per, ref, queries, acc, den, begin):
    def wide(n, lo, hi):
        if per == 1:
            return ref[n, lo:hi, :]
        return jnp.concatenate([ref[n * per + i, lo:hi, :] for i in range(per)], axis=1)

    def body(m, carry):
        q = queries[m]
        total, norm = (None, None) if begin else (acc[m], den[m])
        for n in range(4):
            keys, values = wide(n, HD, 2 * HD), wide(n, 2 * HD, 3 * HD)
            score = lax.dot_general(keys, q, (((0,), (0,)), ((), ())), preferred_element_type=F32)
            e = jnp.exp(score)
            sums = jnp.sum(e, axis=0, keepdims=True)
            term = jnp.dot(values, e.astype(BF), preferred_element_type=F32)
            total = term if total is None else total + term
            norm = sums if norm is None else norm + sums
        acc[m] = total
        den[m] = norm
        return carry

    lax.fori_loop(0, 4, body, 0)


def own_kernel(per, own, gain, queries, acc, den):
    column = jnp.transpose(jnp.broadcast_to(gain[...], (8, 2 * HD)))[:, 0:1]
    g = column[0:HD] * column[HD:] * 0.125
    for n in range(4):
        parts = [own[n * per + i, 0:HD, :] for i in range(per)]
        q = parts[0] if per == 1 else jnp.concatenate(parts, axis=1)
        queries[n] = (q.astype(F32) * g).astype(BF)
    over_keys(per, own, queries, acc, den, True)


def neighbours_kernel(per, lower, upper, queries, acc_in, den_in, out, acc, den):
    x_pos, core, _, _ = position()
    slot = x_pos * NC + core
    acc[...] = acc_in[...]
    den[...] = den_in[...]

    @pl.when(slot > 0)
    def _():
        over_keys(per, lower, queries, acc, den, False)

    @pl.when(slot < NX * NC - 1)
    def _():
        over_keys(per, upper, queries, acc, den, False)

    if per == 1:
        done = [acc[n] / den[n] for n in range(4)]
        for z in range(NZ):
            cols = slice(z * ROWS, (z + 1) * ROWS)
            out[z] = jnp.concatenate([d[:, cols] for d in done], axis=1).astype(BF)
    else:
        for n in range(4):
            done = (acc[n] / den[n]).astype(BF)
            for i in range(per):
                out[n * per + i] = done[:, i * 256 // per : (i + 1) * 256 // per]


def attention(own, lower, upper, gain):
    per = own.shape[0] // 4
    sums = [jax.ShapeDtypeStruct((4, HD, 256), F32), jax.ShapeDtypeStruct((4, 1, 256), F32)]
    queries, acc, den = pl.pallas_call(
        functools.partial(own_kernel, per),
        out_shape=[jax.ShapeDtypeStruct((4, HD, 256), BF)] + sums,
        in_specs=[VM] * 2,
        out_specs=[VM] * 3,
        compiler_params=params(8),
        cost_estimate=pl.CostEstimate(flops=3_000_000_000, bytes_accessed=800_000, transcendentals=0),
        name="own_%d" % per,
    )(own, gain)
    return pl.pallas_call(
        functools.partial(neighbours_kernel, per),
        out_shape=jax.ShapeDtypeStruct((NZ, HD, NY * ROWS), BF),
        in_specs=[VM] * 5,
        out_specs=VM,
        scratch_shapes=[pltpu.VMEM(s.shape, F32) for s in sums],
        compiler_params=params(8),
        cost_estimate=pl.CostEstimate(flops=6_000_000_000, bytes_accessed=1_200_000, transcendentals=0),
        name="neighbours_%d" % per,
    )(lower, upper, queries, acc, den)


def project_kernel(halves, o, *refs):
    (*sources, out, weights, sems) = refs
    _, core, _, _ = position()
    if halves:
        eighths = [(w.at[:, e * HD : (e + 1) * HD, :], 4 * side + e) for w, side in zip(sources, (core, 1 - core)) for e in range(4)]
    else:
        eighths = [(sources[0].at[s], s) for s in range(NX * NC)]
    copies = [pltpu.make_async_copy(w, weights.at[n], sems.at[n]) for n, (w, _) in enumerate(eighths)]
    for copy in copies:
        copy.start()
    rows = o[...].reshape(NZ * HD, NY * ROWS)
    for n in range(0, 8, 2):
        copies[n].wait()
        copies[n + 1].wait()
        w = jnp.concatenate([weights[n + t].reshape(NZ * HD, EIGHTH) for t in range(2)], axis=1)
        term = lax.dot_general(rows, w, (((0,), (0,)), ((), ())), preferred_element_type=F32)
        start = eighths[n][1] * EIGHTH
        out[:, pl.ds(pl.multiple_of(start, 128), QUARTER)] = term.astype(BF)


def project(o, weights):
    halves = len(weights) == 2
    out = pl.pallas_call(
        functools.partial(project_kernel, halves),
        out_shape=jax.ShapeDtypeStruct((NY * ROWS, D), BF),
        in_specs=[VM, HB, ANY][: 1 + len(weights)],
        out_specs=VM,
        scratch_shapes=[pltpu.VMEM((8, NZ, HD, EIGHTH), BF), pltpu.SemaphoreType.DMA((8,))],
        compiler_params=params(12),
        cost_estimate=pl.CostEstimate(flops=420_000_000, bytes_accessed=4_000_000, transcendentals=0),
        name="project_%d" % len(weights),
    )(o, in_hbm(weights[0]), *weights[1:])
    return out.reshape(NY, ROWS, D)


def added(layer, terms, mods, x):
    attn = sum(terms[j].astype(F32) for j in range(NY))
    gate = mods[3 * layer + 2 : 3 * layer + 3, :]
    return (x[...].astype(F32) + gate * attn).astype(BF)


def residual_kernel(terms, mods, x, out):
    out[...] = added(0, terms, mods, x)


def residual(terms, mods, x):
    return pl.pallas_call(
        residual_kernel,
        out_shape=jax.ShapeDtypeStruct((ROWS, D), BF),
        in_specs=[VM] * 3,
        out_specs=VM,
        compiler_params=params(8),
        cost_estimate=pl.CostEstimate(flops=600_000, bytes_accessed=1_400_000, transcendentals=0),
        name="residual",
    )(terms, mods, x)


def last_kernel(terms, mods, x, noise, out, leaving, sem):
    x_pos, core, z, y = position()
    value = added(1, terms, mods, x)
    out[...] = value
    head = jnp.logical_and(x_pos * NC + core == 0, z < NZ // 2)

    @pl.when(head)
    def _():
        at = pl.multiple_of(jnp.minimum(z * NY + y, SEQ // 2 - 1) * ROWS, ROWS)
        copy = pltpu.make_async_copy(noise.at[pl.ds(at, ROWS), :], leaving, sem)
        copy.start()
        copy.wait()

    @pl.when(jnp.logical_not(head))
    def _():
        leaving[...] = value


def last(terms, mods, x, noise):
    shape = jax.ShapeDtypeStruct((ROWS, D), BF)
    return pl.pallas_call(
        last_kernel,
        out_shape=[shape, shape],
        in_specs=[VM] * 3 + [HB],
        out_specs=[VM] * 2,
        scratch_shapes=[pltpu.SemaphoreType.DMA],
        compiler_params=params(8),
        cost_estimate=pl.CostEstimate(flops=600_000, bytes_accessed=1_600_000, transcendentals=0),
        name="last",
    )(terms, mods, x, in_hbm(noise))


def from_ahead(block, axis, size, distance):
    return lax.ppermute(block, axis, [(i, (i - distance) % size) for i in range(size)])


def swap(block):
    return lax.ppermute(block, "core", [(0, 1), (1, 0)])


def shifted(block, axis, distance):
    devices = range(lax.axis_size(axis))
    route = [(i - distance, i) for i in devices if i - distance in devices]
    return lax.ppermute(block, axis, route)


def per_device(
    latent, noise_frame, frame_pos, t_index, pos_table, mod_table, w_qkv, qk_gain, w_out
):
    mods = lax.dynamic_slice_in_dim(mod_table, t_index[0], 1, 0)[0].astype(F32).reshape(6, D)
    gains = qk_gain[:, 0].astype(F32)
    w_t = jnp.transpose(w_qkv[:, :, 0, :], (0, 2, 1))
    x0, pack, half, wo = prepare(frame_pos, latent, pos_table, w_t, w_out)

    later = lax.all_gather(pack, "z", axis=0, tiled=False)
    wo = lax.all_gather(wo, "z", axis=0, tiled=False)

    mine = [from_ahead(half, "y", NY, j) for j in range(1, NY)]
    other = [swap(m) for m in mine]

    def neighbours(own):
        return shifted(own, ("x", "core"), 1), shifted(own, ("x", "core"), -1)

    heads, low, high = qkv_first(later, mods, w_t, mine, other)
    low = lax.all_gather(low, ("x", "core"), axis=0, tiled=False)
    high_1, high_3 = from_ahead(high, "x", NX, 1), from_ahead(high, "x", NX, 3)
    own = lax.all_to_all(heads, "y", 0, 0, tiled=True)
    own, high_1, high_3 = lax.optimization_barrier((own, high_1, high_3))
    done = attention(own, *neighbours(own), gains[0:1])
    done, wo, high, high_1, high_3 = lax.optimization_barrier((done, wo, high, high_1, high_3))
    wo_s, high_2 = swap(wo), from_ahead(high_1, "x", NX, 1)
    wo1 = lax.all_gather(wo[:, 4 * HD :], ("x", "core"), axis=0, tiled=False)
    done = lax.all_to_all(done, "z", 0, 0, tiled=True)
    done, wo_s, high_2 = lax.optimization_barrier((done, wo_s, high_2))
    weights = [high, high_1, high_2, high_3]
    weights += [swap(w) for w in weights]
    terms = lax.all_to_all(project(done, [wo, wo_s]), "y", 0, 0, tiled=True)
    x1 = residual(terms, mods, x0)

    shards = [x1] + [from_ahead(x1, "y", NY, j) for j in range(1, NY)]
    heads = qkv_second(shards, mods, low, weights)
    own = lax.all_to_all(heads, "z", 0, 0, tiled=True)
    done = lax.all_to_all(attention(own, *neighbours(own), gains[1:2]), "z", 0, 0, tiled=True)
    terms = lax.all_to_all(project(done, [wo1]), "y", 0, 0, tiled=True)
    stream, leaving = last(terms, mods, x1, noise_frame)

    ranks = NX * NC * SEQ
    route = [(i, (i - SEQ // 2) % ranks) for i in range(ranks)]
    queue = lax.ppermute(leaving, ("x", "core", "z", "y"), route)
    return (stream[None], queue[None])


def solution(mesh):
    grid = Mesh(mesh.devices.reshape(NX, NC, NZ, NY), ("x", "core", "z", "y"))
    slot, seq = ("x", "core"), ("z", "y")
    placed = (
        P(slot, seq, None),
        P(),
        P(slot, None),
        P(slot),
        P(),
        P(),
        P(None, None, seq, None),
        P(None, seq, None),
        P(None, seq, None),
    )
    return jax.shard_map(
        per_device,
        mesh=grid,
        in_specs=placed,
        out_specs=(P(slot, seq, None), P(slot, seq, None)),
        check_vma=False,
    )
```

```python
import functools

import jax
import jax.numpy as jnp
from jax import lax
from jax.experimental import pallas as pl
from jax.experimental.pallas import tpu as pltpu
from jax.sharding import Mesh, PartitionSpec as P

BF = jnp.bfloat16
F32 = jnp.float32
EPS = 1e-6
NX, NC, NZ, NY = 4, 2, 8, 4
D = 3072
NF = 16
HD = 64
ROWS = 32
SEQ = NZ * NY
QUARTER = D // NY
EIGHTH = QUARTER // 2
PACK = (8 * ROWS, 3 * HD)
LOW = 5

VM = pl.BlockSpec(memory_space=pltpu.VMEM)
SM = pl.BlockSpec(memory_space=pltpu.SMEM)
HB = pl.BlockSpec(memory_space=pltpu.HBM)
ANY = pl.BlockSpec(memory_space=pl.ANY)


def params(mebibytes):
    return pltpu.CompilerParams(vmem_limit_bytes=mebibytes * 1024 * 1024)


def position():
    return [lax.axis_index(name) for name in ("x", "core", "z", "y")]


def in_hbm(array):
    return pltpu.with_memory_space_constraint(array, pltpu.HBM)


def normalized(blocks):
    mean = sum(jnp.sum(b, axis=-1, keepdims=True) for b in blocks) / D
    centers = [b - mean for b in blocks]
    spread = sum(jnp.sum(c * c, axis=-1, keepdims=True) for c in centers) / D
    inv = lax.rsqrt(spread + EPS)
    return [c * inv for c in centers]


def head_rows(value):
    center = value - jnp.mean(value, axis=0, keepdims=True)
    spread = jnp.mean(center * center, axis=0, keepdims=True)
    return center * lax.rsqrt(spread + EPS)


def store_head(out, result):
    out[0:HD, :] = head_rows(result[0:HD]).astype(BF)
    out[HD : 2 * HD, :] = head_rows(result[HD : 2 * HD]).astype(BF)
    out[2 * HD :, :] = result[2 * HD :].astype(BF)


def times(weight, h):
    return lax.dot_general(weight, h, (((1,), (1,)), ((), ())), preferred_element_type=F32)


def prepare_kernel(frame_pos, latent, pos, w_t, w_out, x0, pack, half, wo, x, table, sems):
    x_pos, core, z, _ = position()

    def columns(start, width):
        return pl.ds(pl.multiple_of(start, 128), width)

    eighth = columns((x_pos * NC + core) * EIGHTH, EIGHTH)
    copies = [
        (latent.at[0], x),
        (pos, table),
        (w_t.at[1, :, eighth], pack.at[PACK[0] :, :]),
        (w_t.at[0, :, columns(core * (D // 2), D // 2)], half),
    ]
    for e in range(4):
        part = columns((4 * core + e) * EIGHTH, EIGHTH)
        copies.append((w_out.at[0, :, part], wo.at[e * HD : (e + 1) * HD, :]))
    copies.append((w_out.at[1, :, eighth], wo.at[4 * HD :, :]))
    copies = [pltpu.make_async_copy(*pair, sems.at[n]) for n, pair in enumerate(copies)]
    for copy in copies:
        copy.start()
    frame = jnp.where(z >= NZ // 2, frame_pos[0, 1], frame_pos[0, 0])
    for copy in copies[:2]:
        copy.wait()
    chosen = lax.broadcasted_iota(jnp.int32, table.shape, 0) == frame
    row = jnp.sum(jnp.where(chosen, table[...].astype(F32), 0.0), axis=0, keepdims=True)
    value = (x[...].astype(F32) + row).astype(BF)
    x0[...] = value
    for e in range(8):
        pack[e * ROWS : (e + 1) * ROWS, :] = value[:, e * EIGHTH : (e + 1) * EIGHTH]
    for copy in copies[2:]:
        copy.wait()


def prepare(frame_pos, latent, pos, w_t, w_out):
    shapes = ((ROWS, D), (sum(PACK), EIGHTH), (3 * HD, D // 2), (5 * HD, EIGHTH))
    return pl.pallas_call(
        prepare_kernel,
        out_shape=[jax.ShapeDtypeStruct(shape, BF) for shape in shapes],
        in_specs=[SM] + [HB] * 4,
        out_specs=[VM] * 4,
        scratch_shapes=[
            pltpu.VMEM((ROWS, D), BF),
            pltpu.VMEM((NF, D), BF),
            pltpu.SemaphoreType.DMA((9,)),
        ],
        compiler_params=params(8),
        cost_estimate=pl.CostEstimate(flops=300_000, bytes_accessed=2_500_000, transcendentals=0),
        name="prepare",
    )(frame_pos, *map(in_hbm, (latent, pos, w_t, w_out)))


def qkv_first_kernel(later, mods, w_t, *refs):
    mine, other = refs[0:3], refs[3:6]
    out, wq_low, wq_high, h, x, weights, held, sems = refs[6:]
    _, core, _, y = position()
    first = pl.ds(PACK[0], PACK[1])
    pairs = [
        (later.at[:, : PACK[0], :], x),
        (later.at[:, first, :], held),
        (w_t.at[0], weights.at[: 3 * HD, :]),
    ]
    for group, side in ((mine, core), (other, 1 - core)):
        cols = pl.ds(pl.multiple_of(side * (D // 2), 128), D // 2)
        for n, weight in enumerate(group):
            pairs.append((weight, weights.at[(n + 1) * 3 * HD : (n + 2) * 3 * HD, cols]))
    pairs += [(held.at[:LOW], wq_low), (held.at[LOW:], wq_high)]
    copies = [pltpu.make_async_copy(*pair, sems.at[n]) for n, pair in enumerate(pairs)]
    for copy in copies[:9]:
        copy.start()
    copies[0].wait()
    for z in range(NZ):
        blocks = [x[z, e * ROWS : (e + 1) * ROWS, :].astype(F32) for e in range(8)]
        for e, norm in enumerate(normalized(blocks)):
            cols = slice(e * EIGHTH, (e + 1) * EIGHTH)
            part = norm * (1.0 + mods[1:2, cols]) + mods[0:1, cols]
            h[z * ROWS : (z + 1) * ROWS, cols] = part.astype(BF)
    copies[1].wait()
    for copy in copies[9:]:
        copy.start()
    for copy in copies[2:9]:
        copy.wait()
    result = times(weights[...], h[...])
    for j in range(NY):
        store_head(out.at[lax.rem(y + j, NY)], result[j * 3 * HD : (j + 1) * 3 * HD])
    for copy in copies[9:]:
        copy.wait()


def qkv_first(later, mods, w_t, mine, other):
    parts = [pltpu.HBM((n, 3 * HD, EIGHTH), BF) for n in (LOW, NZ - LOW)]
    return pl.pallas_call(
        qkv_first_kernel,
        out_shape=[jax.ShapeDtypeStruct((NY, 3 * HD, NZ * ROWS), BF), *parts],
        in_specs=[HB, VM, HB] + [ANY] * 6,
        out_specs=[VM, HB, HB],
        scratch_shapes=[
            pltpu.VMEM((NZ * ROWS, D), BF),
            pltpu.VMEM((NZ, PACK[0], EIGHTH), BF),
            pltpu.VMEM((NY * 3 * HD, D), BF),
            pltpu.VMEM((NZ, PACK[1], EIGHTH), BF),
            pltpu.SemaphoreType.DMA((11,)),
        ],
        compiler_params=params(24),
        cost_estimate=pl.CostEstimate(flops=1_200_000_000, bytes_accessed=14_000_000, transcendentals=0),
        name="qkv_first",
    )(in_hbm(later), mods, in_hbm(w_t), *mine, *other)


def qkv_second_kernel(x0, x1, x2, x3, mods, gathered, *refs):
    high, (out, h, weights, sems) = refs[:8], refs[8:]
    x_pos, core, _, y = position()
    copies = []
    for e in range(8):
        target = weights.at[:LOW, :, e * EIGHTH : (e + 1) * EIGHTH]
        copies.append(pltpu.make_async_copy(gathered.at[e], target, sems.at[e]))
    for n, weight in enumerate(high):
        side = core if n < NX else 1 - core
        start = (lax.rem(x_pos + n % NX, NX) * NC + side) * EIGHTH
        target = weights.at[LOW:, :, pl.ds(pl.multiple_of(start, 128), EIGHTH)]
        copies.append(pltpu.make_async_copy(weight, target, sems.at[8 + n]))
    for copy in copies:
        copy.start()
    for j, x in enumerate((x0, x1, x2, x3)):
        (norm,) = normalized([x[...].astype(F32)])
        part = norm * (1.0 + mods[4:5, :]) + mods[3:4, :]
        h[lax.rem(y + j, NY)] = part.astype(BF)
    tokens = h[...].reshape(NY * ROWS, D)
    for part, (begin, end) in enumerate(((0, LOW), (LOW, NZ))):
        for copy in copies[8 * part : 8 * part + 8]:
            copy.wait()
        result = times(weights[begin:end].reshape((end - begin) * 3 * HD, D), tokens)
        for j in range(end - begin):
            store_head(out.at[begin + j], result[j * 3 * HD : (j + 1) * 3 * HD])


def qkv_second(shards, mods, gathered, weights):
    return pl.pallas_call(
        qkv_second_kernel,
        out_shape=jax.ShapeDtypeStruct((NZ, 3 * HD, NY * ROWS), BF),
        in_specs=[VM] * 5 + [HB] + [ANY] * 8,
        out_specs=VM,
        scratch_shapes=[
            pltpu.VMEM((NY, ROWS, D), BF),
            pltpu.VMEM((NZ, 3 * HD, D), BF),
            pltpu.SemaphoreType.DMA((16,)),
        ],
        compiler_params=params(24),
        cost_estimate=pl.CostEstimate(flops=1_200_000_000, bytes_accessed=10_500_000, transcendentals=0),
        name="qkv_second",
    )(*shards, mods, in_hbm(gathered), *weights)


def over_keys(per, ref, queries, acc, den, begin):
    def wide(n, lo, hi):
        if per == 1:
            return ref[n, lo:hi, :]
        return jnp.concatenate([ref[n * per + i, lo:hi, :] for i in range(per)], axis=1)

    def body(m, carry):
        q = queries[m]
        total, norm = (None, None) if begin else (acc[m], den[m])
        for n in range(4):
            keys, values = wide(n, HD, 2 * HD), wide(n, 2 * HD, 3 * HD)
            score = lax.dot_general(keys, q, (((0,), (0,)), ((), ())), preferred_element_type=F32)
            e = jnp.exp(score)
            sums = jnp.sum(e, axis=0, keepdims=True)
            term = jnp.dot(values, e.astype(BF), preferred_element_type=F32)
            total = term if total is None else total + term
            norm = sums if norm is None else norm + sums
        acc[m] = total
        den[m] = norm
        return carry

    lax.fori_loop(0, 4, body, 0)


def own_kernel(per, own, gain, queries, acc, den):
    column = jnp.transpose(jnp.broadcast_to(gain[...], (8, 2 * HD)))[:, 0:1]
    g = column[0:HD] * column[HD:] * 0.125
    for n in range(4):
        parts = [own[n * per + i, 0:HD, :] for i in range(per)]
        q = parts[0] if per == 1 else jnp.concatenate(parts, axis=1)
        queries[n] = (q.astype(F32) * g).astype(BF)
    over_keys(per, own, queries, acc, den, True)


def neighbours_kernel(per, lower, upper, queries, acc_in, den_in, out, acc, den):
    x_pos, core, _, _ = position()
    slot = x_pos * NC + core
    acc[...] = acc_in[...]
    den[...] = den_in[...]

    @pl.when(slot > 0)
    def _():
        over_keys(per, lower, queries, acc, den, False)

    @pl.when(slot < NX * NC - 1)
    def _():
        over_keys(per, upper, queries, acc, den, False)

    if per == 1:
        done = [acc[n] / den[n] for n in range(4)]
        for z in range(NZ):
            cols = slice(z * ROWS, (z + 1) * ROWS)
            out[z] = jnp.concatenate([d[:, cols] for d in done], axis=1).astype(BF)
    else:
        for n in range(4):
            done = (acc[n] / den[n]).astype(BF)
            for i in range(per):
                out[n * per + i] = done[:, i * 256 // per : (i + 1) * 256 // per]


SUMS = (jax.ShapeDtypeStruct((4, HD, 256), F32), jax.ShapeDtypeStruct((4, 1, 256), F32))


def own_keys(own, gain):
    per = own.shape[0] // 4
    return pl.pallas_call(
        functools.partial(own_kernel, per),
        out_shape=[jax.ShapeDtypeStruct((4, HD, 256), BF), *SUMS],
        in_specs=[VM] * 2,
        out_specs=[VM] * 3,
        compiler_params=params(8),
        cost_estimate=pl.CostEstimate(flops=3_000_000_000, bytes_accessed=800_000, transcendentals=0),
        name="own_%d" % per,
    )(own, gain)


def neighbour_keys(lower, upper, queries, acc, den):
    per = lower.shape[0] // 4
    return pl.pallas_call(
        functools.partial(neighbours_kernel, per),
        out_shape=jax.ShapeDtypeStruct((NZ, HD, NY * ROWS), BF),
        in_specs=[VM] * 5,
        out_specs=VM,
        scratch_shapes=[pltpu.VMEM(s.shape, F32) for s in SUMS],
        compiler_params=params(8),
        cost_estimate=pl.CostEstimate(flops=6_000_000_000, bytes_accessed=1_200_000, transcendentals=0),
        name="neighbours_%d" % per,
    )(lower, upper, queries, acc, den)


def project_terms(o, eighths, weights, sems, put):
    copies = [pltpu.make_async_copy(w, weights.at[n], sems.at[n]) for n, (w, _) in enumerate(eighths)]
    for copy in copies:
        copy.start()
    rows = o[...].reshape(NZ * HD, NY * ROWS)
    for n in range(0, 8, 2):
        copies[n].wait()
        copies[n + 1].wait()
        w = jnp.concatenate([weights[n + t].reshape(NZ * HD, EIGHTH) for t in range(2)], axis=1)
        term = lax.dot_general(rows, w, (((0,), (0,)), ((), ())), preferred_element_type=F32)
        put(pl.ds(pl.multiple_of(eighths[n][1] * EIGHTH, 128), QUARTER), term.astype(BF))


def project_first_kernel(o, mine, other, out, wo1, weights, held, sems):
    _, core, _, _ = position()
    inner = pltpu.make_async_copy(mine.at[:, 4 * HD :, :], held, sems.at[8])
    outer = pltpu.make_async_copy(held, wo1, sems.at[9])
    inner.start()
    eighths = [
        (w.at[:, e * HD : (e + 1) * HD, :], 4 * side + e)
        for w, side in ((mine, core), (other, 1 - core))
        for e in range(4)
    ]

    def put(cols, term):
        out[:, cols] = term

    project_terms(o, eighths, weights, sems, put)
    inner.wait()
    outer.start()
    outer.wait()


def project_first(o, mine, other):
    share = (NZ, HD, EIGHTH)
    out, wo1 = pl.pallas_call(
        project_first_kernel,
        out_shape=[jax.ShapeDtypeStruct((NY * ROWS, D), BF), pltpu.HBM(share, BF)],
        in_specs=[VM, HB, ANY],
        out_specs=[VM, HB],
        scratch_shapes=[pltpu.VMEM((8, *share), BF), pltpu.VMEM(share, BF), pltpu.SemaphoreType.DMA((10,))],
        compiler_params=params(12),
        cost_estimate=pl.CostEstimate(flops=420_000_000, bytes_accessed=4_000_000, transcendentals=0),
        name="project_first",
    )(o, in_hbm(mine), other)
    return out.reshape(NY, ROWS, D), wo1


def project_second_kernel(o, gathered, out0, out1, out2, out3, weights, held, sems):
    _, _, _, y = position()

    def put(cols, term):
        held[:, :, cols] = term.reshape(NY, ROWS, QUARTER)

    project_terms(o, [(gathered.at[s], s) for s in range(NX * NC)], weights, sems, put)
    for j, out in enumerate((out0, out1, out2, out3)):
        out[...] = held[lax.rem(y + j, NY)]


def project_second(o, gathered):
    share = (NZ, HD, EIGHTH)
    return pl.pallas_call(
        project_second_kernel,
        out_shape=[jax.ShapeDtypeStruct((ROWS, D), BF)] * NY,
        in_specs=[VM, HB],
        out_specs=[VM] * NY,
        scratch_shapes=[pltpu.VMEM((8, *share), BF), pltpu.VMEM((NY, ROWS, D), BF), pltpu.SemaphoreType.DMA((8,))],
        compiler_params=params(12),
        cost_estimate=pl.CostEstimate(flops=420_000_000, bytes_accessed=4_000_000, transcendentals=0),
        name="project_second",
    )(o, in_hbm(gathered))


def added(layer, terms, mods, x):
    attn = sum(term.astype(F32) for term in terms)
    gate = mods[3 * layer + 2 : 3 * layer + 3, :]
    return (x[...].astype(F32) + gate * attn).astype(BF)


def residual_kernel(terms, mods, x, out):
    out[...] = added(0, [terms[j] for j in range(NY)], mods, x)


def residual(terms, mods, x):
    return pl.pallas_call(
        residual_kernel,
        out_shape=jax.ShapeDtypeStruct((ROWS, D), BF),
        in_specs=[VM] * 3,
        out_specs=VM,
        compiler_params=params(8),
        cost_estimate=pl.CostEstimate(flops=600_000, bytes_accessed=1_400_000, transcendentals=0),
        name="residual",
    )(terms, mods, x)


def last_kernel(t0, t1, t2, t3, mods, x, noise, out, leaving, sem):
    x_pos, core, z, y = position()
    value = added(1, [t[...] for t in (t0, t1, t2, t3)], mods, x)
    out[...] = value
    head = jnp.logical_and(x_pos * NC + core == 0, z < NZ // 2)

    @pl.when(head)
    def _():
        at = pl.multiple_of(jnp.minimum(z * NY + y, SEQ // 2 - 1) * ROWS, ROWS)
        copy = pltpu.make_async_copy(noise.at[pl.ds(at, ROWS), :], leaving, sem)
        copy.start()
        copy.wait()

    @pl.when(jnp.logical_not(head))
    def _():
        leaving[...] = value


def last(terms, mods, x, noise):
    shape = jax.ShapeDtypeStruct((ROWS, D), BF)
    return pl.pallas_call(
        last_kernel,
        out_shape=[shape, shape],
        in_specs=[VM] * 6 + [HB],
        out_specs=[VM] * 2,
        scratch_shapes=[pltpu.SemaphoreType.DMA],
        compiler_params=params(8),
        cost_estimate=pl.CostEstimate(flops=600_000, bytes_accessed=1_600_000, transcendentals=0),
        name="last",
    )(*terms, mods, x, in_hbm(noise))


def from_ahead(block, axis, size, distance):
    return lax.ppermute(block, axis, [(i, (i - distance) % size) for i in range(size)])


def swap(block):
    return lax.ppermute(block, "core", [(0, 1), (1, 0)])


def shifted(block, axis, distance):
    devices = range(lax.axis_size(axis))
    route = [(i - distance, i) for i in devices if i - distance in devices]
    return lax.ppermute(block, axis, route)


def per_device(
    latent, noise_frame, frame_pos, t_index, pos_table, mod_table, w_qkv, qk_gain, w_out
):
    mods = lax.dynamic_slice_in_dim(mod_table, t_index[0], 1, 0)[0].astype(F32).reshape(6, D)
    gains = qk_gain[:, 0].astype(F32)
    w_t = jnp.transpose(w_qkv[:, :, 0, :], (0, 2, 1))
    x0, pack, half, wo = prepare(frame_pos, latent, pos_table, w_t, w_out)

    later = lax.all_gather(pack, "z", axis=0, tiled=False)
    wo = lax.all_gather(wo, "z", axis=0, tiled=False)

    mine = [from_ahead(half, "y", NY, j) for j in range(1, NY)]
    other = [swap(m) for m in mine]

    def neighbours(own):
        return shifted(own, ("x", "core"), 1), shifted(own, ("x", "core"), -1)

    heads, low, high = qkv_first(later, mods, w_t, mine, other)
    low = lax.all_gather(low, ("x", "core"), axis=0, tiled=False)
    high_1, high_3 = from_ahead(high, "x", NX, 1), from_ahead(high, "x", NX, 3)
    own = lax.all_to_all(heads, "y", 0, 0, tiled=True)
    own, high_1, high_3 = lax.optimization_barrier((own, high_1, high_3))
    lower, upper = neighbours(own)
    queries, acc, den = own_keys(own, gains[0:1])
    lower, upper, acc, high_1 = lax.optimization_barrier((lower, upper, acc, high_1))
    high_2 = from_ahead(high_1, "x", NX, 1)
    done = neighbour_keys(lower, upper, queries, acc, den)
    done, wo, high, high_1, high_2, high_3 = lax.optimization_barrier((done, wo, high, high_1, high_2, high_3))
    wo_s = swap(wo)
    done = lax.all_to_all(done, "z", 0, 0, tiled=True)
    done, wo_s, high, high_1, high_2, high_3 = lax.optimization_barrier((done, wo_s, high, high_1, high_2, high_3))
    weights = [high, high_1, high_2, high_3]
    weights += [swap(w) for w in weights]
    terms, wo1 = project_first(done, wo, wo_s)
    wo1 = lax.all_gather(wo1, ("x", "core"), axis=0, tiled=False)
    terms = lax.all_to_all(terms, "y", 0, 0, tiled=True)
    x1 = residual(terms, mods, x0)

    shards = [x1] + [from_ahead(x1, "y", NY, j) for j in range(1, NY)]
    heads = qkv_second(shards, mods, low, weights)
    own = lax.all_to_all(heads, "z", 0, 0, tiled=True)
    lower, upper = neighbours(own)
    done = neighbour_keys(lower, upper, *own_keys(own, gains[1:2]))
    done = lax.all_to_all(done, "z", 0, 0, tiled=True)
    terms = project_second(done, wo1)
    terms = [terms[0]] + [from_ahead(terms[j], "y", NY, NY - j) for j in range(1, NY)]
    stream, leaving = last(terms, mods, x1, noise_frame)

    ranks = NX * NC * SEQ
    route = [(i, (i - SEQ // 2) % ranks) for i in range(ranks)]
    queue = lax.ppermute(leaving, ("x", "core", "z", "y"), route)
    return (stream[None], queue[None])


def solution(mesh):
    grid = Mesh(mesh.devices.reshape(NX, NC, NZ, NY), ("x", "core", "z", "y"))
    slot, seq = ("x", "core"), ("z", "y")
    placed = (
        P(slot, seq, None),
        P(),
        P(slot, None),
        P(slot),
        P(),
        P(),
        P(None, None, seq, None),
        P(None, seq, None),
        P(None, seq, None),
    )
    return jax.shard_map(
        per_device,
        mesh=grid,
        in_specs=placed,
        out_specs=(P(slot, seq, None), P(slot, seq, None)),
        check_vma=False,
    )
```

```python
import functools

import jax
import jax.numpy as jnp
from jax import lax
from jax.experimental import pallas as pl
from jax.experimental.pallas import tpu as pltpu
from jax.sharding import Mesh, PartitionSpec as P

BF = jnp.bfloat16
F32 = jnp.float32
EPS = 1e-6
NX, NC, NZ, NY = 4, 2, 8, 4
D = 3072
NF = 16
HD = 64
ROWS = 32
SEQ = NZ * NY
QUARTER = D // NY
EIGHTH = QUARTER // 2
PACK = (8 * ROWS, 3 * HD)
LOW = 5

VM = pl.BlockSpec(memory_space=pltpu.VMEM)
SM = pl.BlockSpec(memory_space=pltpu.SMEM)
HB = pl.BlockSpec(memory_space=pltpu.HBM)
ANY = pl.BlockSpec(memory_space=pl.ANY)


def params(mebibytes):
    return pltpu.CompilerParams(vmem_limit_bytes=mebibytes * 1024 * 1024)


def position():
    return [lax.axis_index(name) for name in ("x", "core", "z", "y")]


def in_hbm(array):
    return pltpu.with_memory_space_constraint(array, pltpu.HBM)


def normalized(blocks):
    mean = sum(jnp.sum(b, axis=-1, keepdims=True) for b in blocks) / D
    centers = [b - mean for b in blocks]
    spread = sum(jnp.sum(c * c, axis=-1, keepdims=True) for c in centers) / D
    inv = lax.rsqrt(spread + EPS)
    return [c * inv for c in centers]


def head_rows(value):
    center = value - jnp.mean(value, axis=0, keepdims=True)
    spread = jnp.mean(center * center, axis=0, keepdims=True)
    return center * lax.rsqrt(spread + EPS)


def store_head(out, result):
    out[0:HD, :] = head_rows(result[0:HD]).astype(BF)
    out[HD : 2 * HD, :] = head_rows(result[HD : 2 * HD]).astype(BF)
    out[2 * HD :, :] = result[2 * HD :].astype(BF)


def times(weight, h):
    return lax.dot_general(weight, h, (((1,), (1,)), ((), ())), preferred_element_type=F32)


def columns(start, width):
    return pl.ds(pl.multiple_of(start, 128), width)


def prepare_kernel(frame_pos, latent, pos, w_t, x0, pack, x, table, sems):
    x_pos, core, z, _ = position()
    pairs = [
        (latent.at[0], x),
        (pos, table),
        (w_t.at[1, :, columns((x_pos * NC + core) * EIGHTH, EIGHTH)], pack.at[PACK[0] :, :]),
    ]
    copies = [pltpu.make_async_copy(*pair, sems.at[n]) for n, pair in enumerate(pairs)]
    for copy in copies:
        copy.start()
    frame = jnp.where(z >= NZ // 2, frame_pos[0, 1], frame_pos[0, 0])
    for copy in copies[:2]:
        copy.wait()
    chosen = lax.broadcasted_iota(jnp.int32, table.shape, 0) == frame
    row = jnp.sum(jnp.where(chosen, table[...].astype(F32), 0.0), axis=0, keepdims=True)
    value = (x[...].astype(F32) + row).astype(BF)
    x0[...] = value
    for e in range(8):
        pack[e * ROWS : (e + 1) * ROWS, :] = value[:, e * EIGHTH : (e + 1) * EIGHTH]
    copies[2].wait()


def prepare(frame_pos, latent, pos, w_t):
    return pl.pallas_call(
        prepare_kernel,
        out_shape=[jax.ShapeDtypeStruct(shape, BF) for shape in ((ROWS, D), (sum(PACK), EIGHTH))],
        in_specs=[SM] + [HB] * 3,
        out_specs=[VM] * 2,
        scratch_shapes=[
            pltpu.VMEM((ROWS, D), BF),
            pltpu.VMEM((NF, D), BF),
            pltpu.SemaphoreType.DMA((3,)),
        ],
        compiler_params=params(8),
        cost_estimate=pl.CostEstimate(flops=300_000, bytes_accessed=800_000, transcendentals=0),
        name="prepare",
    )(frame_pos, *map(in_hbm, (latent, pos, w_t)))


def shares_kernel(w_t, w_out, half, wo, sems):
    x_pos, core, _, _ = position()
    pairs = [(w_t.at[0, :, columns(core * (D // 2), D // 2)], half)]
    for e in range(4):
        pairs.append((w_out.at[0, :, columns((4 * core + e) * EIGHTH, EIGHTH)], wo.at[e * HD : (e + 1) * HD, :]))
    pairs.append((w_out.at[1, :, columns((x_pos * NC + core) * EIGHTH, EIGHTH)], wo.at[4 * HD :, :]))
    copies = [pltpu.make_async_copy(*pair, sems.at[n]) for n, pair in enumerate(pairs)]
    for copy in copies:
        copy.start()
    for copy in copies:
        copy.wait()


def shares(w_t, w_out):
    return pl.pallas_call(
        shares_kernel,
        out_shape=[jax.ShapeDtypeStruct(shape, BF) for shape in ((3 * HD, D // 2), (5 * HD, EIGHTH))],
        in_specs=[HB] * 2,
        out_specs=[VM] * 2,
        scratch_shapes=[pltpu.SemaphoreType.DMA((6,))],
        compiler_params=params(8),
        cost_estimate=pl.CostEstimate(flops=0, bytes_accessed=1_700_000, transcendentals=0),
        name="shares",
    )(in_hbm(w_t), in_hbm(w_out))


def qkv_first_kernel(later, mods, w_t, *refs):
    mine, other = refs[0:3], refs[3:6]
    out, wq_low, wq_high, h, x, weights, held, sems = refs[6:]
    _, core, _, y = position()
    first = pl.ds(PACK[0], PACK[1])
    pairs = [
        (later.at[:, : PACK[0], :], x),
        (later.at[:, first, :], held),
        (w_t.at[0], weights.at[: 3 * HD, :]),
    ]
    for group, side in ((mine, core), (other, 1 - core)):
        cols = pl.ds(pl.multiple_of(side * (D // 2), 128), D // 2)
        for n, weight in enumerate(group):
            pairs.append((weight, weights.at[(n + 1) * 3 * HD : (n + 2) * 3 * HD, cols]))
    pairs += [(held.at[:LOW], wq_low), (held.at[LOW:], wq_high)]
    copies = [pltpu.make_async_copy(*pair, sems.at[n]) for n, pair in enumerate(pairs)]
    for copy in copies[:9]:
        copy.start()
    copies[0].wait()
    for z in range(NZ):
        blocks = [x[z, e * ROWS : (e + 1) * ROWS, :].astype(F32) for e in range(8)]
        for e, norm in enumerate(normalized(blocks)):
            cols = slice(e * EIGHTH, (e + 1) * EIGHTH)
            part = norm * (1.0 + mods[1:2, cols]) + mods[0:1, cols]
            h[z * ROWS : (z + 1) * ROWS, cols] = part.astype(BF)
    copies[1].wait()
    for copy in copies[9:]:
        copy.start()
    for copy in copies[2:9]:
        copy.wait()
    result = times(weights[...], h[...])
    for j in range(NY):
        store_head(out.at[lax.rem(y + j, NY)], result[j * 3 * HD : (j + 1) * 3 * HD])
    for copy in copies[9:]:
        copy.wait()


def qkv_first(later, mods, w_t, mine, other):
    parts = [pltpu.HBM((n, 3 * HD, EIGHTH), BF) for n in (LOW, NZ - LOW)]
    return pl.pallas_call(
        qkv_first_kernel,
        out_shape=[jax.ShapeDtypeStruct((NY, 3 * HD, NZ * ROWS), BF), *parts],
        in_specs=[HB, VM, HB] + [ANY] * 6,
        out_specs=[VM, HB, HB],
        scratch_shapes=[
            pltpu.VMEM((NZ * ROWS, D), BF),
            pltpu.VMEM((NZ, PACK[0], EIGHTH), BF),
            pltpu.VMEM((NY * 3 * HD, D), BF),
            pltpu.VMEM((NZ, PACK[1], EIGHTH), BF),
            pltpu.SemaphoreType.DMA((11,)),
        ],
        compiler_params=params(24),
        cost_estimate=pl.CostEstimate(flops=1_200_000_000, bytes_accessed=14_000_000, transcendentals=0),
        name="qkv_first",
    )(in_hbm(later), mods, in_hbm(w_t), *mine, *other)


def qkv_second_kernel(x0, x1, x2, x3, mods, gathered, *refs):
    high, (out, h, weights, sems) = refs[:8], refs[8:]
    x_pos, core, _, y = position()
    copies = []
    for e in range(8):
        target = weights.at[:LOW, :, e * EIGHTH : (e + 1) * EIGHTH]
        copies.append(pltpu.make_async_copy(gathered.at[e], target, sems.at[e]))
    for n, weight in enumerate(high):
        side = core if n < NX else 1 - core
        start = (lax.rem(x_pos + n % NX, NX) * NC + side) * EIGHTH
        target = weights.at[LOW:, :, pl.ds(pl.multiple_of(start, 128), EIGHTH)]
        copies.append(pltpu.make_async_copy(weight, target, sems.at[8 + n]))
    for copy in copies:
        copy.start()
    for j, x in enumerate((x0, x1, x2, x3)):
        (norm,) = normalized([x[...].astype(F32)])
        part = norm * (1.0 + mods[4:5, :]) + mods[3:4, :]
        h[lax.rem(y + j, NY)] = part.astype(BF)
    tokens = h[...].reshape(NY * ROWS, D)
    for part, (begin, end) in enumerate(((0, LOW), (LOW, NZ))):
        for copy in copies[8 * part : 8 * part + 8]:
            copy.wait()
        result = jnp.transpose(times(tokens, weights[begin:end].reshape((end - begin) * 3 * HD, D)))
        for j in range(end - begin):
            store_head(out.at[begin + j], result[j * 3 * HD : (j + 1) * 3 * HD])


def qkv_second(shards, mods, gathered, weights):
    return pl.pallas_call(
        qkv_second_kernel,
        out_shape=jax.ShapeDtypeStruct((NZ, 3 * HD, NY * ROWS), BF),
        in_specs=[VM] * 5 + [HB] + [ANY] * 8,
        out_specs=VM,
        scratch_shapes=[
            pltpu.VMEM((NY, ROWS, D), BF),
            pltpu.VMEM((NZ, 3 * HD, D), BF),
            pltpu.SemaphoreType.DMA((16,)),
        ],
        compiler_params=params(24),
        cost_estimate=pl.CostEstimate(flops=1_200_000_000, bytes_accessed=10_500_000, transcendentals=0),
        name="qkv_second",
    )(*shards, mods, in_hbm(gathered), *weights)


def over_keys(per, ref, queries, acc, den, begin):
    def wide(n, lo, hi):
        if per == 1:
            return ref[n, lo:hi, :]
        return jnp.concatenate([ref[n * per + i, lo:hi, :] for i in range(per)], axis=1)

    def body(m, carry):
        q = queries[m]
        total, norm = (None, None) if begin else (acc[m], den[m])
        for n in range(4):
            keys, values = wide(n, HD, 2 * HD), wide(n, 2 * HD, 3 * HD)
            score = lax.dot_general(keys, q, (((0,), (0,)), ((), ())), preferred_element_type=F32)
            e = jnp.exp(score)
            sums = jnp.sum(e, axis=0, keepdims=True)
            term = jnp.dot(values, e.astype(BF), preferred_element_type=F32)
            total = term if total is None else total + term
            norm = sums if norm is None else norm + sums
        acc[m] = total
        den[m] = norm
        return carry

    lax.fori_loop(0, 4, body, 0)


def own_kernel(per, own, gain, queries, acc, den):
    column = jnp.transpose(jnp.broadcast_to(gain[...], (8, 2 * HD)))[:, 0:1]
    g = column[0:HD] * column[HD:] * 0.125
    for n in range(4):
        parts = [own[n * per + i, 0:HD, :] for i in range(per)]
        q = parts[0] if per == 1 else jnp.concatenate(parts, axis=1)
        queries[n] = (q.astype(F32) * g).astype(BF)
    over_keys(per, own, queries, acc, den, True)


def neighbours_kernel(per, lower, upper, queries, acc_in, den_in, out, acc, den):
    x_pos, core, _, _ = position()
    slot = x_pos * NC + core
    acc[...] = acc_in[...]
    den[...] = den_in[...]

    @pl.when(slot > 0)
    def _():
        over_keys(per, lower, queries, acc, den, False)

    @pl.when(slot < NX * NC - 1)
    def _():
        over_keys(per, upper, queries, acc, den, False)

    if per == 1:
        done = [acc[n] / den[n] for n in range(4)]
        for z in range(NZ):
            cols = slice(z * ROWS, (z + 1) * ROWS)
            out[z] = jnp.concatenate([d[:, cols] for d in done], axis=1).astype(BF)
    else:
        for n in range(4):
            done = (acc[n] / den[n]).astype(BF)
            for i in range(per):
                out[n * per + i] = done[:, i * 256 // per : (i + 1) * 256 // per]


SUMS = (jax.ShapeDtypeStruct((4, HD, 256), F32), jax.ShapeDtypeStruct((4, 1, 256), F32))


def own_keys(own, gain):
    per = own.shape[0] // 4
    return pl.pallas_call(
        functools.partial(own_kernel, per),
        out_shape=[jax.ShapeDtypeStruct((4, HD, 256), BF), *SUMS],
        in_specs=[VM] * 2,
        out_specs=[VM] * 3,
        compiler_params=params(8),
        cost_estimate=pl.CostEstimate(flops=3_000_000_000, bytes_accessed=800_000, transcendentals=0),
        name="own_%d" % per,
    )(own, gain)


def neighbour_keys(lower, upper, queries, acc, den):
    per = lower.shape[0] // 4
    return pl.pallas_call(
        functools.partial(neighbours_kernel, per),
        out_shape=jax.ShapeDtypeStruct((NZ, HD, NY * ROWS), BF),
        in_specs=[VM] * 5,
        out_specs=VM,
        scratch_shapes=[pltpu.VMEM(s.shape, F32) for s in SUMS],
        compiler_params=params(8),
        cost_estimate=pl.CostEstimate(flops=6_000_000_000, bytes_accessed=1_200_000, transcendentals=0),
        name="neighbours_%d" % per,
    )(lower, upper, queries, acc, den)


def project_terms(o, eighths, weights, sems, put):
    copies = [pltpu.make_async_copy(w, weights.at[n], sems.at[n]) for n, (w, _) in enumerate(eighths)]
    for copy in copies:
        copy.start()
    rows = o[...].reshape(NZ * HD, NY * ROWS)
    for n in range(0, 8, 2):
        copies[n].wait()
        copies[n + 1].wait()
        w = jnp.concatenate([weights[n + t].reshape(NZ * HD, EIGHTH) for t in range(2)], axis=1)
        term = lax.dot_general(rows, w, (((0,), (0,)), ((), ())), preferred_element_type=F32)
        put(pl.ds(pl.multiple_of(eighths[n][1] * EIGHTH, 128), QUARTER), term.astype(BF))


def project_first_kernel(o, mine, other, out, wo1, weights, held, sems):
    _, core, _, _ = position()
    inner = pltpu.make_async_copy(mine.at[:, 4 * HD :, :], held, sems.at[8])
    outer = pltpu.make_async_copy(held, wo1, sems.at[9])
    inner.start()
    eighths = [
        (w.at[:, e * HD : (e + 1) * HD, :], 4 * side + e)
        for w, side in ((mine, core), (other, 1 - core))
        for e in range(4)
    ]

    def put(cols, term):
        out[:, cols] = term

    project_terms(o, eighths, weights, sems, put)
    inner.wait()
    outer.start()
    outer.wait()


def project_first(o, mine, other):
    share = (NZ, HD, EIGHTH)
    out, wo1 = pl.pallas_call(
        project_first_kernel,
        out_shape=[jax.ShapeDtypeStruct((NY * ROWS, D), BF), pltpu.HBM(share, BF)],
        in_specs=[VM, HB, ANY],
        out_specs=[VM, HB],
        scratch_shapes=[pltpu.VMEM((8, *share), BF), pltpu.VMEM(share, BF), pltpu.SemaphoreType.DMA((10,))],
        compiler_params=params(12),
        cost_estimate=pl.CostEstimate(flops=420_000_000, bytes_accessed=4_000_000, transcendentals=0),
        name="project_first",
    )(o, in_hbm(mine), other)
    return out.reshape(NY, ROWS, D), wo1


def project_second_kernel(o, gathered, out0, out1, out2, out3, weights, held, sems):
    _, _, _, y = position()

    def put(cols, term):
        held[:, :, cols] = term.reshape(NY, ROWS, QUARTER)

    project_terms(o, [(gathered.at[s], s) for s in range(NX * NC)], weights, sems, put)
    for j, out in enumerate((out0, out1, out2, out3)):
        out[...] = held[lax.rem(y + j, NY)]


def project_second(o, gathered):
    share = (NZ, HD, EIGHTH)
    return pl.pallas_call(
        project_second_kernel,
        out_shape=[jax.ShapeDtypeStruct((ROWS, D), BF)] * NY,
        in_specs=[VM, HB],
        out_specs=[VM] * NY,
        scratch_shapes=[pltpu.VMEM((8, *share), BF), pltpu.VMEM((NY, ROWS, D), BF), pltpu.SemaphoreType.DMA((8,))],
        compiler_params=params(12),
        cost_estimate=pl.CostEstimate(flops=420_000_000, bytes_accessed=4_000_000, transcendentals=0),
        name="project_second",
    )(o, in_hbm(gathered))


def added(layer, terms, mods, x):
    attn = sum(term.astype(F32) for term in terms)
    gate = mods[3 * layer + 2 : 3 * layer + 3, :]
    return (x[...].astype(F32) + gate * attn).astype(BF)


def residual_kernel(terms, mods, x, out):
    out[...] = added(0, [terms[j] for j in range(NY)], mods, x)


def residual(terms, mods, x):
    return pl.pallas_call(
        residual_kernel,
        out_shape=jax.ShapeDtypeStruct((ROWS, D), BF),
        in_specs=[VM] * 3,
        out_specs=VM,
        compiler_params=params(8),
        cost_estimate=pl.CostEstimate(flops=600_000, bytes_accessed=1_400_000, transcendentals=0),
        name="residual",
    )(terms, mods, x)


def last_kernel(t0, t1, t2, t3, mods, x, noise, out, leaving, sem):
    x_pos, core, z, y = position()
    value = added(1, [t[...] for t in (t0, t1, t2, t3)], mods, x)
    out[...] = value
    head = jnp.logical_and(x_pos * NC + core == 0, z < NZ // 2)

    @pl.when(head)
    def _():
        at = pl.multiple_of(jnp.minimum(z * NY + y, SEQ // 2 - 1) * ROWS, ROWS)
        copy = pltpu.make_async_copy(noise.at[pl.ds(at, ROWS), :], leaving, sem)
        copy.start()
        copy.wait()

    @pl.when(jnp.logical_not(head))
    def _():
        leaving[...] = value


def last(terms, mods, x, noise):
    shape = jax.ShapeDtypeStruct((ROWS, D), BF)
    return pl.pallas_call(
        last_kernel,
        out_shape=[shape, shape],
        in_specs=[VM] * 6 + [HB],
        out_specs=[VM] * 2,
        scratch_shapes=[pltpu.SemaphoreType.DMA],
        compiler_params=params(8),
        cost_estimate=pl.CostEstimate(flops=600_000, bytes_accessed=1_600_000, transcendentals=0),
        name="last",
    )(*terms, mods, x, in_hbm(noise))


def from_ahead(block, axis, size, distance):
    return lax.ppermute(block, axis, [(i, (i - distance) % size) for i in range(size)])


def swap(block):
    return lax.ppermute(block, "core", [(0, 1), (1, 0)])


def shifted(block, axis, distance):
    devices = range(lax.axis_size(axis))
    route = [(i - distance, i) for i in devices if i - distance in devices]
    return lax.ppermute(block, axis, route)


def per_device(
    latent, noise_frame, frame_pos, t_index, pos_table, mod_table, w_qkv, qk_gain, w_out
):
    mods = lax.dynamic_slice_in_dim(mod_table, t_index[0], 1, 0)[0].astype(F32).reshape(6, D)
    gains = qk_gain[:, 0].astype(F32)
    w_t = jnp.transpose(w_qkv[:, :, 0, :], (0, 2, 1))
    x0, pack = prepare(frame_pos, latent, pos_table, w_t)
    half, wo = shares(w_t, w_out)

    later = lax.all_gather(pack, "z", axis=0, tiled=False)
    wo = lax.all_gather(wo, "z", axis=0, tiled=False)

    mine = [from_ahead(half, "y", NY, j) for j in range(1, NY)]
    other = [swap(m) for m in mine]

    def neighbours(own):
        return shifted(own, ("x", "core"), 1), shifted(own, ("x", "core"), -1)

    heads, low, high = qkv_first(later, mods, w_t, mine, other)
    low = lax.all_gather(low, ("x", "core"), axis=0, tiled=False)
    high_1, high_3 = from_ahead(high, "x", NX, 1), from_ahead(high, "x", NX, 3)
    own = lax.all_to_all(heads, "y", 0, 0, tiled=True)
    own, high_1, high_3 = lax.optimization_barrier((own, high_1, high_3))
    lower, upper = neighbours(own)
    queries, acc, den = own_keys(own, gains[0:1])
    lower, upper, acc, high_1 = lax.optimization_barrier((lower, upper, acc, high_1))
    high_2 = from_ahead(high_1, "x", NX, 1)
    done = neighbour_keys(lower, upper, queries, acc, den)
    done, wo, high, high_1, high_2, high_3 = lax.optimization_barrier((done, wo, high, high_1, high_2, high_3))
    wo_s = swap(wo)
    done = lax.all_to_all(done, "z", 0, 0, tiled=True)
    done, wo_s, high, high_1, high_2, high_3 = lax.optimization_barrier((done, wo_s, high, high_1, high_2, high_3))
    weights = [high, high_1, high_2, high_3]
    weights += [swap(w) for w in weights]
    terms, wo1 = project_first(done, wo, wo_s)
    wo1 = lax.all_gather(wo1, ("x", "core"), axis=0, tiled=False)
    terms = lax.all_to_all(terms, "y", 0, 0, tiled=True)
    x1 = residual(terms, mods, x0)

    shards = [x1] + [from_ahead(x1, "y", NY, j) for j in range(1, NY)]
    heads = qkv_second(shards, mods, low, weights)
    own = lax.all_to_all(heads, "z", 0, 0, tiled=True)
    lower, upper = neighbours(own)
    done = neighbour_keys(lower, upper, *own_keys(own, gains[1:2]))
    done = lax.all_to_all(done, "z", 0, 0, tiled=True)
    terms = project_second(done, wo1)
    terms = [terms[0]] + [from_ahead(terms[j], "y", NY, NY - j) for j in range(1, NY)]
    stream, leaving = last(terms, mods, x1, noise_frame)

    ranks = NX * NC * SEQ
    route = [(i, (i - SEQ // 2) % ranks) for i in range(ranks)]
    queue = lax.ppermute(leaving, ("x", "core", "z", "y"), route)
    return (stream[None], queue[None])


def solution(mesh):
    grid = Mesh(mesh.devices.reshape(NX, NC, NZ, NY), ("x", "core", "z", "y"))
    slot, seq = ("x", "core"), ("z", "y")
    placed = (
        P(slot, seq, None),
        P(),
        P(slot, None),
        P(slot),
        P(),
        P(),
        P(None, None, seq, None),
        P(None, seq, None),
        P(None, seq, None),
    )
    return jax.shard_map(
        per_device,
        mesh=grid,
        in_specs=placed,
        out_specs=(P(slot, seq, None), P(slot, seq, None)),
        check_vma=False,
    )
```

```python
import functools

import jax
import jax.numpy as jnp
from jax import lax
from jax.experimental import pallas as pl
from jax.experimental.pallas import tpu as pltpu
from jax.sharding import Mesh, PartitionSpec as P

BF = jnp.bfloat16
F32 = jnp.float32
EPS = 1e-6
NX, NC, NZ, NY = 4, 2, 8, 4
D = 3072
NF = 16
HD = 64
ROWS = 32
SEQ = NZ * NY
QUARTER = D // NY
EIGHTH = QUARTER // 2
PACK = (8 * ROWS, 3 * HD)
LOW = 5

VM = pl.BlockSpec(memory_space=pltpu.VMEM)
SM = pl.BlockSpec(memory_space=pltpu.SMEM)
HB = pl.BlockSpec(memory_space=pltpu.HBM)
ANY = pl.BlockSpec(memory_space=pl.ANY)


def params(mebibytes):
    return pltpu.CompilerParams(vmem_limit_bytes=mebibytes * 1024 * 1024)


def position():
    return [lax.axis_index(name) for name in ("x", "core", "z", "y")]


def in_hbm(array):
    return pltpu.with_memory_space_constraint(array, pltpu.HBM)


def normalized(blocks):
    mean = sum(jnp.sum(b, axis=-1, keepdims=True) for b in blocks) / D
    centers = [b - mean for b in blocks]
    spread = sum(jnp.sum(c * c, axis=-1, keepdims=True) for c in centers) / D
    inv = lax.rsqrt(spread + EPS)
    return [c * inv for c in centers]


def head_rows(value):
    center = value - jnp.mean(value, axis=0, keepdims=True)
    spread = jnp.mean(center * center, axis=0, keepdims=True)
    return center * lax.rsqrt(spread + EPS)


def store_head(out, result):
    out[0:HD, :] = head_rows(result[0:HD]).astype(BF)
    out[HD : 2 * HD, :] = head_rows(result[HD : 2 * HD]).astype(BF)
    out[2 * HD :, :] = result[2 * HD :].astype(BF)


def times(weight, h):
    return lax.dot_general(weight, h, (((1,), (1,)), ((), ())), preferred_element_type=F32)


def columns(start, width):
    return pl.ds(pl.multiple_of(start, 128), width)


def prepare_kernel(frame_pos, latent, pos, w_t, x0, pack, x, table, sems):
    x_pos, core, z, _ = position()
    pairs = [
        (latent.at[0], x),
        (pos, table),
        (w_t.at[1, :, columns((x_pos * NC + core) * EIGHTH, EIGHTH)], pack.at[PACK[0] :, :]),
    ]
    copies = [pltpu.make_async_copy(*pair, sems.at[n]) for n, pair in enumerate(pairs)]
    for copy in copies:
        copy.start()
    frame = jnp.where(z >= NZ // 2, frame_pos[0, 1], frame_pos[0, 0])
    for copy in copies[:2]:
        copy.wait()
    chosen = lax.broadcasted_iota(jnp.int32, table.shape, 0) == frame
    row = jnp.sum(jnp.where(chosen, table[...].astype(F32), 0.0), axis=0, keepdims=True)
    value = (x[...].astype(F32) + row).astype(BF)
    x0[...] = value
    for e in range(8):
        pack[e * ROWS : (e + 1) * ROWS, :] = value[:, e * EIGHTH : (e + 1) * EIGHTH]
    copies[2].wait()


def prepare(frame_pos, latent, pos, w_t):
    return pl.pallas_call(
        prepare_kernel,
        out_shape=[jax.ShapeDtypeStruct(shape, BF) for shape in ((ROWS, D), (sum(PACK), EIGHTH))],
        in_specs=[SM] + [HB] * 3,
        out_specs=[VM] * 2,
        scratch_shapes=[
            pltpu.VMEM((ROWS, D), BF),
            pltpu.VMEM((NF, D), BF),
            pltpu.SemaphoreType.DMA((3,)),
        ],
        compiler_params=params(8),
        cost_estimate=pl.CostEstimate(flops=300_000, bytes_accessed=800_000, transcendentals=0),
        name="prepare",
    )(frame_pos, *map(in_hbm, (latent, pos, w_t)))


def shares_kernel(w_t, w_out, half, wo, sems):
    x_pos, core, _, _ = position()
    pairs = [(w_t.at[0, :, columns(core * (D // 2), D // 2)], half)]
    for e in range(4):
        pairs.append((w_out.at[0, :, columns((4 * core + e) * EIGHTH, EIGHTH)], wo.at[e * HD : (e + 1) * HD, :]))
    pairs.append((w_out.at[1, :, columns((x_pos * NC + core) * EIGHTH, EIGHTH)], wo.at[4 * HD :, :]))
    copies = [pltpu.make_async_copy(*pair, sems.at[n]) for n, pair in enumerate(pairs)]
    for copy in copies:
        copy.start()
    for copy in copies:
        copy.wait()


def shares(w_t, w_out):
    return pl.pallas_call(
        shares_kernel,
        out_shape=[jax.ShapeDtypeStruct(shape, BF) for shape in ((3 * HD, D // 2), (5 * HD, EIGHTH))],
        in_specs=[HB] * 2,
        out_specs=[VM] * 2,
        scratch_shapes=[pltpu.SemaphoreType.DMA((6,))],
        compiler_params=params(8),
        cost_estimate=pl.CostEstimate(flops=0, bytes_accessed=1_700_000, transcendentals=0),
        name="shares",
    )(in_hbm(w_t), in_hbm(w_out))


def qkv_first_kernel(later, mods, w_t, *refs):
    mine, other = refs[0:3], refs[3:6]
    out, wq_low, wq_high, h, x, weights, held, sems = refs[6:]
    _, core, _, y = position()
    first = pl.ds(PACK[0], PACK[1])
    pairs = [
        (later.at[:, : PACK[0], :], x),
        (later.at[:, first, :], held),
        (w_t.at[0], weights.at[: 3 * HD, :]),
    ]
    for group, side in ((mine, core), (other, 1 - core)):
        cols = pl.ds(pl.multiple_of(side * (D // 2), 128), D // 2)
        for n, weight in enumerate(group):
            pairs.append((weight, weights.at[(n + 1) * 3 * HD : (n + 2) * 3 * HD, cols]))
    pairs += [(held.at[:LOW], wq_low), (held.at[LOW:], wq_high)]
    copies = [pltpu.make_async_copy(*pair, sems.at[n]) for n, pair in enumerate(pairs)]
    for copy in copies[:9]:
        copy.start()
    copies[0].wait()
    for z in range(NZ):
        blocks = [x[z, e * ROWS : (e + 1) * ROWS, :].astype(F32) for e in range(8)]
        for e, norm in enumerate(normalized(blocks)):
            cols = slice(e * EIGHTH, (e + 1) * EIGHTH)
            part = norm * (1.0 + mods[1:2, cols]) + mods[0:1, cols]
            h[z * ROWS : (z + 1) * ROWS, cols] = part.astype(BF)
    copies[1].wait()
    for copy in copies[9:]:
        copy.start()
    for copy in copies[2:9]:
        copy.wait()
    result = times(weights[...], h[...])
    for j in range(NY):
        store_head(out.at[lax.rem(y + j, NY)], result[j * 3 * HD : (j + 1) * 3 * HD])
    for copy in copies[9:]:
        copy.wait()


def qkv_first(later, mods, w_t, mine, other):
    parts = [pltpu.HBM((n, 3 * HD, EIGHTH), BF) for n in (LOW, NZ - LOW)]
    return pl.pallas_call(
        qkv_first_kernel,
        out_shape=[jax.ShapeDtypeStruct((NY, 3 * HD, NZ * ROWS), BF), *parts],
        in_specs=[HB, VM, HB] + [ANY] * 6,
        out_specs=[VM, HB, HB],
        scratch_shapes=[
            pltpu.VMEM((NZ * ROWS, D), BF),
            pltpu.VMEM((NZ, PACK[0], EIGHTH), BF),
            pltpu.VMEM((NY * 3 * HD, D), BF),
            pltpu.VMEM((NZ, PACK[1], EIGHTH), BF),
            pltpu.SemaphoreType.DMA((11,)),
        ],
        compiler_params=params(24),
        cost_estimate=pl.CostEstimate(flops=1_200_000_000, bytes_accessed=14_000_000, transcendentals=0),
        name="qkv_first",
    )(in_hbm(later), mods, in_hbm(w_t), *mine, *other)


def qkv_second_kernel(x0, x1, x2, x3, mods, gathered, *refs):
    high, (out, h, weights, sems) = refs[:8], refs[8:]
    x_pos, core, _, y = position()
    copies = []
    for e in range(8):
        target = weights.at[:LOW, :, e * EIGHTH : (e + 1) * EIGHTH]
        copies.append(pltpu.make_async_copy(gathered.at[e], target, sems.at[e]))
    for n, weight in enumerate(high):
        side = core if n < NX else 1 - core
        start = (lax.rem(x_pos + n % NX, NX) * NC + side) * EIGHTH
        target = weights.at[LOW:, :, pl.ds(pl.multiple_of(start, 128), EIGHTH)]
        copies.append(pltpu.make_async_copy(weight, target, sems.at[8 + n]))
    for copy in copies:
        copy.start()
    for j, x in enumerate((x0, x1, x2, x3)):
        (norm,) = normalized([x[...].astype(F32)])
        part = norm * (1.0 + mods[4:5, :]) + mods[3:4, :]
        h[lax.rem(y + j, NY)] = part.astype(BF)
    tokens = h[...].reshape(NY * ROWS, D)
    for part, (begin, end) in enumerate(((0, LOW), (LOW, NZ))):
        for copy in copies[8 * part : 8 * part + 8]:
            copy.wait()
        result = jnp.transpose(times(tokens, weights[begin:end].reshape((end - begin) * 3 * HD, D)))
        for j in range(end - begin):
            store_head(out.at[begin + j], result[j * 3 * HD : (j + 1) * 3 * HD])


def qkv_second(shards, mods, gathered, weights):
    return pl.pallas_call(
        qkv_second_kernel,
        out_shape=jax.ShapeDtypeStruct((NZ, 3 * HD, NY * ROWS), BF),
        in_specs=[VM] * 5 + [HB] + [ANY] * 8,
        out_specs=VM,
        scratch_shapes=[
            pltpu.VMEM((NY, ROWS, D), BF),
            pltpu.VMEM((NZ, 3 * HD, D), BF),
            pltpu.SemaphoreType.DMA((16,)),
        ],
        compiler_params=params(24),
        cost_estimate=pl.CostEstimate(flops=1_200_000_000, bytes_accessed=10_500_000, transcendentals=0),
        name="qkv_second",
    )(*shards, mods, in_hbm(gathered), *weights)


def over_keys(per, ref, queries, acc, den, keys, begin):
    def wide(n, lo, hi):
        if per == 1:
            return ref[n, lo:hi, :]
        return jnp.concatenate([ref[n * per + i, lo:hi, :] for i in range(per)], axis=1)

    for n in range(4):
        keys[n] = jnp.transpose(wide(n, HD, 2 * HD))

    def body(m, carry):
        q = queries[m]
        total, norm = (None, None) if begin else (acc[m], den[m])
        for n in range(4):
            score = jnp.dot(keys[n], q, preferred_element_type=F32)
            e = jnp.exp(score)
            sums = jnp.sum(e, axis=0, keepdims=True)
            term = jnp.dot(wide(n, 2 * HD, 3 * HD), e.astype(BF), preferred_element_type=F32)
            total = term if total is None else total + term
            norm = sums if norm is None else norm + sums
        acc[m] = total
        den[m] = norm
        return carry

    lax.fori_loop(0, 4, body, 0)


def own_kernel(per, own, gain, queries, acc, den, keys):
    column = jnp.transpose(jnp.broadcast_to(gain[...], (8, 2 * HD)))[:, 0:1]
    g = column[0:HD] * column[HD:] * 0.125
    for n in range(4):
        parts = [own[n * per + i, 0:HD, :] for i in range(per)]
        q = parts[0] if per == 1 else jnp.concatenate(parts, axis=1)
        queries[n] = (q.astype(F32) * g).astype(BF)
    over_keys(per, own, queries, acc, den, keys, True)


def below_kernel(per, lower, queries, acc_in, den_in, acc, den, keys):
    x_pos, core, _, _ = position()
    acc[...] = acc_in[...]
    den[...] = den_in[...]

    @pl.when(x_pos * NC + core > 0)
    def _():
        over_keys(per, lower, queries, acc, den, keys, False)


def above_kernel(per, upper, queries, acc_in, den_in, out, acc, den, keys):
    x_pos, core, _, _ = position()
    acc[...] = acc_in[...]
    den[...] = den_in[...]

    @pl.when(x_pos * NC + core < NX * NC - 1)
    def _():
        over_keys(per, upper, queries, acc, den, keys, False)

    if per == 1:
        done = [acc[n] / den[n] for n in range(4)]
        for z in range(NZ):
            cols = slice(z * ROWS, (z + 1) * ROWS)
            out[z] = jnp.concatenate([d[:, cols] for d in done], axis=1).astype(BF)
    else:
        for n in range(4):
            done = (acc[n] / den[n]).astype(BF)
            for i in range(per):
                out[n * per + i] = done[:, i * 256 // per : (i + 1) * 256 // per]


SUMS = (jax.ShapeDtypeStruct((4, HD, 256), F32), jax.ShapeDtypeStruct((4, 1, 256), F32))


def own_keys(own, gain):
    per = own.shape[0] // 4
    return pl.pallas_call(
        functools.partial(own_kernel, per),
        out_shape=[jax.ShapeDtypeStruct((4, HD, 256), BF), *SUMS],
        in_specs=[VM] * 2,
        out_specs=[VM] * 3,
        scratch_shapes=[pltpu.VMEM((4, 256, HD), BF)],
        compiler_params=params(8),
        cost_estimate=pl.CostEstimate(flops=3_000_000_000, bytes_accessed=800_000, transcendentals=0),
        name="own_%d" % per,
    )(own, gain)


def below_keys(lower, queries, acc, den):
    per = lower.shape[0] // 4
    return pl.pallas_call(
        functools.partial(below_kernel, per),
        out_shape=list(SUMS),
        in_specs=[VM] * 4,
        out_specs=[VM] * 2,
        scratch_shapes=[pltpu.VMEM((4, 256, HD), BF)],
        compiler_params=params(8),
        cost_estimate=pl.CostEstimate(flops=3_000_000_000, bytes_accessed=1_000_000, transcendentals=0),
        name="below_%d" % per,
    )(lower, queries, acc, den)


def above_keys(upper, queries, acc, den):
    per = upper.shape[0] // 4
    return pl.pallas_call(
        functools.partial(above_kernel, per),
        out_shape=jax.ShapeDtypeStruct((NZ, HD, NY * ROWS), BF),
        in_specs=[VM] * 4,
        out_specs=VM,
        scratch_shapes=[pltpu.VMEM(s.shape, F32) for s in SUMS] + [pltpu.VMEM((4, 256, HD), BF)],
        compiler_params=params(8),
        cost_estimate=pl.CostEstimate(flops=3_000_000_000, bytes_accessed=1_000_000, transcendentals=0),
        name="above_%d" % per,
    )(upper, queries, acc, den)


def project_terms(o, eighths, weights, sems, put):
    copies = [pltpu.make_async_copy(w, weights.at[n], sems.at[n]) for n, (w, _) in enumerate(eighths)]
    for copy in copies:
        copy.start()
    rows = jnp.transpose(o[...].reshape(NZ * HD, NY * ROWS))
    for n in range(0, 8, 2):
        copies[n].wait()
        copies[n + 1].wait()
        w = jnp.concatenate([weights[n + t].reshape(NZ * HD, EIGHTH) for t in range(2)], axis=1)
        term = jnp.dot(rows, w, preferred_element_type=F32)
        put(pl.ds(pl.multiple_of(eighths[n][1] * EIGHTH, 128), QUARTER), term.astype(BF))


def project_first_kernel(o, mine, other, out, wo1, weights, held, sems):
    _, core, _, _ = position()
    inner = pltpu.make_async_copy(mine.at[:, 4 * HD :, :], held, sems.at[8])
    outer = pltpu.make_async_copy(held, wo1, sems.at[9])
    inner.start()
    eighths = [
        (w.at[:, e * HD : (e + 1) * HD, :], 4 * side + e)
        for w, side in ((mine, core), (other, 1 - core))
        for e in range(4)
    ]

    def put(cols, term):
        out[:, cols] = term

    project_terms(o, eighths, weights, sems, put)
    inner.wait()
    outer.start()
    outer.wait()


def project_first(o, mine, other):
    share = (NZ, HD, EIGHTH)
    out, wo1 = pl.pallas_call(
        project_first_kernel,
        out_shape=[jax.ShapeDtypeStruct((NY * ROWS, D), BF), pltpu.HBM(share, BF)],
        in_specs=[VM, HB, ANY],
        out_specs=[VM, HB],
        scratch_shapes=[pltpu.VMEM((8, *share), BF), pltpu.VMEM(share, BF), pltpu.SemaphoreType.DMA((10,))],
        compiler_params=params(12),
        cost_estimate=pl.CostEstimate(flops=420_000_000, bytes_accessed=4_000_000, transcendentals=0),
        name="project_first",
    )(o, in_hbm(mine), other)
    return out.reshape(NY, ROWS, D), wo1


def project_second_kernel(o, gathered, out0, out1, out2, out3, weights, held, sems):
    _, _, _, y = position()

    def put(cols, term):
        held[:, :, cols] = term.reshape(NY, ROWS, QUARTER)

    project_terms(o, [(gathered.at[s], s) for s in range(NX * NC)], weights, sems, put)
    for j, out in enumerate((out0, out1, out2, out3)):
        out[...] = held[lax.rem(y + j, NY)]


def project_second(o, gathered):
    share = (NZ, HD, EIGHTH)
    return pl.pallas_call(
        project_second_kernel,
        out_shape=[jax.ShapeDtypeStruct((ROWS, D), BF)] * NY,
        in_specs=[VM, HB],
        out_specs=[VM] * NY,
        scratch_shapes=[pltpu.VMEM((8, *share), BF), pltpu.VMEM((NY, ROWS, D), BF), pltpu.SemaphoreType.DMA((8,))],
        compiler_params=params(12),
        cost_estimate=pl.CostEstimate(flops=420_000_000, bytes_accessed=4_000_000, transcendentals=0),
        name="project_second",
    )(o, in_hbm(gathered))


def added(layer, terms, mods, x):
    attn = sum(term.astype(F32) for term in terms)
    gate = mods[3 * layer + 2 : 3 * layer + 3, :]
    return (x[...].astype(F32) + gate * attn).astype(BF)


def residual_kernel(terms, mods, x, out):
    out[...] = added(0, [terms[j] for j in range(NY)], mods, x)


def residual(terms, mods, x):
    return pl.pallas_call(
        residual_kernel,
        out_shape=jax.ShapeDtypeStruct((ROWS, D), BF),
        in_specs=[VM] * 3,
        out_specs=VM,
        compiler_params=params(8),
        cost_estimate=pl.CostEstimate(flops=600_000, bytes_accessed=1_400_000, transcendentals=0),
        name="residual",
    )(terms, mods, x)


def last_kernel(t0, t1, t2, t3, mods, x, noise, out, leaving, sem):
    x_pos, core, z, y = position()
    value = added(1, [t[...] for t in (t0, t1, t2, t3)], mods, x)
    out[...] = value
    head = jnp.logical_and(x_pos * NC + core == 0, z < NZ // 2)

    @pl.when(head)
    def _():
        at = pl.multiple_of(jnp.minimum(z * NY + y, SEQ // 2 - 1) * ROWS, ROWS)
        copy = pltpu.make_async_copy(noise.at[pl.ds(at, ROWS), :], leaving, sem)
        copy.start()
        copy.wait()

    @pl.when(jnp.logical_not(head))
    def _():
        leaving[...] = value


def last(terms, mods, x, noise):
    shape = jax.ShapeDtypeStruct((ROWS, D), BF)
    return pl.pallas_call(
        last_kernel,
        out_shape=[shape, shape],
        in_specs=[VM] * 6 + [HB],
        out_specs=[VM] * 2,
        scratch_shapes=[pltpu.SemaphoreType.DMA],
        compiler_params=params(8),
        cost_estimate=pl.CostEstimate(flops=600_000, bytes_accessed=1_600_000, transcendentals=0),
        name="last",
    )(*terms, mods, x, in_hbm(noise))


def from_ahead(block, axis, size, distance):
    return lax.ppermute(block, axis, [(i, (i - distance) % size) for i in range(size)])


def swap(block):
    return lax.ppermute(block, "core", [(0, 1), (1, 0)])


def shifted(block, axis, distance):
    devices = range(lax.axis_size(axis))
    route = [(i - distance, i) for i in devices if i - distance in devices]
    return lax.ppermute(block, axis, route)


def per_device(
    latent, noise_frame, frame_pos, t_index, pos_table, mod_table, w_qkv, qk_gain, w_out
):
    mods = lax.dynamic_slice_in_dim(mod_table, t_index[0], 1, 0)[0].astype(F32).reshape(6, D)
    gains = qk_gain[:, 0].astype(F32)
    w_t = jnp.transpose(w_qkv[:, :, 0, :], (0, 2, 1))
    x0, pack = prepare(frame_pos, latent, pos_table, w_t)
    half, wo = shares(w_t, w_out)

    later = lax.all_gather(pack, "z", axis=0, tiled=False)
    wo = lax.all_gather(wo, "z", axis=0, tiled=False)

    mine = [from_ahead(half, "y", NY, j) for j in range(1, NY)]
    other = [swap(m) for m in mine]

    def neighbours(own):
        return shifted(own, ("x", "core"), 1), shifted(own, ("x", "core"), -1)

    heads, low, high = qkv_first(later, mods, w_t, mine, other)
    low = lax.all_gather(low, ("x", "core"), axis=0, tiled=False)
    high_1, high_3 = from_ahead(high, "x", NX, 1), from_ahead(high, "x", NX, 3)
    own = lax.all_to_all(heads, "y", 0, 0, tiled=True)
    own, high_1, high_3 = lax.optimization_barrier((own, high_1, high_3))
    lower, upper = neighbours(own)
    queries, acc, den = own_keys(own, gains[0:1])
    lower, acc, high_1 = lax.optimization_barrier((lower, acc, high_1))
    acc, den = below_keys(lower, queries, acc, den)
    upper, high_1 = lax.optimization_barrier((upper, high_1))
    high_2 = from_ahead(high_1, "x", NX, 1)
    done = above_keys(upper, queries, acc, den)
    done, wo, high, high_1, high_2, high_3 = lax.optimization_barrier((done, wo, high, high_1, high_2, high_3))
    wo_s = swap(wo)
    done = lax.all_to_all(done, "z", 0, 0, tiled=True)
    done, wo_s, high, high_1, high_2, high_3 = lax.optimization_barrier((done, wo_s, high, high_1, high_2, high_3))
    weights = [high, high_1, high_2, high_3]
    weights += [swap(w) for w in weights]
    terms, wo1 = project_first(done, wo, wo_s)
    wo1 = lax.all_gather(wo1, ("x", "core"), axis=0, tiled=False)
    terms = lax.all_to_all(terms, "y", 0, 0, tiled=True)
    x1 = residual(terms, mods, x0)

    shards = [x1] + [from_ahead(x1, "y", NY, j) for j in range(1, NY)]
    heads = qkv_second(shards, mods, low, weights)
    own = lax.all_to_all(heads, "z", 0, 0, tiled=True)
    lower, upper = neighbours(own)
    queries, acc, den = own_keys(own, gains[1:2])
    acc, den = below_keys(lower, queries, acc, den)
    done = above_keys(upper, queries, acc, den)
    done = lax.all_to_all(done, "z", 0, 0, tiled=True)
    terms = project_second(done, wo1)
    terms = [terms[0]] + [from_ahead(terms[j], "y", NY, NY - j) for j in range(1, NY)]
    stream, leaving = last(terms, mods, x1, noise_frame)

    ranks = NX * NC * SEQ
    route = [(i, (i - SEQ // 2) % ranks) for i in range(ranks)]
    queue = lax.ppermute(leaving, ("x", "core", "z", "y"), route)
    return (stream[None], queue[None])


def solution(mesh):
    grid = Mesh(mesh.devices.reshape(NX, NC, NZ, NY), ("x", "core", "z", "y"))
    slot, seq = ("x", "core"), ("z", "y")
    placed = (
        P(slot, seq, None),
        P(),
        P(slot, None),
        P(slot),
        P(),
        P(),
        P(None, None, seq, None),
        P(None, seq, None),
        P(None, seq, None),
    )
    return jax.shard_map(
        per_device,
        mesh=grid,
        in_specs=placed,
        out_specs=(P(slot, seq, None), P(slot, seq, None)),
        check_vma=False,
    )
```

```python
import functools

import jax
import jax.numpy as jnp
from jax import lax
from jax.experimental import pallas as pl
from jax.experimental.pallas import tpu as pltpu
from jax.sharding import Mesh, PartitionSpec as P

BF = jnp.bfloat16
F32 = jnp.float32
EPS = 1e-6
NX, NC, NZ, NY = 4, 2, 8, 4
D = 3072
NF = 16
HD = 64
ROWS = 32
SEQ = NZ * NY
QUARTER = D // NY
EIGHTH = QUARTER // 2
PACK = (8 * ROWS, 3 * HD)
LOW = 5

VM = pl.BlockSpec(memory_space=pltpu.VMEM)
SM = pl.BlockSpec(memory_space=pltpu.SMEM)
HB = pl.BlockSpec(memory_space=pltpu.HBM)
ANY = pl.BlockSpec(memory_space=pl.ANY)


def params(mebibytes):
    return pltpu.CompilerParams(vmem_limit_bytes=mebibytes * 1024 * 1024)


def position():
    return [lax.axis_index(name) for name in ("x", "core", "z", "y")]


def in_hbm(array):
    return pltpu.with_memory_space_constraint(array, pltpu.HBM)


def normalized(blocks):
    mean = sum(jnp.sum(b, axis=-1, keepdims=True) for b in blocks) / D
    centers = [b - mean for b in blocks]
    spread = sum(jnp.sum(c * c, axis=-1, keepdims=True) for c in centers) / D
    inv = lax.rsqrt(spread + EPS)
    return [c * inv for c in centers]


def head_rows(value):
    center = value - jnp.mean(value, axis=0, keepdims=True)
    spread = jnp.mean(center * center, axis=0, keepdims=True)
    return center * lax.rsqrt(spread + EPS)


def store_head(out, result):
    out[0:HD, :] = head_rows(result[0:HD]).astype(BF)
    out[HD : 2 * HD, :] = head_rows(result[HD : 2 * HD]).astype(BF)
    out[2 * HD :, :] = result[2 * HD :].astype(BF)


def times(weight, h):
    return lax.dot_general(weight, h, (((1,), (1,)), ((), ())), preferred_element_type=F32)


def columns(start, width):
    return pl.ds(pl.multiple_of(start, 128), width)


def prepare_kernel(frame_pos, latent, pos, w_t, x0, pack, x, table, sems):
    x_pos, core, z, _ = position()
    pairs = [
        (latent.at[0], x),
        (pos, table),
        (w_t.at[1, :, columns((x_pos * NC + core) * EIGHTH, EIGHTH)], pack.at[PACK[0] :, :]),
    ]
    copies = [pltpu.make_async_copy(*pair, sems.at[n]) for n, pair in enumerate(pairs)]
    for copy in copies:
        copy.start()
    frame = jnp.where(z >= NZ // 2, frame_pos[0, 1], frame_pos[0, 0])
    for copy in copies[:2]:
        copy.wait()
    chosen = lax.broadcasted_iota(jnp.int32, table.shape, 0) == frame
    row = jnp.sum(jnp.where(chosen, table[...].astype(F32), 0.0), axis=0, keepdims=True)
    value = (x[...].astype(F32) + row).astype(BF)
    x0[...] = value
    for e in range(8):
        pack[e * ROWS : (e + 1) * ROWS, :] = value[:, e * EIGHTH : (e + 1) * EIGHTH]
    copies[2].wait()


def prepare(frame_pos, latent, pos, w_t):
    return pl.pallas_call(
        prepare_kernel,
        out_shape=[jax.ShapeDtypeStruct(shape, BF) for shape in ((ROWS, D), (sum(PACK), EIGHTH))],
        in_specs=[SM] + [HB] * 3,
        out_specs=[VM] * 2,
        scratch_shapes=[
            pltpu.VMEM((ROWS, D), BF),
            pltpu.VMEM((NF, D), BF),
            pltpu.SemaphoreType.DMA((3,)),
        ],
        compiler_params=params(8),
        cost_estimate=pl.CostEstimate(flops=300_000, bytes_accessed=800_000, transcendentals=0),
        name="prepare",
    )(frame_pos, *map(in_hbm, (latent, pos, w_t)))


def shares_kernel(w_t, w_out, half, wo, sems):
    x_pos, core, _, _ = position()
    pairs = [(w_t.at[0, :, columns(core * (D // 2), D // 2)], half)]
    for e in range(4):
        pairs.append((w_out.at[0, :, columns((4 * core + e) * EIGHTH, EIGHTH)], wo.at[e * HD : (e + 1) * HD, :]))
    pairs.append((w_out.at[1, :, columns((x_pos * NC + core) * EIGHTH, EIGHTH)], wo.at[4 * HD :, :]))
    copies = [pltpu.make_async_copy(*pair, sems.at[n]) for n, pair in enumerate(pairs)]
    for copy in copies:
        copy.start()
    for copy in copies:
        copy.wait()


def shares(w_t, w_out):
    return pl.pallas_call(
        shares_kernel,
        out_shape=[jax.ShapeDtypeStruct(shape, BF) for shape in ((3 * HD, D // 2), (5 * HD, EIGHTH))],
        in_specs=[HB] * 2,
        out_specs=[VM] * 2,
        scratch_shapes=[pltpu.SemaphoreType.DMA((6,))],
        compiler_params=params(8),
        cost_estimate=pl.CostEstimate(flops=0, bytes_accessed=1_700_000, transcendentals=0),
        name="shares",
    )(in_hbm(w_t), in_hbm(w_out))


def qkv_first_kernel(later, mods, w_t, *refs):
    mine, other = refs[0:3], refs[3:6]
    out, wq_low, wq_high, h, x, weights, held, sems = refs[6:]
    _, core, _, y = position()
    first = pl.ds(PACK[0], PACK[1])
    pairs = [
        (later.at[:, : PACK[0], :], x),
        (later.at[:, first, :], held),
        (w_t.at[0], weights.at[: 3 * HD, :]),
    ]
    for group, side in ((mine, core), (other, 1 - core)):
        cols = pl.ds(pl.multiple_of(side * (D // 2), 128), D // 2)
        for n, weight in enumerate(group):
            pairs.append((weight, weights.at[(n + 1) * 3 * HD : (n + 2) * 3 * HD, cols]))
    pairs += [(held.at[:LOW], wq_low), (held.at[LOW:], wq_high)]
    copies = [pltpu.make_async_copy(*pair, sems.at[n]) for n, pair in enumerate(pairs)]
    for copy in copies[:9]:
        copy.start()
    copies[0].wait()
    for z in range(NZ):
        blocks = [x[z, e * ROWS : (e + 1) * ROWS, :].astype(F32) for e in range(8)]
        for e, norm in enumerate(normalized(blocks)):
            cols = slice(e * EIGHTH, (e + 1) * EIGHTH)
            part = norm * (1.0 + mods[1:2, cols]) + mods[0:1, cols]
            h[z * ROWS : (z + 1) * ROWS, cols] = part.astype(BF)
    copies[1].wait()
    for copy in copies[9:]:
        copy.start()
    for copy in copies[2:9]:
        copy.wait()
    result = times(weights[...], h[...])
    for j in range(NY):
        store_head(out.at[lax.rem(y + j, NY)], result[j * 3 * HD : (j + 1) * 3 * HD])
    for copy in copies[9:]:
        copy.wait()


def qkv_first(later, mods, w_t, mine, other):
    parts = [pltpu.HBM((n, 3 * HD, EIGHTH), BF) for n in (LOW, NZ - LOW)]
    return pl.pallas_call(
        qkv_first_kernel,
        out_shape=[jax.ShapeDtypeStruct((NY, 3 * HD, NZ * ROWS), BF), *parts],
        in_specs=[HB, VM, HB] + [ANY] * 6,
        out_specs=[VM, HB, HB],
        scratch_shapes=[
            pltpu.VMEM((NZ * ROWS, D), BF),
            pltpu.VMEM((NZ, PACK[0], EIGHTH), BF),
            pltpu.VMEM((NY * 3 * HD, D), BF),
            pltpu.VMEM((NZ, PACK[1], EIGHTH), BF),
            pltpu.SemaphoreType.DMA((11,)),
        ],
        compiler_params=params(24),
        cost_estimate=pl.CostEstimate(flops=1_200_000_000, bytes_accessed=14_000_000, transcendentals=0),
        name="qkv_first",
    )(in_hbm(later), mods, in_hbm(w_t), *mine, *other)


def qkv_second_kernel(x0, x1, x2, x3, mods, gathered, *refs):
    high, (out, h, weights, sems) = refs[:8], refs[8:]
    x_pos, core, _, y = position()
    copies = []
    for e in range(8):
        target = weights.at[:LOW, :, e * EIGHTH : (e + 1) * EIGHTH]
        copies.append(pltpu.make_async_copy(gathered.at[e], target, sems.at[e]))
    for n, weight in enumerate(high):
        side = core if n < NX else 1 - core
        start = (lax.rem(x_pos + n % NX, NX) * NC + side) * EIGHTH
        target = weights.at[LOW:, :, pl.ds(pl.multiple_of(start, 128), EIGHTH)]
        copies.append(pltpu.make_async_copy(weight, target, sems.at[8 + n]))
    for copy in copies[8:] + copies[:8]:
        copy.start()
    for j, x in enumerate((x0, x1, x2, x3)):
        (norm,) = normalized([x[...].astype(F32)])
        part = norm * (1.0 + mods[4:5, :]) + mods[3:4, :]
        h[lax.rem(y + j, NY)] = part.astype(BF)
    tokens = h[...].reshape(NY * ROWS, D)
    for part, begin, end in ((1, LOW, NZ), (0, 0, LOW)):
        for copy in copies[8 * part : 8 * part + 8]:
            copy.wait()
        result = jnp.transpose(times(tokens, weights[begin:end].reshape((end - begin) * 3 * HD, D)))
        for j in range(end - begin):
            store_head(out.at[begin + j], result[j * 3 * HD : (j + 1) * 3 * HD])


def qkv_second(shards, mods, gathered, weights):
    return pl.pallas_call(
        qkv_second_kernel,
        out_shape=jax.ShapeDtypeStruct((NZ, 3 * HD, NY * ROWS), BF),
        in_specs=[VM] * 5 + [HB] + [ANY] * 8,
        out_specs=VM,
        scratch_shapes=[
            pltpu.VMEM((NY, ROWS, D), BF),
            pltpu.VMEM((NZ, 3 * HD, D), BF),
            pltpu.SemaphoreType.DMA((16,)),
        ],
        compiler_params=params(24),
        cost_estimate=pl.CostEstimate(flops=1_200_000_000, bytes_accessed=10_500_000, transcendentals=0),
        name="qkv_second",
    )(*shards, mods, in_hbm(gathered), *weights)


def over_keys(per, ref, queries, acc, den, keys, begin):
    def wide(n, lo, hi):
        if per == 1:
            return ref[n, lo:hi, :]
        return jnp.concatenate([ref[n * per + i, lo:hi, :] for i in range(per)], axis=1)

    for n in range(4):
        keys[n] = jnp.transpose(wide(n, HD, 2 * HD))

    def body(m, carry):
        q = queries[m]
        total, norm = (None, None) if begin else (acc[m], den[m])
        for n in range(4):
            score = jnp.dot(keys[n], q, preferred_element_type=F32)
            e = jnp.exp(score)
            sums = jnp.sum(e, axis=0, keepdims=True)
            term = jnp.dot(wide(n, 2 * HD, 3 * HD), e.astype(BF), preferred_element_type=F32)
            total = term if total is None else total + term
            norm = sums if norm is None else norm + sums
        acc[m] = total
        den[m] = norm
        return carry

    lax.fori_loop(0, 4, body, 0)


def own_kernel(per, own, gain, queries, acc, den, keys):
    column = jnp.transpose(jnp.broadcast_to(gain[...], (8, 2 * HD)))[:, 0:1]
    g = column[0:HD] * column[HD:] * 0.125
    for n in range(4):
        parts = [own[n * per + i, 0:HD, :] for i in range(per)]
        q = parts[0] if per == 1 else jnp.concatenate(parts, axis=1)
        queries[n] = (q.astype(F32) * g).astype(BF)
    over_keys(per, own, queries, acc, den, keys, True)


def below_kernel(per, lower, queries, acc_in, den_in, acc, den, keys):
    x_pos, core, _, _ = position()
    acc[...] = acc_in[...]
    den[...] = den_in[...]

    @pl.when(x_pos * NC + core > 0)
    def _():
        over_keys(per, lower, queries, acc, den, keys, False)


def above_kernel(per, upper, queries, acc_in, den_in, out, acc, den, keys):
    x_pos, core, _, _ = position()
    acc[...] = acc_in[...]
    den[...] = den_in[...]

    @pl.when(x_pos * NC + core < NX * NC - 1)
    def _():
        over_keys(per, upper, queries, acc, den, keys, False)

    if per == 1:
        done = [acc[n] / den[n] for n in range(4)]
        for z in range(NZ):
            cols = slice(z * ROWS, (z + 1) * ROWS)
            out[z] = jnp.concatenate([d[:, cols] for d in done], axis=1).astype(BF)
    else:
        for n in range(4):
            done = (acc[n] / den[n]).astype(BF)
            for i in range(per):
                out[n * per + i] = done[:, i * 256 // per : (i + 1) * 256 // per]


SUMS = (jax.ShapeDtypeStruct((4, HD, 256), F32), jax.ShapeDtypeStruct((4, 1, 256), F32))


def own_keys(own, gain):
    per = own.shape[0] // 4
    return pl.pallas_call(
        functools.partial(own_kernel, per),
        out_shape=[jax.ShapeDtypeStruct((4, HD, 256), BF), *SUMS],
        in_specs=[VM] * 2,
        out_specs=[VM] * 3,
        scratch_shapes=[pltpu.VMEM((4, 256, HD), BF)],
        compiler_params=params(8),
        cost_estimate=pl.CostEstimate(flops=3_000_000_000, bytes_accessed=800_000, transcendentals=0),
        name="own_%d" % per,
    )(own, gain)


def below_keys(lower, queries, acc, den):
    per = lower.shape[0] // 4
    return pl.pallas_call(
        functools.partial(below_kernel, per),
        out_shape=list(SUMS),
        in_specs=[VM] * 4,
        out_specs=[VM] * 2,
        scratch_shapes=[pltpu.VMEM((4, 256, HD), BF)],
        compiler_params=params(8),
        cost_estimate=pl.CostEstimate(flops=3_000_000_000, bytes_accessed=1_000_000, transcendentals=0),
        name="below_%d" % per,
    )(lower, queries, acc, den)


def above_keys(upper, queries, acc, den):
    per = upper.shape[0] // 4
    return pl.pallas_call(
        functools.partial(above_kernel, per),
        out_shape=jax.ShapeDtypeStruct((NZ, HD, NY * ROWS), BF),
        in_specs=[VM] * 4,
        out_specs=VM,
        scratch_shapes=[pltpu.VMEM(s.shape, F32) for s in SUMS] + [pltpu.VMEM((4, 256, HD), BF)],
        compiler_params=params(8),
        cost_estimate=pl.CostEstimate(flops=3_000_000_000, bytes_accessed=1_000_000, transcendentals=0),
        name="above_%d" % per,
    )(upper, queries, acc, den)


def project_terms(o, eighths, weights, sems, put):
    copies = [pltpu.make_async_copy(w, weights.at[n], sems.at[n]) for n, (w, _) in enumerate(eighths)]
    for copy in copies:
        copy.start()
    rows = jnp.transpose(o[...].reshape(NZ * HD, NY * ROWS))
    for n in range(0, 8, 2):
        copies[n].wait()
        copies[n + 1].wait()
        w = jnp.concatenate([weights[n + t].reshape(NZ * HD, EIGHTH) for t in range(2)], axis=1)
        term = jnp.dot(rows, w, preferred_element_type=F32)
        put(pl.ds(pl.multiple_of(eighths[n][1] * EIGHTH, 128), QUARTER), term.astype(BF))


def project_first_kernel(o, mine, other, out, wo1, weights, held, sems):
    _, core, _, _ = position()
    inner = pltpu.make_async_copy(mine.at[:, 4 * HD :, :], held, sems.at[8])
    outer = pltpu.make_async_copy(held, wo1, sems.at[9])
    inner.start()
    eighths = [
        (w.at[:, e * HD : (e + 1) * HD, :], 4 * side + e)
        for w, side in ((mine, core), (other, 1 - core))
        for e in range(4)
    ]

    def put(cols, term):
        out[:, cols] = term

    project_terms(o, eighths, weights, sems, put)
    inner.wait()
    outer.start()
    outer.wait()


def project_first(o, mine, other):
    share = (NZ, HD, EIGHTH)
    out, wo1 = pl.pallas_call(
        project_first_kernel,
        out_shape=[jax.ShapeDtypeStruct((NY * ROWS, D), BF), pltpu.HBM(share, BF)],
        in_specs=[VM, HB, ANY],
        out_specs=[VM, HB],
        scratch_shapes=[pltpu.VMEM((8, *share), BF), pltpu.VMEM(share, BF), pltpu.SemaphoreType.DMA((10,))],
        compiler_params=params(12),
        cost_estimate=pl.CostEstimate(flops=420_000_000, bytes_accessed=4_000_000, transcendentals=0),
        name="project_first",
    )(o, in_hbm(mine), other)
    return out.reshape(NY, ROWS, D), wo1


def project_second_kernel(o, gathered, out0, out1, out2, out3, weights, held, sems):
    _, _, _, y = position()

    def put(cols, term):
        held[:, :, cols] = term.reshape(NY, ROWS, QUARTER)

    project_terms(o, [(gathered.at[s], s) for s in range(NX * NC)], weights, sems, put)
    for j, out in enumerate((out0, out1, out2, out3)):
        out[...] = held[lax.rem(y + j, NY)]


def project_second(o, gathered):
    share = (NZ, HD, EIGHTH)
    return pl.pallas_call(
        project_second_kernel,
        out_shape=[jax.ShapeDtypeStruct((ROWS, D), BF)] * NY,
        in_specs=[VM, HB],
        out_specs=[VM] * NY,
        scratch_shapes=[pltpu.VMEM((8, *share), BF), pltpu.VMEM((NY, ROWS, D), BF), pltpu.SemaphoreType.DMA((8,))],
        compiler_params=params(12),
        cost_estimate=pl.CostEstimate(flops=420_000_000, bytes_accessed=4_000_000, transcendentals=0),
        name="project_second",
    )(o, in_hbm(gathered))


def added(layer, terms, mods, x):
    attn = sum(term.astype(F32) for term in terms)
    gate = mods[3 * layer + 2 : 3 * layer + 3, :]
    return (x[...].astype(F32) + gate * attn).astype(BF)


def residual_kernel(terms, mods, x, out):
    out[...] = added(0, [terms[j] for j in range(NY)], mods, x)


def residual(terms, mods, x):
    return pl.pallas_call(
        residual_kernel,
        out_shape=jax.ShapeDtypeStruct((ROWS, D), BF),
        in_specs=[VM] * 3,
        out_specs=VM,
        compiler_params=params(8),
        cost_estimate=pl.CostEstimate(flops=600_000, bytes_accessed=1_400_000, transcendentals=0),
        name="residual",
    )(terms, mods, x)


def last_kernel(t0, t1, t2, t3, mods, x, noise, out, leaving, sem):
    x_pos, core, z, y = position()
    value = added(1, [t[...] for t in (t0, t1, t2, t3)], mods, x)
    out[...] = value
    head = jnp.logical_and(x_pos * NC + core == 0, z < NZ // 2)

    @pl.when(head)
    def _():
        at = pl.multiple_of(jnp.minimum(z * NY + y, SEQ // 2 - 1) * ROWS, ROWS)
        copy = pltpu.make_async_copy(noise.at[pl.ds(at, ROWS), :], leaving, sem)
        copy.start()
        copy.wait()

    @pl.when(jnp.logical_not(head))
    def _():
        leaving[...] = value


def last(terms, mods, x, noise):
    shape = jax.ShapeDtypeStruct((ROWS, D), BF)
    return pl.pallas_call(
        last_kernel,
        out_shape=[shape, shape],
        in_specs=[VM] * 6 + [HB],
        out_specs=[VM] * 2,
        scratch_shapes=[pltpu.SemaphoreType.DMA],
        compiler_params=params(8),
        cost_estimate=pl.CostEstimate(flops=600_000, bytes_accessed=1_600_000, transcendentals=0),
        name="last",
    )(*terms, mods, x, in_hbm(noise))


def from_ahead(block, axis, size, distance):
    return lax.ppermute(block, axis, [(i, (i - distance) % size) for i in range(size)])


def swap(block):
    return lax.ppermute(block, "core", [(0, 1), (1, 0)])


def shifted(block, axis, distance):
    devices = range(lax.axis_size(axis))
    route = [(i - distance, i) for i in devices if i - distance in devices]
    return lax.ppermute(block, axis, route)


def per_device(
    latent, noise_frame, frame_pos, t_index, pos_table, mod_table, w_qkv, qk_gain, w_out
):
    mods = lax.dynamic_slice_in_dim(mod_table, t_index[0], 1, 0)[0].astype(F32).reshape(6, D)
    gains = qk_gain[:, 0].astype(F32)
    w_t = jnp.transpose(w_qkv[:, :, 0, :], (0, 2, 1))
    x0, pack = prepare(frame_pos, latent, pos_table, w_t)
    half, wo = shares(w_t, w_out)

    later = lax.all_gather(pack, "z", axis=0, tiled=False)
    wo = lax.all_gather(wo, "z", axis=0, tiled=False)

    mine = [from_ahead(half, "y", NY, j) for j in range(1, NY)]
    other = [swap(m) for m in mine]

    def neighbours(own):
        return shifted(own, ("x", "core"), 1), shifted(own, ("x", "core"), -1)

    heads, low, high = qkv_first(later, mods, w_t, mine, other)
    low = lax.all_gather(low, ("x", "core"), axis=0, tiled=False)
    high_1, high_3 = from_ahead(high, "x", NX, 1), from_ahead(high, "x", NX, 3)
    own = lax.all_to_all(heads, "y", 0, 0, tiled=True)
    own, high_1, high_3 = lax.optimization_barrier((own, high_1, high_3))
    lower, upper = neighbours(own)
    queries, acc, den = own_keys(own, gains[0:1])
    lower, acc, high_1 = lax.optimization_barrier((lower, acc, high_1))
    acc, den = below_keys(lower, queries, acc, den)
    upper, high_1 = lax.optimization_barrier((upper, high_1))
    high_2 = from_ahead(high_1, "x", NX, 1)
    done = above_keys(upper, queries, acc, den)
    done, wo, high, high_1, high_2, high_3 = lax.optimization_barrier((done, wo, high, high_1, high_2, high_3))
    wo_s = swap(wo)
    done = lax.all_to_all(done, "z", 0, 0, tiled=True)
    done, wo_s, high, high_1, high_2, high_3 = lax.optimization_barrier((done, wo_s, high, high_1, high_2, high_3))
    weights = [high, high_1, high_2, high_3]
    weights += [swap(w) for w in weights]
    terms, wo1 = project_first(done, wo, wo_s)
    wo1 = lax.all_gather(wo1, ("x", "core"), axis=0, tiled=False)
    terms = lax.all_to_all(terms, "y", 0, 0, tiled=True)
    x1 = residual(terms, mods, x0)

    shards = [x1] + [from_ahead(x1, "y", NY, j) for j in range(1, NY)]
    heads = qkv_second(shards, mods, low, weights)
    own = lax.all_to_all(heads, "z", 0, 0, tiled=True)
    lower, upper = neighbours(own)
    queries, acc, den = own_keys(own, gains[1:2])
    acc, den = below_keys(lower, queries, acc, den)
    done = above_keys(upper, queries, acc, den)
    done = lax.all_to_all(done, "z", 0, 0, tiled=True)
    terms = project_second(done, wo1)
    terms = [terms[0]] + [from_ahead(terms[j], "y", NY, NY - j) for j in range(1, NY)]
    stream, leaving = last(terms, mods, x1, noise_frame)

    ranks = NX * NC * SEQ
    route = [(i, (i - SEQ // 2) % ranks) for i in range(ranks)]
    queue = lax.ppermute(leaving, ("x", "core", "z", "y"), route)
    return (stream[None], queue[None])


def solution(mesh):
    grid = Mesh(mesh.devices.reshape(NX, NC, NZ, NY), ("x", "core", "z", "y"))
    slot, seq = ("x", "core"), ("z", "y")
    placed = (
        P(slot, seq, None),
        P(),
        P(slot, None),
        P(slot),
        P(),
        P(),
        P(None, None, seq, None),
        P(None, seq, None),
        P(None, seq, None),
    )
    return jax.shard_map(
        per_device,
        mesh=grid,
        in_specs=placed,
        out_specs=(P(slot, seq, None), P(slot, seq, None)),
        check_vma=False,
    )
```
